32 devices in a mesh: groups: 2 (over y), seq: 16 (over z, x, core).
Axes of the slice: x: 2, y: 2, z: 4, core: 2. Of those that a mesh axis runs over, the one named last changes fastest.
Arguments:
- inputs: bfloat16 [4096, 2048], P(('groups', 'seq')), parts along dimension 0, may hold values from -6 to 6
- gate_in: bfloat16 [4096, 2048], P(('groups', 'seq')), parts along dimension 0, may hold values from -6 to 6
- value_weight: bfloat16 [2048, 2048], P('seq'), may hold values from -0.125 to 0.125
- short_taps: float32 [3, 2048], replicated, may hold values from -3 to 3
- filter_taps: bfloat16 [2048, 2048], P('seq'), may hold values from -0.125 to 0.125
- skip_scale: float32 [2048], replicated, may hold values from -5 to 5
- output_weight: bfloat16 [2048, 2048], P('seq'), may hold values from -0.125 to 0.125
Outputs:
- layer_out: bfloat16 [4096, 2048], P(('groups', 'seq')), parts along dimension 0
The draws below stay inside these ranges and needn't reach their ends.
There are 2 independent parts, one for each index of `groups`. The reference program is written for one: setup_inputs(seed, part) draws one part's arguments, and reference() takes and returns one part's arrays. A program takes and returns all parts, laid end to end along the dimension named above; an argument that names none is the same for every part. Nothing has to cross between parts.
All inputs are finite; a program needn't handle non-finite values.
Results may differ from the reference program's by a relative error of at most 0.0095.
Values may be sent and summed in bfloat16 or wider, within the bound.
No kernel may reach another device: no remote copies, remote signals or barrier semaphores. Data moves between devices by JAX's collectives and lax.ppermute only.
A program may use at most 128 MiB of HBM per device.

```python
import math
import jax
import jax.numpy as jnp
from jax import lax

FEATURES = 2048
CHANNELS = 2048
TOK_DEV = 128
BLOCKS = 16
TOKENS = 2048


def steps_of(stream_key, extent, split, low, high):
    def one(dim, blocks):
        steps = jax.random.uniform(jax.random.fold_in(jax.random.fold_in(stream_key, 6), dim), (blocks,), jnp.float32, low / len(split), high / len(split))
        return jnp.repeat(jnp.exp(steps), extent[dim] // blocks).reshape((-1,) + (1,) * (len(extent) - dim - 1))

    loudness = one(*split[0])
    for cut in split[1:]:
        loudness = loudness * one(*cut)
    return loudness


def centred(stream_key, extent, scale, limit, cuts=(), kind=jnp.bfloat16):
    factor_of = steps_of(stream_key, extent, cuts, -0.22, 0.18) if cuts else 1.0
    values = jax.random.normal(stream_key, extent, jnp.float32) * scale * factor_of
    return jnp.minimum(jnp.maximum(values, -limit), limit).astype(kind)


def setup_inputs(seed: int = 0, part: int = 0) -> dict:
    keys = jax.random.split(jax.random.key(seed), 8)
    own_keys = jax.random.split(jax.random.fold_in(keys[7], part), 8)
    inputs = centred(own_keys[0], (TOKENS, FEATURES), 1.0, 6.0, ((0, 16),))
    gate_in = centred(own_keys[1], (TOKENS, CHANNELS), 1.0, 6.0, ((0, 16),))
    value_weight = centred(keys[2], (FEATURES, CHANNELS), FEATURES ** -0.5, 0.125, ((0, 16),))
    short_taps = centred(keys[3], (3, CHANNELS), 0.5, 3.0, (), jnp.float32)
    filter_taps = centred(keys[4], (TOKENS, CHANNELS), TOKENS ** -0.5, 0.125, ((0, 16),))
    skip_scale = centred(keys[5], (CHANNELS,), 1.0, 5.0, (), jnp.float32)
    output_weight = centred(keys[6], (CHANNELS, FEATURES), CHANNELS ** -0.5, 0.125, ((0, 16),))
    return dict(inputs=inputs, gate_in=gate_in, value_weight=value_weight, short_taps=short_taps, filter_taps=filter_taps, skip_scale=skip_scale, output_weight=output_weight)


def turning(index, count):
    return jnp.float32(2.0 * math.pi) * index.astype(jnp.float32) / jnp.float32(count)


def tables(count):
    grid = jnp.arange(count, dtype=jnp.int32)
    angle = turning((grid[:, None] * grid[None, :]) % count, count)
    return jnp.cos(angle).astype(jnp.bfloat16), jnp.sin(angle).astype(jnp.bfloat16)


def contract(form, table, data):
    return jnp.einsum(form, table.astype(jnp.float32), data.astype(jnp.float32), precision=lax.Precision.HIGHEST)


def spectral(value_blk, taps_blk):
    cos_local, sin_local = tables(TOK_DEV)
    freq_index = jnp.arange(2 * BLOCKS, dtype=jnp.int32)
    offset_index = jnp.arange(TOK_DEV, dtype=jnp.int32)
    angle = turning(freq_index[:, None] * offset_index[None, :], 2 * TOKENS)[:, :, None]
    cos_turn = jnp.cos(angle)
    sin_turn = jnp.sin(angle)

    def forward(signal):
        cube = signal.astype(jnp.float32).reshape(BLOCKS, TOK_DEV, -1)
        first = jnp.fft.fft(cube, n=2 * BLOCKS, axis=0)
        first_re = jnp.real(first)
        first_im = jnp.imag(first)
        partial_re = (first_re * cos_turn + first_im * sin_turn).astype(jnp.bfloat16)
        partial_im = (first_im * cos_turn - first_re * sin_turn).astype(jnp.bfloat16)
        spec_re = (contract('km,fmc->fkc', cos_local, partial_re) + contract('km,fmc->fkc', sin_local, partial_im)).astype(jnp.bfloat16)
        spec_im = (contract('km,fmc->fkc', cos_local, partial_im) - contract('km,fmc->fkc', sin_local, partial_re)).astype(jnp.bfloat16)
        return spec_re.astype(jnp.float32), spec_im.astype(jnp.float32)

    value_re, value_im = forward(value_blk)
    resp_re, resp_im = forward(taps_blk)
    product_re = (value_re * resp_re - value_im * resp_im).astype(jnp.bfloat16)
    product_im = (value_re * resp_im + value_im * resp_re).astype(jnp.bfloat16)
    back_re = (contract('mk,fkc->fmc', cos_local, product_re) - contract('mk,fkc->fmc', sin_local, product_im)) * (1.0 / TOK_DEV)
    back_im = (contract('mk,fkc->fmc', cos_local, product_im) + contract('mk,fkc->fmc', sin_local, product_re)) * (1.0 / TOK_DEV)
    inverse_re = (back_re * cos_turn - back_im * sin_turn).astype(jnp.bfloat16)
    inverse_im = (back_im * cos_turn + back_re * sin_turn).astype(jnp.bfloat16)
    joined = lax.complex(inverse_re.astype(jnp.float32), inverse_im.astype(jnp.float32))
    whole = jnp.fft.ifft(joined, axis=0)
    return jnp.real(whole[:BLOCKS]).reshape(TOKENS, -1).astype(jnp.bfloat16)


def reference(inputs, gate_in, value_weight, short_taps, filter_taps, skip_scale, output_weight):
    projected = jnp.dot(inputs, value_weight, preferred_element_type=jnp.float32).astype(jnp.bfloat16)
    extended = jnp.concatenate([jnp.zeros((2, CHANNELS), jnp.bfloat16), projected], 0)
    value = (short_taps[0] * extended[2:] + short_taps[1] * extended[1:-1] + short_taps[2] * extended[:-2]).astype(jnp.bfloat16)
    count = CHANNELS // 128
    value_blocks = value.reshape(TOKENS, count, 128).transpose(1, 0, 2)
    taps_blocks = filter_taps.reshape(TOKENS, count, 128).transpose(1, 0, 2)

    def one_block(pair):
        return spectral(pair[0], pair[1])

    convs = lax.map(one_block, (value_blocks, taps_blocks))
    conv = convs.transpose(1, 0, 2).reshape(TOKENS, CHANNELS)
    mixed = (gate_in.astype(jnp.float32) * (conv.astype(jnp.float32) + skip_scale * value.astype(jnp.float32))).astype(jnp.bfloat16)
    return jnp.dot(mixed, output_weight, preferred_element_type=jnp.float32).astype(jnp.bfloat16)
```

```python
import functools
import math

import jax
import jax.numpy as jnp
import ml_dtypes
import numpy as np
from jax import lax
from jax.experimental import pallas as pl
from jax.experimental.pallas import tpu as pltpu
from jax.sharding import PartitionSpec as P

PLANE = 4
LANES = 128
ROWS = 16
MIB = 1 << 20


def stage_tables(blocks):
    width = 2 * blocks
    b = np.arange(blocks)
    forward = [np.ones(blocks), np.cos(np.pi * b)]
    backward = [np.ones(blocks), np.cos(np.pi * b)]
    for f in range(1, blocks):
        angle = 2.0 * np.pi * (f * b % width) / width
        forward += [np.cos(angle), -np.sin(angle)]
        backward += [2.0 * np.cos(angle), -2.0 * np.sin(angle)]
    eye = np.eye(ROWS)
    first = np.kron(np.stack(forward, 0), eye)
    last = np.kron(np.stack(backward, 1), eye) / (width * LANES)
    return first.astype(ml_dtypes.bfloat16), last.astype(ml_dtypes.bfloat16)


def turned_tables(blocks, rows):
    width = 2 * blocks
    k = np.arange(rows)[:, None]
    m = np.arange(rows)[None, :]
    out = []
    for f in range(blocks + 1):
        angle = 2.0 * np.pi * ((width * k + f) * m % (width * rows)) / (width * rows)
        cos, sin = np.cos(angle), np.sin(angle)
        out.append(np.block([[cos, sin], [-sin, cos]]))
    forward = np.stack(out, 0)
    return (
        forward.astype(ml_dtypes.bfloat16),
        np.swapaxes(forward, 1, 2).astype(ml_dtypes.bfloat16),
    )


def dot(left, right):
    return jnp.dot(left, right, preferred_element_type=jnp.float32)


def call(kernel, outs, scratch, pos, args, flops):
    in_specs = [pl.BlockSpec(memory_space=pltpu.SMEM)]
    in_specs += [pl.BlockSpec(memory_space=pltpu.VMEM)] * len(args)
    moved = sum(a.size * a.dtype.itemsize for a in args)
    moved += sum(math.prod(o.shape) * o.dtype.itemsize for o in outs)
    return pl.pallas_call(
        kernel,
        out_shape=outs,
        in_specs=in_specs,
        out_specs=[pl.BlockSpec(memory_space=pltpu.VMEM)] * len(outs),
        scratch_shapes=scratch,
        compiler_params=pltpu.CompilerParams(vmem_limit_bytes=48 * MIB),
        cost_estimate=pl.CostEstimate(flops=flops, bytes_accessed=moved, transcendentals=0),
    )(pos, *args)


def block_at(pos, s, d, rows):
    block = jnp.bitwise_xor(pos[1], s) * PLANE + jnp.bitwise_xor(pos[2], d)
    return pl.multiple_of(block * rows, rows)


def project_kernel(planes, pos, *refs):
    x = refs[:PLANE]
    own = refs[PLANE]
    mine = refs[PLANE + 1 : PLANE + planes]
    other = refs[PLANE + planes : PLANE + 2 * planes - 1]
    outs = refs[PLANE + 2 * planes - 1 : PLANE + 3 * planes - 1]
    xs, ws, ps = refs[PLANE + 3 * planes - 1 :]
    rows = x[0].shape[0]
    deep = own.shape[1]
    share = outs[0].shape[1]
    half = PLANE // 2
    y = pos[0]
    for d in range(PLANE):
        xs[d * rows : (d + 1) * rows, :] = x[d][...]
        ws[pl.ds(block_at(pos, 0, d, deep), deep), :] = own[d]
    for s in range(1, planes):
        for j in range(half):
            for side, part in ((y, mine[s - 1]), (1 - y, other[s - 1])):
                at = block_at(pos, s, side * half + j, deep)
                ws[pl.ds(at, deep), :] = part[j * deep : (j + 1) * deep, :]
    ps[...] = dot(xs[...], ws[...]).astype(ps.dtype)
    for s in range(planes):
        at = pl.multiple_of(jnp.bitwise_xor(pos[1], s) * share, share)
        outs[s][...] = ps[:, pl.ds(at, share)]


def forward_stage(signal, first, work, blocks, rows):
    share = signal.shape[1]
    for pair in range(rows // (2 * ROWS)):
        halves = []
        for h in range(2):
            at = (2 * pair + h) * ROWS
            halves.append(
                jnp.concatenate(
                    [signal[b * rows + at : b * rows + at + ROWS, :] for b in range(blocks)], 0
                )
            )
        got = dot(first[...], jnp.concatenate(halves, 1)).astype(jnp.bfloat16)
        for h in range(2):
            at = (2 * pair + h) * ROWS
            for f in range(2 * blocks):
                work[f, at : at + ROWS, :] = got[
                    f * ROWS : (f + 1) * ROWS, h * share : (h + 1) * share
                ]


def spectrum_at(f, work, turned, blocks, rows):
    if f == 0 or f == blocks:
        return dot(turned[f, :, :rows], work[0 if f == 0 else 1])
    both = jnp.concatenate([work[2 * f], work[2 * f + 1]], 0)
    return dot(turned[f], both)


def taps_kernel(blocks, planes, pos, *refs):
    parts = refs[:PLANE]
    first, turned, out, signal, work = refs[PLANE:]
    rows = signal.shape[0] // blocks
    for d in range(PLANE):
        for s in range(planes):
            signal[pl.ds(block_at(pos, s, d, rows), rows), :] = parts[d][s]
    forward_stage(signal, first, work, blocks, rows)
    for f in range(blocks + 1):
        out[f] = spectrum_at(f, work, turned, blocks, rows).astype(out.dtype)


def conv_kernel(blocks, planes, pos, *refs):
    parts = refs[:planes]
    taps, skip, response, first, last, turned, back = refs[planes : planes + 7]
    outs = refs[planes + 7 : 2 * planes + 7]
    wide, value, work, result = refs[2 * planes + 7 :]
    rows = value.shape[0] // blocks
    share = value.shape[1]
    lead = wide.shape[0] - value.shape[0]
    wide[:lead, :] = jnp.zeros((lead, share), jnp.float32)
    for s in range(planes):
        for d in range(PLANE):
            at = block_at(pos, s, d, rows)
            wide[pl.ds(pl.multiple_of(lead + at, 8), rows), :] = parts[s][
                d * rows : (d + 1) * rows, :
            ].astype(jnp.float32)
    for b in range(blocks):
        at = lead + b * rows
        value[b * rows : (b + 1) * rows, :] = (
            taps[0:1, :] * wide[at : at + rows, :]
            + taps[1:2, :] * wide[at - 1 : at - 1 + rows, :]
            + taps[2:3, :] * wide[at - 2 : at - 2 + rows, :]
        ).astype(value.dtype)
    forward_stage(value, first, work, blocks, rows)
    for f in range(blocks + 1):
        got = spectrum_at(f, work, turned, blocks, rows)
        re, im = got[:rows], got[rows:]
        response_re = response[f, :rows, :].astype(jnp.float32)
        response_im = response[f, rows:, :].astype(jnp.float32)
        product = jnp.concatenate(
            [re * response_re - im * response_im, re * response_im + im * response_re], 0
        ).astype(jnp.bfloat16)
        if f == 0 or f == blocks:
            work[0 if f == 0 else 1] = dot(back[f, :rows, :], product).astype(work.dtype)
        else:
            inverse = dot(back[f], product).astype(work.dtype)
            work[2 * f] = inverse[:rows]
            work[2 * f + 1] = inverse[rows:]
    for pair in range(rows // (2 * ROWS)):
        halves = []
        for h in range(2):
            at = (2 * pair + h) * ROWS
            halves.append(
                jnp.concatenate([work[f, at : at + ROWS, :] for f in range(2 * blocks)], 0)
            )
        got = dot(last[...], jnp.concatenate(halves, 1))
        for h in range(2):
            at = (2 * pair + h) * ROWS
            for b in range(blocks):
                here = slice(b * rows + at, b * rows + at + ROWS)
                conv = got[b * ROWS : (b + 1) * ROWS, h * share : (h + 1) * share]
                result[here, :] = (
                    conv + skip[...] * value[here, :].astype(jnp.float32)
                ).astype(result.dtype)
    for s in range(planes):
        for d in range(PLANE):
            outs[s][d * rows : (d + 1) * rows, :] = result[
                pl.ds(block_at(pos, s, d, rows), rows), :
            ]


def output_kernel(planes, pos, *refs):
    u = refs[:planes]
    gate = refs[planes]
    own = refs[planes + 1]
    mine = refs[planes + 2 : 2 * planes + 1]
    other = refs[2 * planes + 1 : 3 * planes]
    outs = refs[3 * planes : 3 * planes + PLANE]
    mixed, ws = refs[3 * planes + PLANE :]
    share = u[0].shape[1]
    rows = gate.shape[1]
    half = mine[0].shape[1]
    y = pos[0]
    for s in range(planes):
        at = pl.multiple_of(jnp.bitwise_xor(pos[1], s) * share, share)
        for d in range(PLANE):
            mixed[d * rows : (d + 1) * rows, s * share : (s + 1) * share] = (
                gate[d, :, pl.ds(at, share)].astype(jnp.float32)
                * u[s][d * rows : (d + 1) * rows, :].astype(jnp.float32)
            ).astype(mixed.dtype)
        if s == 0:
            ws[:share, :] = own[...]
        else:
            here = slice(s * share, (s + 1) * share)
            ws[here, pl.ds(pl.multiple_of(y * half, half), half)] = mine[s - 1][...]
            ws[here, pl.ds(pl.multiple_of((1 - y) * half, half), half)] = other[s - 1][...]
    for d in range(PLANE):
        outs[d][...] = dot(mixed[d * rows : (d + 1) * rows, :], ws[...]).astype(outs[d].dtype)


def local(inputs, gate_in, value_weight, short_taps, filter_taps, skip_scale, output_weight):
    rows, features = inputs.shape
    deep, channels = value_weight.shape
    devices = lax.axis_size("seq")
    planes = devices // PLANE
    share = channels // devices
    wide = planes * share
    blocks = devices
    index = lax.axis_index("seq")
    y = lax.axis_index("groups")
    z, place = index // PLANE, index % PLANE
    pos = jnp.stack([y, z, place]).astype(jnp.int32)

    def to_place(block, d):
        return lax.ppermute(block, "seq", [(i, i ^ d) for i in range(devices)])

    def to_plane(block, s):
        return lax.ppermute(block, "seq", [(i, i ^ (s * PLANE)) for i in range(devices)])

    def to_group(block):
        return lax.ppermute(block, "groups", [(0, 1), (1, 0)])

    def of_place(array, d):
        cut = array.reshape(array.shape[0], planes, PLANE, share)
        at = jnp.bitwise_xor(place, d)
        return lax.dynamic_index_in_dim(cut, at, 2, keepdims=False).reshape(-1, wide)

    def around(array):
        parts = [of_place(array, 0)]
        return parts + [to_place(of_place(array, d), d) for d in range(1, PLANE)]

    first, last = stage_tables(blocks)
    turned, back = turned_tables(blocks, rows)

    value_parts = around(value_weight)
    stacked = jnp.stack(value_parts)
    half = PLANE // 2
    sent = lax.dynamic_slice_in_dim(stacked, y * half, half, 0).reshape(half * deep, wide)
    mine = [to_plane(sent, s) for s in range(1, planes)]
    other = [to_group(block) for block in mine]
    from_x = to_place(inputs, 2)
    x_parts = [inputs, to_place(inputs, 1), from_x, to_place(from_x, 1)]

    cut = filter_taps.reshape(rows, planes, PLANE * share)
    part = rows // 2

    def taps_for(s):
        block = lax.dynamic_index_in_dim(cut, jnp.bitwise_xor(z, s), 1, keepdims=False)
        return block if s == 0 else lax.dynamic_slice_in_dim(block, y * part, part, 0)

    taps_mine = jnp.stack([to_plane(taps_for(s), s) for s in range(1, planes)])
    taps_other = to_group(taps_mine)
    taps_all = jnp.where(
        y == 0,
        jnp.concatenate([taps_mine, taps_other], 1),
        jnp.concatenate([taps_other, taps_mine], 1),
    )
    taps_all = jnp.concatenate([taps_for(0)[None], taps_all], 0)
    taps_all = taps_all.reshape(planes, rows, PLANE, share)
    taps_parts = []
    for d in range(PLANE):
        block = lax.dynamic_index_in_dim(taps_all, jnp.bitwise_xor(place, d), 2, keepdims=False)
        taps_parts.append(to_place(block, d) if d else block)
    positions = blocks * rows
    response = call(
        functools.partial(taps_kernel, blocks, planes),
        [jax.ShapeDtypeStruct((blocks + 1, 2 * rows, share), jnp.bfloat16)],
        [
            pltpu.VMEM((positions, share), jnp.bfloat16),
            pltpu.VMEM((2 * blocks, rows, share), jnp.bfloat16),
        ],
        pos,
        [*taps_parts, jnp.asarray(first), jnp.asarray(turned)],
        2 * positions * share * (32 * ROWS + 4 * rows),
    )[0]

    gate = jnp.stack(around(gate_in))
    width = output_weight.shape[1] // 2
    out_half = lax.dynamic_slice_in_dim(output_weight, y * width, width, 1)
    out_mine = [to_plane(out_half, s) for s in range(1, planes)]
    out_other = [to_group(block) for block in out_mine]

    projected = call(
        functools.partial(project_kernel, planes),
        [jax.ShapeDtypeStruct((PLANE * rows, share), jnp.bfloat16)] * planes,
        [
            pltpu.VMEM((PLANE * rows, features), jnp.bfloat16),
            pltpu.VMEM((features, wide), jnp.bfloat16),
            pltpu.VMEM((PLANE * rows, wide), jnp.bfloat16),
        ],
        pos,
        [*x_parts, stacked, *mine, *other],
        2 * PLANE * rows * features * wide,
    )
    signal = [projected[0]] + [to_plane(projected[s], s) for s in range(1, planes)]
    taps = lax.dynamic_slice_in_dim(short_taps, index * share, share, 1)
    skip = lax.dynamic_slice_in_dim(skip_scale, index * share, share, 0)[None]
    mixed = call(
        functools.partial(conv_kernel, blocks, planes),
        [jax.ShapeDtypeStruct((PLANE * rows, share), jnp.bfloat16)] * planes,
        [
            pltpu.VMEM((positions + 8, share), jnp.float32),
            pltpu.VMEM((positions, share), jnp.bfloat16),
            pltpu.VMEM((2 * blocks, rows, share), jnp.bfloat16),
            pltpu.VMEM((positions, share), jnp.bfloat16),
        ],
        pos,
        [
            *signal,
            taps,
            skip,
            response,
            jnp.asarray(first),
            jnp.asarray(last),
            jnp.asarray(turned),
            jnp.asarray(back),
        ],
        4 * positions * share * (32 * ROWS + 4 * rows),
    )
    spread = [mixed[0]] + [to_plane(mixed[s], s) for s in range(1, planes)]
    partial = call(
        functools.partial(output_kernel, planes),
        [
            jax.ShapeDtypeStruct((rows, features), jnp.bfloat16 if d % 2 else jnp.float32)
            for d in range(PLANE)
        ],
        [
            pltpu.VMEM((PLANE * rows, wide), jnp.bfloat16),
            pltpu.VMEM((wide, features), jnp.bfloat16),
        ],
        pos,
        [*spread, gate, output_weight, *out_mine, *out_other],
        2 * PLANE * rows * features * wide,
    )
    across = partial[2] + to_place(partial[3], 1).astype(jnp.float32)
    across = to_place(across.astype(jnp.bfloat16), 2).astype(jnp.float32)
    beside = to_place(partial[1], 1).astype(jnp.float32)
    return (partial[0] + beside + across).astype(jnp.bfloat16)


def passed_along(block, axis, distance):
    devices = range(lax.axis_size(axis))
    route = [(i - distance, i) for i in devices if i - distance in devices]
    return lax.ppermute(block, axis, route)


def local_narrow(inputs, gate_in, value_weight, short_taps, filter_taps, skip_scale, output_weight):
    rows, features = inputs.shape
    channels = value_weight.shape[1]
    blocks = lax.axis_size("seq")
    share = channels // blocks
    index = lax.axis_index("seq")
    projected = dot(inputs, lax.all_gather(value_weight, "seq", axis=0, tiled=True)).astype(
        jnp.bfloat16
    )
    earlier = passed_along(projected[rows - 2 :], "seq", 1)
    extended = jnp.concatenate([earlier, projected], 0).astype(jnp.float32)
    value = (
        short_taps[0] * extended[2:]
        + short_taps[1] * extended[1:-1]
        + short_taps[2] * extended[:-2]
    ).astype(jnp.bfloat16)

    def by_channel(signal):
        cut = signal.reshape(rows, blocks, share)
        got = lax.all_to_all(cut, "seq", split_axis=1, concat_axis=0, tiled=True)
        return got.reshape(blocks, rows, share)

    grid = np.arange(2 * blocks)
    angle = 2.0 * np.pi * (grid[:, None] * grid[None, :] % (2 * blocks)) / (2 * blocks)
    wide = np.exp(-1j * angle)[: blocks + 1, :blocks]
    turned, back = (jnp.asarray(t) for t in turned_tables(blocks, rows))
    weight = np.full((blocks + 1, 1), 2.0)
    weight[0] = weight[-1] = 1.0
    narrow = weight * np.conj(wide) / (2 * blocks * rows)

    def einsum(form, table, data):
        return jnp.einsum(form, table, data, preferred_element_type=jnp.float32)

    def table(values):
        return jnp.asarray(values.astype(ml_dtypes.bfloat16))

    def forward(signal):
        re = einsum("fb,bmc->fmc", table(np.real(wide)), signal)
        im = einsum("fb,bmc->fmc", table(np.imag(wide)), signal)
        both = jnp.concatenate([re, im], 1).astype(jnp.bfloat16)
        return einsum("fkm,fmc->fkc", turned, both)

    response = forward(by_channel(filter_taps))
    got = forward(by_channel(value))
    re, im = got[:, :rows], got[:, rows:]
    response_re, response_im = response[:, :rows], response[:, rows:]
    product = jnp.concatenate(
        [re * response_re - im * response_im, re * response_im + im * response_re], 1
    ).astype(jnp.bfloat16)
    inverse = einsum("fmk,fkc->fmc", back, product).astype(jnp.bfloat16)
    conv = einsum("fb,fmc->bmc", table(np.real(narrow)), inverse[:, :rows]) - einsum(
        "fb,fmc->bmc", table(np.imag(narrow)), inverse[:, rows:]
    )
    conv = lax.all_to_all(
        conv.astype(jnp.bfloat16), "seq", split_axis=0, concat_axis=2, tiled=True
    ).reshape(rows, channels)
    mixed = (
        gate_in.astype(jnp.float32)
        * (conv.astype(jnp.float32) + skip_scale * value.astype(jnp.float32))
    ).astype(jnp.bfloat16)
    result = dot(mixed, lax.all_gather(output_weight, "seq", axis=0, tiled=True))
    return result.astype(jnp.bfloat16)


def solution(mesh):
    split = P(("groups", "seq"), None)
    placed = (split, split, P("seq", None), P(), P("seq", None), P(), P("seq", None))

    def run(*args):
        devices = mesh.shape["seq"]
        share = args[2].shape[1] // devices
        tiled = share % LANES == 0 and args[0].shape[0] // mesh.size == LANES
        paired = devices % PLANE == 0 and mesh.shape["groups"] == 2
        body = local if tiled and paired and devices & (devices - 1) == 0 else local_narrow
        return jax.shard_map(body, mesh=mesh, in_specs=placed, out_specs=split, check_vma=False)(
            *args
        )

    return run
```

```python
import functools
import math

import jax
import jax.numpy as jnp
import ml_dtypes
import numpy as np
from jax import lax
from jax.experimental import pallas as pl
from jax.experimental.pallas import tpu as pltpu
from jax.sharding import PartitionSpec as P

PLANE = 4
LANES = 128
ROWS = 16
MIB = 1 << 20


def stage_tables(blocks):
    width = 2 * blocks
    b = np.arange(blocks)
    forward = [np.ones(blocks), np.cos(np.pi * b)]
    backward = [np.ones(blocks), np.cos(np.pi * b)]
    for f in range(1, blocks):
        angle = 2.0 * np.pi * (f * b % width) / width
        forward += [np.cos(angle), -np.sin(angle)]
        backward += [2.0 * np.cos(angle), -2.0 * np.sin(angle)]
    eye = np.eye(ROWS)
    first = np.kron(np.stack(forward, 0), eye)
    last = np.kron(np.stack(backward, 1), eye) / (width * LANES)
    return first.astype(ml_dtypes.bfloat16), last.astype(ml_dtypes.bfloat16)


def turned_tables(blocks, rows):
    width = 2 * blocks
    k = np.arange(rows)[:, None]
    m = np.arange(rows)[None, :]
    out = []
    for f in range(blocks + 1):
        angle = 2.0 * np.pi * ((width * k + f) * m % (width * rows)) / (width * rows)
        cos, sin = np.cos(angle), np.sin(angle)
        out.append(np.block([[cos, sin], [-sin, cos]]))
    forward = np.stack(out, 0)
    return (
        forward.astype(ml_dtypes.bfloat16),
        np.swapaxes(forward, 1, 2).astype(ml_dtypes.bfloat16),
    )


def dot(left, right):
    return jnp.dot(left, right, preferred_element_type=jnp.float32)


def call(kernel, outs, scratch, pos, args, flops, vmem=4):
    in_specs = [pl.BlockSpec(memory_space=pltpu.SMEM)]
    in_specs += [pl.BlockSpec(memory_space=pltpu.VMEM)] * len(args)
    moved = sum(a.size * a.dtype.itemsize for a in args)
    moved += sum(math.prod(o.shape) * o.dtype.itemsize for o in outs)
    return pl.pallas_call(
        kernel,
        out_shape=outs,
        in_specs=in_specs,
        out_specs=[pl.BlockSpec(memory_space=pltpu.VMEM)] * len(outs),
        scratch_shapes=scratch,
        compiler_params=pltpu.CompilerParams(vmem_limit_bytes=vmem * MIB),
        cost_estimate=pl.CostEstimate(flops=flops, bytes_accessed=moved, transcendentals=0),
    )(pos, *args)


def block_at(pos, s, d, rows):
    block = jnp.bitwise_xor(pos[1], s) * PLANE + jnp.bitwise_xor(pos[2], d)
    return pl.multiple_of(block * rows, rows)


def split_kernel(share, pos, src, *outs):
    rows = src.shape[0]
    for d in range(PLANE):
        out = outs[min(d, len(outs) - 1)]
        first = (d - len(outs) + 1) * rows if d >= len(outs) else 0
        place = jnp.bitwise_xor(pos[2], d)
        for p in range(out.shape[1] // share):
            at = pl.multiple_of((p * PLANE + place) * share, share)
            out[first : first + rows, p * share : (p + 1) * share] = src[:, pl.ds(at, share)]


def filter_kernel(pos, taps, own, whole, half):
    wide = own.shape[1]
    part = half.shape[0]

    def columns(s):
        return pl.ds(pl.multiple_of(jnp.bitwise_xor(pos[1], s) * wide, wide), wide)

    own[...] = taps[:, columns(0)]
    whole[...] = taps[:, columns(1 + pos[0])]
    half[...] = taps[pl.ds(pl.multiple_of(pos[0] * part, part), part), columns(3)]


def half_kernel(pos, *refs):
    parts, (whole, half), (out, lower, upper, joined) = refs[:PLANE], refs[PLANE:-4], refs[-4:]
    deep = parts[0].shape[0]
    for y in range(2):

        @pl.when(pos[0] == y)
        def _():
            for j, far in enumerate((lower, upper)):
                out[j * deep : (j + 1) * deep, :] = parts[2 * y + j][...]
                far[...] = parts[2 * y + j][...]

    joined[: whole.shape[0], :] = whole[...]
    joined[whole.shape[0] :, :] = half[...]


def join(out, parts):
    at = 0
    for part in parts:
        out[at : at + part.shape[0], :] = part[...]
        at += part.shape[0]


def join_kernel(pos, near, far_a, far_b, x, from_x, weight, *outs):
    got, passed, both_x, out_a, out_b, out_half = outs
    join(got, (near, far_a, far_b))
    join(passed, (far_a, far_b))
    join(both_x, (x, from_x))
    part, width = out_a.shape
    columns = pl.ds(pl.multiple_of(pos[0] * width, width), width)
    out_a[...] = weight[:part, columns]
    out_b[...] = weight[part:, columns]
    out_half[...] = weight[:, columns]


def pair_kernel(pos, first, second, out):
    join(out, (first, second))


def places_kernel(pos, own, mine, other, *outs):
    planes, rows, share = outs[0].shape
    part = rows // 2
    for d, out in enumerate(outs):
        columns = pl.ds(pl.multiple_of(jnp.bitwise_xor(pos[2], d) * share, share), share)
        out[0] = own[:, columns]
        for side, block in ((pos[0], mine), (1 - pos[0], other)):
            out[1 + side] = block[:rows, columns]
            out[3, pl.ds(pl.multiple_of(side * part, part), part), :] = block[rows:, columns]


def project_kernel(planes, pos, *refs):
    x, from_x, beside = refs[:3]
    own, halves = refs[3 : 3 + PLANE], refs[3 + PLANE : 7 + PLANE]
    out_near, out_a, out_b = refs[7 + PLANE : 10 + PLANE]
    outs, (out_got, out_passed) = refs[10 + PLANE : 10 + PLANE + planes], refs[-5:-3]
    xs, ws, ps = refs[-3:]
    rows = x.shape[0]
    deep = own[0].shape[0]
    share = outs[0].shape[1]

    def put(s, d, block):
        ws[pl.ds(block_at(pos, s, d, deep), deep), :] = block

    join(xs, (x, beside.at[:rows], from_x, beside.at[rows:]))
    for d in range(PLANE):
        put(0, d, own[d][...])
    for k in range(2):
        got, passed = halves[2 * k : 2 * k + 2]
        d = 2 * (pos[0] if k == 0 else 1 - pos[0])
        for i, (s, j) in enumerate(((1, 0), (1, 1), (2, 0), (3, 1))):
            put(s, d + j, got[i * deep : (i + 1) * deep, :])
        put(3, d, passed[:deep, :])
        put(2, d + 1, passed[deep:, :])
    ps[...] = dot(xs[...], ws[...]).astype(ps.dtype)
    for s in range(planes):
        at = pl.multiple_of(jnp.bitwise_xor(pos[1], s) * share, share)
        outs[s][...] = ps[:, pl.ds(at, share)]
    join(out_got, (out_near, out_a, out_b))
    join(out_passed, (out_a, out_b))


def forward_stage(signal, first, work, blocks, rows):
    share = signal.shape[1]
    for pair in range(rows // (2 * ROWS)):
        halves = []
        for h in range(2):
            at = (2 * pair + h) * ROWS
            halves.append(
                jnp.concatenate(
                    [signal[b * rows + at : b * rows + at + ROWS, :] for b in range(blocks)], 0
                )
            )
        got = dot(first[...], jnp.concatenate(halves, 1)).astype(jnp.bfloat16)
        for h in range(2):
            at = (2 * pair + h) * ROWS
            for f in range(2 * blocks):
                work[f, at : at + ROWS, :] = got[
                    f * ROWS : (f + 1) * ROWS, h * share : (h + 1) * share
                ]


def spectrum_at(f, work, turned, blocks, rows):
    if f == 0 or f == blocks:
        return dot(turned[f, :, :rows], work[0 if f == 0 else 1])
    both = jnp.concatenate([work[2 * f], work[2 * f + 1]], 0)
    return dot(turned[f], both)


def taps_kernel(blocks, planes, pos, *refs):
    parts = refs[:PLANE]
    first, turned, out, signal, work = refs[PLANE:]
    rows = signal.shape[0] // blocks
    for d in range(PLANE):
        for s in range(planes):
            signal[pl.ds(block_at(pos, s, d, rows), rows), :] = parts[d][s]
    forward_stage(signal, first, work, blocks, rows)
    for f in range(blocks + 1):
        out[f] = spectrum_at(f, work, turned, blocks, rows).astype(out.dtype)


def conv_kernel(blocks, planes, pos, *refs):
    parts = refs[:planes]
    taps, skip, response, first, last, turned, back = refs[planes : planes + 7]
    outs = refs[planes + 7 : 3 * planes + 7]
    wide, value, work, result = refs[3 * planes + 7 :]
    rows = value.shape[0] // blocks
    share = value.shape[1]
    lead = wide.shape[0] - value.shape[0]
    wide[:lead, :] = jnp.zeros((lead, share), jnp.float32)
    for s in range(planes):
        for d in range(PLANE):
            at = block_at(pos, s, d, rows)
            wide[pl.ds(pl.multiple_of(lead + at, 8), rows), :] = parts[s][
                d * rows : (d + 1) * rows, :
            ].astype(jnp.float32)
    for b in range(blocks):
        at = lead + b * rows
        value[b * rows : (b + 1) * rows, :] = (
            taps[0:1, :] * wide[at : at + rows, :]
            + taps[1:2, :] * wide[at - 1 : at - 1 + rows, :]
            + taps[2:3, :] * wide[at - 2 : at - 2 + rows, :]
        ).astype(value.dtype)
    forward_stage(value, first, work, blocks, rows)
    for f in range(blocks + 1):
        got = spectrum_at(f, work, turned, blocks, rows)
        re, im = got[:rows], got[rows:]
        response_re = response[f, :rows, :].astype(jnp.float32)
        response_im = response[f, rows:, :].astype(jnp.float32)
        product = jnp.concatenate(
            [re * response_re - im * response_im, re * response_im + im * response_re], 0
        ).astype(jnp.bfloat16)
        if f == 0 or f == blocks:
            work[0 if f == 0 else 1] = dot(back[f, :rows, :], product).astype(work.dtype)
        else:
            inverse = dot(back[f], product).astype(work.dtype)
            work[2 * f] = inverse[:rows]
            work[2 * f + 1] = inverse[rows:]
    for pair in range(rows // (2 * ROWS)):
        halves = []
        for h in range(2):
            at = (2 * pair + h) * ROWS
            halves.append(
                jnp.concatenate([work[f, at : at + ROWS, :] for f in range(2 * blocks)], 0)
            )
        got = dot(last[...], jnp.concatenate(halves, 1))
        for h in range(2):
            at = (2 * pair + h) * ROWS
            for b in range(blocks):
                here = slice(b * rows + at, b * rows + at + ROWS)
                conv = got[b * ROWS : (b + 1) * ROWS, h * share : (h + 1) * share]
                result[here, :] = (
                    conv + skip[...] * value[here, :].astype(jnp.float32)
                ).astype(result.dtype)
    for s in range(planes):
        for d in range(PLANE):
            half, at = d // 2, d % 2 * rows
            outs[half * planes + s][at : at + rows, :] = result[
                pl.ds(block_at(pos, s, d, rows), rows), :
            ]


def mixed_dots(planes, pos, u, gate, ws, mixed, outs):
    share = u[0].shape[1]
    rows = gate[0].shape[0]
    for s in range(planes):
        at = pl.multiple_of(jnp.bitwise_xor(pos[1], s) * share, share)
        for d in range(2):
            mixed[d * rows : (d + 1) * rows, s * share : (s + 1) * share] = (
                gate[d][:, pl.ds(at, share)].astype(jnp.float32)
                * u[s][d * rows : (d + 1) * rows, :].astype(jnp.float32)
            ).astype(mixed.dtype)
    got = dot(mixed[...], ws[...])
    for d in range(2):
        outs[d][...] = got[d * rows : (d + 1) * rows].astype(outs[d].dtype)


def upper_kernel(planes, pos, *refs):
    u, gate = refs[:planes], refs[planes : planes + 2]
    own, halves = refs[planes + 2], refs[planes + 3 : planes + 7]
    outs, ws, mixed = refs[planes + 7 : planes + 9], refs[planes + 9], refs[planes + 10]
    share = u[0].shape[1]
    width = halves[0].shape[1]
    part = share // 2
    ws[:share, :] = own[...]
    for k in range(2):
        got, passed = halves[2 * k : 2 * k + 2]
        side = pos[0] if k == 0 else 1 - pos[0]
        columns = pl.ds(pl.multiple_of(side * width, width), width)
        ws[share : 2 * share, columns] = got[:share, :]
        ws[2 * share : 2 * share + part, columns] = got[share : share + part, :]
        ws[2 * share + part : 3 * share, columns] = passed[part:, :]
        ws[3 * share : 3 * share + part, columns] = passed[:part, :]
        ws[3 * share + part :, columns] = got[share + part :, :]
    mixed_dots(planes, pos, u, gate, ws, mixed, outs)


def lower_kernel(planes, pos, *refs):
    u, gate, ws = refs[:planes], refs[planes : planes + 2], refs[planes + 2]
    mixed_dots(planes, pos, u, gate, ws, refs[planes + 5], refs[planes + 3 : planes + 5])


def local(inputs, gate_in, value_weight, short_taps, filter_taps, skip_scale, output_weight):
    rows, features = inputs.shape
    deep, channels = value_weight.shape
    devices = lax.axis_size("seq")
    planes = devices // PLANE
    share = channels // devices
    wide = planes * share
    blocks = devices
    index = lax.axis_index("seq")
    y = lax.axis_index("groups")
    z, place = index // PLANE, index % PLANE
    pos = jnp.stack([y, z, place]).astype(jnp.int32)

    def to_place(block, d):
        return lax.ppermute(block, "seq", [(i, i ^ d) for i in range(devices)])

    def to_plane(block, s):
        return lax.ppermute(block, "seq", [(i, i ^ (s * PLANE)) for i in range(devices)])

    def to_group(block):
        return lax.ppermute(block, "groups", [(0, 1), (1, 0)])

    def shaped(*shape, dtype=jnp.bfloat16):
        return jax.ShapeDtypeStruct(shape, dtype)

    def small(kernel, outs, *args):
        return list(call(kernel, outs, [], pos, args, 0, vmem=2))

    def split(array, *heights):
        kernel = functools.partial(split_kernel, share)
        return small(kernel, [shaped(rows * h, wide) for h in heights], array)

    stage = lax.optimization_barrier
    first, last, turned, back = (
        jnp.asarray(t) for t in (*stage_tables(blocks), *turned_tables(blocks, rows))
    )
    part, width, positions = rows // 2, features // 2, blocks * rows

    cut = split(value_weight, 1, 1, 1, 1)
    taps_in, cut[0] = stage((filter_taps, cut[0]))
    taps_own, taps_whole, taps_half = small(
        filter_kernel, [shaped(rows, wide), shaped(rows, wide), shaped(part, wide)], taps_in
    )
    cut = [cut[0]] + [to_place(cut[d], d) for d in range(1, PLANE)]
    route = [
        (y0 * devices + i, y0 * devices + (i ^ (1 + y0) * PLANE))
        for y0 in range(2)
        for i in range(devices)
    ]
    taps_whole = lax.ppermute(taps_whole, ("groups", "seq"), route)
    taps_half = to_plane(taps_half, 3)
    cut, taps_whole, taps_half, late = stage((cut, taps_whole, taps_half, inputs))

    sent, lower, upper, taps_mine = small(
        half_kernel,
        [shaped(2 * deep, wide), shaped(deep, wide), shaped(deep, wide), shaped(rows + part, wide)],
        *cut,
        taps_whole,
        taps_half,
    )
    near, far_a, far_b = to_plane(sent, 1), to_plane(lower, 2), to_plane(upper, 3)
    from_x = to_place(late, 2)
    taps_other = to_group(taps_mine)
    near, far_a, far_b, from_x, taps_other, late = stage(
        (near, far_a, far_b, from_x, taps_other, output_weight)
    )

    got, passed, both_x, out_a, out_b, out_half = small(
        join_kernel,
        [shaped(4 * deep, wide), shaped(2 * deep, wide), shaped(2 * rows, features)]
        + [shaped(deep // 2, width), shaped(deep // 2, width), shaped(deep, width)],
        near,
        far_a,
        far_b,
        inputs,
        from_x,
        late,
    )
    passed = to_plane(passed, 1)
    got_other = to_group(got)
    out_a, out_b = to_plane(out_a, 2), to_plane(out_b, 3)
    beside = to_place(both_x, 1)
    taps_parts = small(
        places_kernel, [shaped(planes, rows, share)] * PLANE, taps_own, taps_mine, taps_other
    )
    passed, got_other, out_a, out_b, beside, taps_parts, out_half = stage(
        (passed, got_other, out_a, out_b, beside, taps_parts, out_half)
    )

    passed_other = to_group(passed)
    out_near = to_plane(out_half, 1)
    taps_parts = [taps_parts[0]] + [to_place(taps_parts[d], d) for d in range(1, PLANE)]
    passed, passed_other, out_near, taps_parts, late = stage(
        (passed, passed_other, out_near, taps_parts, gate_in)
    )

    gate_own, gate_beside, gate_x = split(late, 1, 1, 2)
    *projected, out_got, out_passed = call(
        functools.partial(project_kernel, planes),
        [shaped(PLANE * rows, share)] * planes + [shaped(2 * deep, width), shaped(deep, width)],
        [
            pltpu.VMEM((PLANE * rows, features), jnp.bfloat16),
            pltpu.VMEM((features, wide), jnp.bfloat16),
            pltpu.VMEM((PLANE * rows, wide), jnp.bfloat16),
        ],
        pos,
        [inputs, from_x, beside, *cut, got, passed, got_other, passed_other]
        + [out_near, out_a, out_b],
        2 * PLANE * rows * features * wide,
        vmem=12,
    )
    projected, out_got, out_passed, gate_x = stage((projected, out_got, out_passed, gate_x))

    def spread(parts):
        return [parts[0]] + [to_plane(parts[s], s) for s in range(1, planes)]

    signal = spread(projected)
    out_other = to_group(out_got)
    gate_x = to_place(gate_x, 2)
    response = call(
        functools.partial(taps_kernel, blocks, planes),
        [shaped(blocks + 1, 2 * rows, share)],
        [
            pltpu.VMEM((positions, share), jnp.bfloat16),
            pltpu.VMEM((2 * blocks, rows, share), jnp.bfloat16),
        ],
        pos,
        [*taps_parts, first, turned],
        2 * positions * share * (32 * ROWS + 4 * rows),
        vmem=8,
    )[0]
    taps = lax.dynamic_slice_in_dim(short_taps, index * share, share, 1)
    skip = lax.dynamic_slice_in_dim(skip_scale, index * share, share, 0)[None]
    signal, out_other, gate_x, response, taps, skip, out_passed = stage(
        (signal, out_other, gate_x, response, taps, skip, out_passed)
    )

    out_passed = to_plane(out_passed, 1)
    mixed = call(
        functools.partial(conv_kernel, blocks, planes),
        [shaped(2 * rows, share)] * (2 * planes),
        [
            pltpu.VMEM((positions + 8, share), jnp.float32),
            pltpu.VMEM((positions, share), jnp.bfloat16),
            pltpu.VMEM((2 * blocks, rows, share), jnp.bfloat16),
            pltpu.VMEM((positions, share), jnp.bfloat16),
        ],
        pos,
        [*signal, taps, skip, response, first, last, turned, back],
        4 * positions * share * (32 * ROWS + 4 * rows),
        vmem=12,
    )
    gate_beside = small(pair_kernel, [shaped(2 * rows, wide)], gate_beside, gate_x[rows:])[0]
    mixed, out_passed, gate_beside = stage((mixed, out_passed, gate_beside))

    upper = spread(mixed[planes:])
    passed_other = to_group(out_passed)
    gate_beside = to_place(gate_beside, 1)
    upper, passed_other, gate_beside, lower = stage(
        (upper, passed_other, gate_beside, mixed[:planes])
    )
    scratch = [pltpu.VMEM((2 * rows, wide), jnp.bfloat16)]
    flops = 4 * rows * features * wide
    partial_two, partial_three, gathered = call(
        functools.partial(upper_kernel, planes),
        [shaped(rows, features, dtype=jnp.float32), shaped(rows, features)]
        + [shaped(wide, features)],
        scratch,
        pos,
        [*upper, gate_x[:rows], gate_beside[rows:], output_weight]
        + [out_got, out_passed, out_other, passed_other],
        flops,
        vmem=12,
    )
    across = partial_two + to_place(partial_three, 1).astype(jnp.float32)
    across, lower = stage((across.astype(jnp.bfloat16), lower))

    across = to_place(across, 2)
    lower = spread(lower)
    partial_zero, partial_one = call(
        functools.partial(lower_kernel, planes),
        [shaped(rows, features, dtype=jnp.float32), shaped(rows, features)],
        scratch,
        pos,
        [*lower, gate_own, gate_beside[:rows], gathered],
        flops,
        vmem=12,
    )
    result = partial_zero + to_place(partial_one, 1).astype(jnp.float32)
    return (result + across.astype(jnp.float32)).astype(jnp.bfloat16)


def passed_along(block, axis, distance):
    devices = range(lax.axis_size(axis))
    route = [(i - distance, i) for i in devices if i - distance in devices]
    return lax.ppermute(block, axis, route)


def local_narrow(inputs, gate_in, value_weight, short_taps, filter_taps, skip_scale, output_weight):
    rows, features = inputs.shape
    channels = value_weight.shape[1]
    blocks = lax.axis_size("seq")
    share = channels // blocks
    index = lax.axis_index("seq")
    projected = dot(inputs, lax.all_gather(value_weight, "seq", axis=0, tiled=True)).astype(
        jnp.bfloat16
    )
    earlier = passed_along(projected[rows - 2 :], "seq", 1)
    extended = jnp.concatenate([earlier, projected], 0).astype(jnp.float32)
    value = (
        short_taps[0] * extended[2:]
        + short_taps[1] * extended[1:-1]
        + short_taps[2] * extended[:-2]
    ).astype(jnp.bfloat16)

    def by_channel(signal):
        cut = signal.reshape(rows, blocks, share)
        got = lax.all_to_all(cut, "seq", split_axis=1, concat_axis=0, tiled=True)
        return got.reshape(blocks, rows, share)

    grid = np.arange(2 * blocks)
    angle = 2.0 * np.pi * (grid[:, None] * grid[None, :] % (2 * blocks)) / (2 * blocks)
    wide = np.exp(-1j * angle)[: blocks + 1, :blocks]
    turned, back = (jnp.asarray(t) for t in turned_tables(blocks, rows))
    weight = np.full((blocks + 1, 1), 2.0)
    weight[0] = weight[-1] = 1.0
    narrow = weight * np.conj(wide) / (2 * blocks * rows)

    def einsum(form, table, data):
        return jnp.einsum(form, table, data, preferred_element_type=jnp.float32)

    def table(values):
        return jnp.asarray(values.astype(ml_dtypes.bfloat16))

    def forward(signal):
        re = einsum("fb,bmc->fmc", table(np.real(wide)), signal)
        im = einsum("fb,bmc->fmc", table(np.imag(wide)), signal)
        both = jnp.concatenate([re, im], 1).astype(jnp.bfloat16)
        return einsum("fkm,fmc->fkc", turned, both)

    response = forward(by_channel(filter_taps))
    got = forward(by_channel(value))
    re, im = got[:, :rows], got[:, rows:]
    response_re, response_im = response[:, :rows], response[:, rows:]
    product = jnp.concatenate(
        [re * response_re - im * response_im, re * response_im + im * response_re], 1
    ).astype(jnp.bfloat16)
    inverse = einsum("fmk,fkc->fmc", back, product).astype(jnp.bfloat16)
    conv = einsum("fb,fmc->bmc", table(np.real(narrow)), inverse[:, :rows]) - einsum(
        "fb,fmc->bmc", table(np.imag(narrow)), inverse[:, rows:]
    )
    conv = lax.all_to_all(
        conv.astype(jnp.bfloat16), "seq", split_axis=0, concat_axis=2, tiled=True
    ).reshape(rows, channels)
    mixed = (
        gate_in.astype(jnp.float32)
        * (conv.astype(jnp.float32) + skip_scale * value.astype(jnp.float32))
    ).astype(jnp.bfloat16)
    result = dot(mixed, lax.all_gather(output_weight, "seq", axis=0, tiled=True))
    return result.astype(jnp.bfloat16)


def solution(mesh):
    split = P(("groups", "seq"), None)
    placed = (split, split, P("seq", None), P(), P("seq", None), P(), P("seq", None))

    def run(*args):
        devices = mesh.shape["seq"]
        share = args[2].shape[1] // devices
        tiled = share % LANES == 0 and args[0].shape[0] // mesh.size == LANES
        paired = devices == 4 * PLANE and mesh.shape["groups"] == 2
        body = local if tiled and paired else local_narrow
        return jax.shard_map(body, mesh=mesh, in_specs=placed, out_specs=split, check_vma=False)(
            *args
        )

    return run
```

```python
import functools
import math

import jax
import jax.numpy as jnp
import ml_dtypes
import numpy as np
from jax import lax
from jax.experimental import pallas as pl
from jax.experimental.pallas import tpu as pltpu
from jax.sharding import PartitionSpec as P

PLANE = 4
LANES = 128
ROWS = 16
MIB = 1 << 20


def stage_tables(blocks):
    width = 2 * blocks
    b = np.arange(blocks)
    forward = [np.ones(blocks), np.cos(np.pi * b)]
    backward = [np.ones(blocks), np.cos(np.pi * b)]
    for f in range(1, blocks):
        angle = 2.0 * np.pi * (f * b % width) / width
        forward += [np.cos(angle), -np.sin(angle)]
        backward += [2.0 * np.cos(angle), -2.0 * np.sin(angle)]
    eye = np.eye(ROWS)
    first = np.kron(np.stack(forward, 0), eye)
    last = np.kron(np.stack(backward, 1), eye) / (width * LANES)
    return first.astype(ml_dtypes.bfloat16), last.astype(ml_dtypes.bfloat16)


def turned_tables(blocks, rows):
    width = 2 * blocks
    k = np.arange(rows)[:, None]
    m = np.arange(rows)[None, :]
    out = []
    for f in range(blocks + 1):
        angle = 2.0 * np.pi * ((width * k + f) * m % (width * rows)) / (width * rows)
        cos, sin = np.cos(angle), np.sin(angle)
        out.append(np.block([[cos, sin], [-sin, cos]]))
    forward = np.stack(out, 0)
    return (
        forward.astype(ml_dtypes.bfloat16),
        np.swapaxes(forward, 1, 2).astype(ml_dtypes.bfloat16),
    )


def dot(left, right):
    return jnp.dot(left, right, preferred_element_type=jnp.float32)


def call(kernel, outs, scratch, pos, args, flops, vmem=4, fetched=0):
    in_specs = [pl.BlockSpec(memory_space=pltpu.SMEM)]
    in_specs += [pl.BlockSpec(memory_space=pltpu.HBM)] * fetched
    in_specs += [pl.BlockSpec(memory_space=pltpu.VMEM)] * (len(args) - fetched)
    moved = sum(a.size * a.dtype.itemsize for a in args) if flops else 0
    moved += sum(math.prod(o.shape) * o.dtype.itemsize for o in outs) if flops else 0
    return pl.pallas_call(
        kernel,
        out_shape=outs,
        in_specs=in_specs,
        out_specs=[pl.BlockSpec(memory_space=pltpu.VMEM)] * len(outs),
        scratch_shapes=scratch,
        compiler_params=pltpu.CompilerParams(vmem_limit_bytes=vmem * MIB),
        cost_estimate=pl.CostEstimate(flops=flops, bytes_accessed=moved, transcendentals=0),
    )(pos, *args)


def block_at(pos, s, d, rows):
    block = jnp.bitwise_xor(pos[1], s) * PLANE + jnp.bitwise_xor(pos[2], d)
    return pl.multiple_of(block * rows, rows)


def fetch(pairs, sems):
    copies = [pltpu.make_async_copy(src, dst, sems.at[i]) for i, (src, dst) in enumerate(pairs)]
    for copy in copies:
        copy.start()
    return copies


def start_kernel(share, pos, weight, taps, out_weight, *refs):
    outs, (own, whole, near, out_half) = refs[:PLANE], refs[PLANE : PLANE + 4]
    weight_here, taps_here, sems = refs[PLANE + 4 :]
    rows, wide = own.shape
    deep, width = out_half.shape
    quarter = rows // 4
    side = pl.ds(pl.multiple_of(pos[0] * width, width), width)
    pairs = []
    for source, here in ((weight, weight_here), (taps, taps_here)):
        for q in range(4):
            cut = pl.ds(q * quarter, quarter)
            pairs.append((source.at[cut], here.at[cut]))
    pairs.append((out_weight.at[:, side], out_half))
    copies = fetch(pairs, sems)
    for copy in copies[:4]:
        copy.wait()
    for d, out in enumerate(outs):
        place = jnp.bitwise_xor(pos[2], d)
        for p in range(wide // share):
            at = pl.multiple_of((p * PLANE + place) * share, share)
            out[:, p * share : (p + 1) * share] = weight_here[:, pl.ds(at, share)]
    for copy in copies[4:]:
        copy.wait()

    def columns(s):
        return pl.ds(pl.multiple_of(jnp.bitwise_xor(pos[1], s) * wide, wide), wide)

    own[...] = taps_here[:, columns(0)]
    whole[...] = taps_here[:, columns(2 + pos[0])]
    near[:deep, :] = out_half[...]
    for q in range(2):
        first = pl.multiple_of(pos[0] * (rows // 2) + q * quarter, quarter)
        near[deep:, q * wide : (q + 1) * wide] = taps_here[pl.ds(first, quarter), columns(1)]


def across_kernel(share, pos, x, gate, own, core, across, sems):
    rows = x.shape[0]
    part, wide = rows // 4, own.shape[1]
    pairs = [(x, core.at[pl.ds(0, rows)]), (x, across.at[pl.ds(0, rows)])]
    for d in range(PLANE):
        place = jnp.bitwise_xor(pos[2], d)
        for p in range(wide // share):
            at = pl.multiple_of((p * PLANE + place) * share, share)
            if d == 0:
                here = pl.ds(p * share, share)
                pairs.append((gate.at[:, pl.ds(at, share)], own.at[:, here]))
                continue
            out, first = (core, rows) if d == 1 else (across, rows + (d - 2) * part)
            for q in range(4):
                columns = pl.ds(q * wide + p * share, share)
                source = gate.at[pl.ds(q * part, part), pl.ds(at, share)]
                pairs.append((source, out.at[pl.ds(first, part), columns]))
    for copy in fetch(pairs, sems):
        copy.wait()


def unfold_kernel(pos, core, from_x, both, *outs):
    rows, wide = outs[0].shape
    part = rows // 4
    for source, first, out in zip((core, from_x, both), (0, 0, part), outs):
        for q in range(4):
            out[q * part : (q + 1) * part, :] = source[
                rows + first : rows + first + part, q * wide : (q + 1) * wide
            ]


def join(out, parts):
    at = 0
    for part in parts:
        out[at : at + part.shape[0], :] = part[...]
        at += part.shape[0]


def half_kernel(pos, *refs):
    parts, (whole, near), (out, joined) = refs[:PLANE], refs[PLANE:-2], refs[-2:]
    deep = parts[0].shape[0]
    rows, wide = whole.shape
    quarter = rows // 4
    for y in range(2):

        @pl.when(pos[0] == y)
        def _():
            for j in range(2):
                out[j * deep : (j + 1) * deep, :] = parts[2 * y + j][...]

    joined[:rows, :] = whole[...]
    for q in range(2):
        here = slice(rows + q * quarter, rows + (q + 1) * quarter)
        joined[here, :] = near[deep:, q * wide : (q + 1) * wide]


def join_kernel(pos, *refs):
    join(refs[-1], refs[:-1])


def places_kernel(pos, own, mine, other, *outs):
    planes, rows, share = outs[0].shape
    part = rows // 2
    for d, out in enumerate(outs):
        columns = pl.ds(pl.multiple_of(jnp.bitwise_xor(pos[2], d) * share, share), share)
        out[0] = own[:, columns]
        for side, block in ((pos[0], mine), (1 - pos[0], other)):
            out[2 + side] = block[:rows, columns]
            out[1, pl.ds(pl.multiple_of(side * part, part), part), :] = block[rows:, columns]


def project_kernel(planes, pos, x, core, from_x, both, own, *refs):
    halves, outs = refs[: 2 * planes - 2], refs[2 * planes - 2 : -3]
    xs, ws, ps = refs[-3:]
    rows = x.shape[0]
    deep = own.shape[0] // PLANE
    share = outs[0].shape[1]
    join(xs, [block.at[:rows] for block in (x, core, from_x, both)])
    for d in range(PLANE):
        ws[pl.ds(block_at(pos, 0, d, deep), deep), :] = own[d * deep : (d + 1) * deep, :]
    for i, half in enumerate(halves):
        side = pos[0] if i < planes - 1 else 1 - pos[0]
        for j in range(2):
            at = block_at(pos, 1 + i % (planes - 1), 2 * side + j, deep)
            ws[pl.ds(at, deep), :] = half[j * deep : (j + 1) * deep, :]
    ps[...] = dot(xs[...], ws[...]).astype(ps.dtype)
    for s in range(planes):
        at = pl.multiple_of(jnp.bitwise_xor(pos[1], s) * share, share)
        outs[s][...] = ps[:, pl.ds(at, share)]


def forward_stage(signal, first, work, blocks, rows):
    share = signal.shape[1]
    for pair in range(rows // (2 * ROWS)):
        halves = []
        for h in range(2):
            at = (2 * pair + h) * ROWS
            halves.append(
                jnp.concatenate(
                    [signal[b * rows + at : b * rows + at + ROWS, :] for b in range(blocks)], 0
                )
            )
        got = dot(first[...], jnp.concatenate(halves, 1)).astype(jnp.bfloat16)
        for h in range(2):
            at = (2 * pair + h) * ROWS
            for f in range(2 * blocks):
                work[f, at : at + ROWS, :] = got[
                    f * ROWS : (f + 1) * ROWS, h * share : (h + 1) * share
                ]


def spectrum_at(f, work, turned, blocks, rows):
    if f == 0 or f == blocks:
        return dot(turned[f, :, :rows], work[0 if f == 0 else 1])
    both = jnp.concatenate([work[2 * f], work[2 * f + 1]], 0)
    return dot(turned[f], both)


def taps_kernel(blocks, planes, pos, *refs):
    parts = refs[:PLANE]
    first, turned, out, signal, work = refs[PLANE:]
    rows = signal.shape[0] // blocks
    for d in range(PLANE):
        for s in range(planes):
            signal[pl.ds(block_at(pos, s, d, rows), rows), :] = parts[d][s]
    forward_stage(signal, first, work, blocks, rows)
    for f in range(blocks + 1):
        out[f] = spectrum_at(f, work, turned, blocks, rows).astype(out.dtype)


def conv_kernel(blocks, planes, pos, *refs):
    parts = refs[:planes]
    taps, skip, response, first, last, turned, back = refs[planes : planes + 7]
    outs = refs[planes + 7 : 3 * planes + 7]
    wide, value, work, result = refs[3 * planes + 7 :]
    rows = value.shape[0] // blocks
    share = value.shape[1]
    lead = wide.shape[0] - value.shape[0]
    own = pos[1] * PLANE + pos[2]
    columns = pl.ds(pl.multiple_of(own * share, share), share)
    taps, skip = taps[:, columns], skip[:, columns]
    wide[:lead, :] = jnp.zeros((lead, share), jnp.float32)
    for s in range(planes):
        for d in range(PLANE):
            at = block_at(pos, s, d, rows)
            wide[pl.ds(pl.multiple_of(lead + at, 8), rows), :] = parts[s][
                d * rows : (d + 1) * rows, :
            ].astype(jnp.float32)
    for b in range(blocks):
        at = lead + b * rows
        value[b * rows : (b + 1) * rows, :] = (
            taps[0:1, :] * wide[at : at + rows, :]
            + taps[1:2, :] * wide[at - 1 : at - 1 + rows, :]
            + taps[2:3, :] * wide[at - 2 : at - 2 + rows, :]
        ).astype(value.dtype)
    forward_stage(value, first, work, blocks, rows)
    for f in range(blocks + 1):
        got = spectrum_at(f, work, turned, blocks, rows)
        re, im = got[:rows], got[rows:]
        response_re = response[f, :rows, :].astype(jnp.float32)
        response_im = response[f, rows:, :].astype(jnp.float32)
        product = jnp.concatenate(
            [re * response_re - im * response_im, re * response_im + im * response_re], 0
        ).astype(jnp.bfloat16)
        if f == 0 or f == blocks:
            work[0 if f == 0 else 1] = dot(back[f, :rows, :], product).astype(work.dtype)
        else:
            inverse = dot(back[f], product).astype(work.dtype)
            work[2 * f] = inverse[:rows]
            work[2 * f + 1] = inverse[rows:]
    for pair in range(rows // (2 * ROWS)):
        halves = []
        for h in range(2):
            at = (2 * pair + h) * ROWS
            halves.append(
                jnp.concatenate([work[f, at : at + ROWS, :] for f in range(2 * blocks)], 0)
            )
        got = dot(last[...], jnp.concatenate(halves, 1))
        for h in range(2):
            at = (2 * pair + h) * ROWS
            for b in range(blocks):
                here = slice(b * rows + at, b * rows + at + ROWS)
                conv = got[b * ROWS : (b + 1) * ROWS, h * share : (h + 1) * share]
                result[here, :] = (
                    conv + skip * value[here, :].astype(jnp.float32)
                ).astype(result.dtype)
    for s in range(planes):
        for d in range(PLANE):
            half, at = d // 2, d % 2 * rows
            outs[half * planes + s][at : at + rows, :] = result[
                pl.ds(block_at(pos, s, d, rows), rows), :
            ]


def mixed_dots(planes, pos, u, gate, ws, mixed, outs):
    share = u[0].shape[1]
    rows = gate[0].shape[0]
    for s in range(planes):
        at = pl.multiple_of(jnp.bitwise_xor(pos[1], s) * share, share)
        for d in range(2):
            mixed[d * rows : (d + 1) * rows, s * share : (s + 1) * share] = (
                gate[d][:, pl.ds(at, share)].astype(jnp.float32)
                * u[s][d * rows : (d + 1) * rows, :].astype(jnp.float32)
            ).astype(mixed.dtype)
    got = dot(mixed[...], ws[...])
    outs[0][...] = got[:rows].astype(outs[0].dtype)
    width = outs[1].shape[1]
    for i, out in enumerate(outs[1:]):
        out[...] = got[rows:, i * width : (i + 1) * width].astype(out.dtype)


def upper_kernel(planes, pos, *refs):
    u, gate = refs[:planes], refs[planes : planes + 2]
    own, halves = refs[planes + 2], refs[planes + 3 : 3 * planes + 1]
    outs, ws, mixed = refs[3 * planes + 1 : -2], refs[-2], refs[-1]
    share = u[0].shape[1]
    width = halves[0].shape[1]
    ws[:share, :] = own[...]
    for i, half in enumerate(halves):
        side = pos[0] if i < planes - 1 else 1 - pos[0]
        columns = pl.ds(pl.multiple_of(side * width, width), width)
        s = 1 + i % (planes - 1)
        ws[s * share : (s + 1) * share, columns] = half[:share, :]
    mixed_dots(planes, pos, u, gate, ws, mixed, outs)


def lower_kernel(planes, pos, *refs):
    u, gate, ws = refs[:planes], refs[planes : planes + 2], refs[planes + 2]
    mixed_dots(planes, pos, u, gate, ws, refs[-1], refs[planes + 3 : -1])


def local(inputs, gate_in, value_weight, short_taps, filter_taps, skip_scale, output_weight):
    rows, features = inputs.shape
    deep, channels = value_weight.shape
    devices = lax.axis_size("seq")
    planes = devices // PLANE
    share = channels // devices
    wide = planes * share
    blocks = devices
    index = lax.axis_index("seq")
    y = lax.axis_index("groups")
    z, place = index // PLANE, index % PLANE
    pos = jnp.stack([y, z, place]).astype(jnp.int32)

    def to_place(block, d):
        return lax.ppermute(block, "seq", [(i, i ^ d) for i in range(devices)])

    def to_plane(block, s):
        return lax.ppermute(block, "seq", [(i, i ^ (s * PLANE)) for i in range(devices)])

    def to_group(block):
        return lax.ppermute(block, "groups", [(0, 1), (1, 0)])

    def shaped(*shape, dtype=jnp.bfloat16):
        return jax.ShapeDtypeStruct(shape, dtype)

    def small(kernel, outs, *args, copies=0, fetched=0, vmem=2):
        scratch = [pltpu.SemaphoreType.DMA((copies,))] if copies else []
        return list(call(kernel, outs, scratch, pos, args, 0, vmem=vmem, fetched=fetched))

    stage = lax.optimization_barrier
    first, last, turned, back = (
        jnp.asarray(t) for t in (*stage_tables(blocks), *turned_tables(blocks, rows))
    )
    part, width, positions = rows // 2, features // 2, blocks * rows

    *cut, taps_own, taps_whole, out_near, out_half = call(
        functools.partial(start_kernel, share),
        [shaped(deep, wide)] * PLANE
        + [shaped(rows, wide), shaped(rows, wide)]
        + [shaped(deep + rows // 4, width), shaped(deep, width)],
        [
            pltpu.VMEM((deep, channels), jnp.bfloat16),
            pltpu.VMEM((rows, channels), jnp.bfloat16),
            pltpu.SemaphoreType.DMA((9,)),
        ],
        pos,
        [value_weight, filter_taps, output_weight],
        0,
        vmem=60,
        fetched=3,
    )
    cut = list(cut)
    out_near = to_plane(out_near, 1)
    gate_own, core, message = small(
        functools.partial(across_kernel, share),
        [shaped(rows, wide), shaped(rows * 5 // 4, features), shaped(rows * 3 // 2, features)],
        inputs,
        gate_in,
        copies=13 * planes + 2,
        fetched=2,
    )
    cut = [cut[0]] + [to_place(cut[d], d) for d in range(1, PLANE)]
    route = [
        (y0 * devices + i, y0 * devices + (i ^ (2 + y0) * PLANE))
        for y0 in range(2)
        for i in range(devices)
    ]
    taps_whole = lax.ppermute(taps_whole, ("groups", "seq"), route)
    cut, taps_whole, message, core, out_near = stage((cut, taps_whole, message, core, out_near))

    sent, taps_mine = small(
        half_kernel, [shaped(2 * deep, wide), shaped(rows + part, wide)], *cut, taps_whole, out_near
    )
    near, far = to_plane(sent, 1), to_plane(sent, 2)
    from_x = to_place(message, 2)
    core = to_place(core, 1)
    taps_other = to_group(taps_mine)
    near, far, from_x, taps_other, core, out_half = stage(
        (near, far, from_x, taps_other, core, out_half)
    )

    passed = to_plane(far, 1)
    near_other, far_other = to_group(near), to_group(far)
    out_far = to_plane(out_half, 2)
    both = to_place(from_x, 1)
    taps_parts = small(
        places_kernel, [shaped(planes, rows, share)] * PLANE, taps_own, taps_mine, taps_other
    )
    passed, near_other, far_other, out_far, both, taps_parts = stage(
        (passed, near_other, far_other, out_far, both, taps_parts)
    )

    passed_other = to_group(passed)
    out_passed = to_plane(out_far, 1)
    taps_parts = [taps_parts[0]] + [to_place(taps_parts[d], d) for d in range(1, PLANE)]
    held = small(join_kernel, [shaped(PLANE * deep, wide)], *cut)[0]
    passed, passed_other, out_passed, taps_parts, held = stage(
        (passed, passed_other, out_passed, taps_parts, held)
    )
    projected = call(
        functools.partial(project_kernel, planes),
        [shaped(PLANE * rows, share)] * planes,
        [
            pltpu.VMEM((PLANE * rows, features), jnp.bfloat16),
            pltpu.VMEM((features, wide), jnp.bfloat16),
            pltpu.VMEM((PLANE * rows, wide), jnp.bfloat16),
        ],
        pos,
        [inputs, core, from_x, both, held, near, far, passed]
        + [near_other, far_other, passed_other],
        2 * PLANE * rows * features * wide,
        vmem=8,
    )
    projected, out_far, out_near = stage((projected, out_far, out_near))

    def spread(parts):
        return [parts[0]] + [to_plane(parts[s], s) for s in range(1, planes)]

    signal = spread(projected)
    out_other = [to_group(out_near), to_group(out_far)]
    response = call(
        functools.partial(taps_kernel, blocks, planes),
        [shaped(blocks + 1, 2 * rows, share)],
        [
            pltpu.VMEM((positions, share), jnp.bfloat16),
            pltpu.VMEM((2 * blocks, rows, share), jnp.bfloat16),
        ],
        pos,
        [*taps_parts, first, turned],
        2 * positions * share * (32 * ROWS + 4 * rows),
        vmem=4,
    )[0]
    gate = [gate_own] + small(unfold_kernel, [shaped(rows, wide)] * 3, core, from_x, both)
    signal, out_other, response = stage((signal, out_other, response))

    mixed = call(
        functools.partial(conv_kernel, blocks, planes),
        [shaped(2 * rows, share)] * (2 * planes),
        [
            pltpu.VMEM((positions + 8, share), jnp.float32),
            pltpu.VMEM((positions, share), jnp.bfloat16),
            pltpu.VMEM((2 * blocks, rows, share), jnp.bfloat16),
            pltpu.VMEM((positions, share), jnp.bfloat16),
        ],
        pos,
        [*signal, short_taps, skip_scale[None], response, first, last, turned, back],
        4 * positions * share * (32 * ROWS + 4 * rows),
        vmem=8,
    )
    mixed, out_passed = stage((mixed, out_passed))

    upper = spread(mixed[planes:])
    out_other += [to_group(out_passed)]
    upper, out_other, lower = stage((upper, out_other, mixed[:planes]))
    scratch = [pltpu.VMEM((2 * rows, wide), jnp.bfloat16)]
    flops = 4 * rows * features * wide
    partial_two, partial_three, gathered = call(
        functools.partial(upper_kernel, planes),
        [shaped(rows, features, dtype=jnp.float32), shaped(rows, features)]
        + [shaped(wide, features)],
        scratch,
        pos,
        [*upper, *gate[2:], output_weight]
        + [out_near, out_far, out_passed, *out_other],
        flops,
        vmem=8,
    )
    across = partial_two + to_place(partial_three, 1).astype(jnp.float32)
    across, lower = stage((across.astype(jnp.bfloat16), lower))

    across = to_place(across, 2)
    lower = spread(lower)
    partial_zero, *partial_one = call(
        functools.partial(lower_kernel, planes),
        [shaped(rows, features, dtype=jnp.float32)] + [shaped(rows, features // 4)] * 4,
        scratch,
        pos,
        [*lower, *gate[:2], gathered],
        0,
        vmem=8,
    )
    partial_one = jnp.concatenate([to_place(block, 1) for block in partial_one], 1)
    result = partial_zero + partial_one.astype(jnp.float32) + across.astype(jnp.float32)
    return result.astype(jnp.bfloat16)


def passed_along(block, axis, distance):
    devices = range(lax.axis_size(axis))
    route = [(i - distance, i) for i in devices if i - distance in devices]
    return lax.ppermute(block, axis, route)


def local_narrow(inputs, gate_in, value_weight, short_taps, filter_taps, skip_scale, output_weight):
    rows, features = inputs.shape
    channels = value_weight.shape[1]
    blocks = lax.axis_size("seq")
    share = channels // blocks
    index = lax.axis_index("seq")
    projected = dot(inputs, lax.all_gather(value_weight, "seq", axis=0, tiled=True)).astype(
        jnp.bfloat16
    )
    earlier = passed_along(projected[rows - 2 :], "seq", 1)
    extended = jnp.concatenate([earlier, projected], 0).astype(jnp.float32)
    value = (
        short_taps[0] * extended[2:]
        + short_taps[1] * extended[1:-1]
        + short_taps[2] * extended[:-2]
    ).astype(jnp.bfloat16)

    def by_channel(signal):
        cut = signal.reshape(rows, blocks, share)
        got = lax.all_to_all(cut, "seq", split_axis=1, concat_axis=0, tiled=True)
        return got.reshape(blocks, rows, share)

    grid = np.arange(2 * blocks)
    angle = 2.0 * np.pi * (grid[:, None] * grid[None, :] % (2 * blocks)) / (2 * blocks)
    wide = np.exp(-1j * angle)[: blocks + 1, :blocks]
    turned, back = (jnp.asarray(t) for t in turned_tables(blocks, rows))
    weight = np.full((blocks + 1, 1), 2.0)
    weight[0] = weight[-1] = 1.0
    narrow = weight * np.conj(wide) / (2 * blocks * rows)

    def einsum(form, table, data):
        return jnp.einsum(form, table, data, preferred_element_type=jnp.float32)

    def table(values):
        return jnp.asarray(values.astype(ml_dtypes.bfloat16))

    def forward(signal):
        re = einsum("fb,bmc->fmc", table(np.real(wide)), signal)
        im = einsum("fb,bmc->fmc", table(np.imag(wide)), signal)
        both = jnp.concatenate([re, im], 1).astype(jnp.bfloat16)
        return einsum("fkm,fmc->fkc", turned, both)

    response = forward(by_channel(filter_taps))
    got = forward(by_channel(value))
    re, im = got[:, :rows], got[:, rows:]
    response_re, response_im = response[:, :rows], response[:, rows:]
    product = jnp.concatenate(
        [re * response_re - im * response_im, re * response_im + im * response_re], 1
    ).astype(jnp.bfloat16)
    inverse = einsum("fmk,fkc->fmc", back, product).astype(jnp.bfloat16)
    conv = einsum("fb,fmc->bmc", table(np.real(narrow)), inverse[:, :rows]) - einsum(
        "fb,fmc->bmc", table(np.imag(narrow)), inverse[:, rows:]
    )
    conv = lax.all_to_all(
        conv.astype(jnp.bfloat16), "seq", split_axis=0, concat_axis=2, tiled=True
    ).reshape(rows, channels)
    mixed = (
        gate_in.astype(jnp.float32)
        * (conv.astype(jnp.float32) + skip_scale * value.astype(jnp.float32))
    ).astype(jnp.bfloat16)
    result = dot(mixed, lax.all_gather(output_weight, "seq", axis=0, tiled=True))
    return result.astype(jnp.bfloat16)


def solution(mesh):
    split = P(("groups", "seq"), None)
    placed = (split, split, P("seq", None), P(), P("seq", None), P(), P("seq", None))

    def run(*args):
        devices = mesh.shape["seq"]
        share = args[2].shape[1] // devices
        tiled = share % LANES == 0 and args[0].shape[0] // mesh.size == LANES
        paired = devices == 4 * PLANE and mesh.shape["groups"] == 2
        body = local if tiled and paired else local_narrow
        return jax.shard_map(body, mesh=mesh, in_specs=placed, out_specs=split, check_vma=False)(
            *args
        )

    return run
```

```python
import functools
import math

import jax
import jax.numpy as jnp
import ml_dtypes
import numpy as np
from jax import lax
from jax.experimental import pallas as pl
from jax.experimental.pallas import tpu as pltpu
from jax.sharding import PartitionSpec as P

PLANE = 4
LANES = 128
ROWS = 16
MIB = 1 << 20


def stage_tables(blocks):
    width = 2 * blocks
    b = np.arange(blocks)
    forward = [np.ones(blocks), np.cos(np.pi * b)]
    backward = [np.ones(blocks), np.cos(np.pi * b)]
    for f in range(1, blocks):
        angle = 2.0 * np.pi * (f * b % width) / width
        forward += [np.cos(angle), -np.sin(angle)]
        backward += [2.0 * np.cos(angle), -2.0 * np.sin(angle)]
    eye = np.eye(ROWS)
    first = np.kron(np.stack(forward, 0), eye)
    last = np.kron(np.stack(backward, 1), eye) / (width * LANES)
    return first.astype(ml_dtypes.bfloat16), last.astype(ml_dtypes.bfloat16)


def turned_tables(blocks, rows):
    width = 2 * blocks
    k = np.arange(rows)[:, None]
    m = np.arange(rows)[None, :]
    out = []
    for f in range(blocks + 1):
        angle = 2.0 * np.pi * ((width * k + f) * m % (width * rows)) / (width * rows)
        cos, sin = np.cos(angle), np.sin(angle)
        out.append(np.block([[cos, sin], [-sin, cos]]))
    forward = np.stack(out, 0)
    return (
        forward.astype(ml_dtypes.bfloat16),
        np.swapaxes(forward, 1, 2).astype(ml_dtypes.bfloat16),
    )


def dot(left, right):
    return jnp.dot(left, right, preferred_element_type=jnp.float32)


def call(kernel, outs, scratch, pos, args, flops, vmem=4, fetched=0):
    in_specs = [pl.BlockSpec(memory_space=pltpu.SMEM)]
    in_specs += [pl.BlockSpec(memory_space=pltpu.HBM)] * fetched
    in_specs += [pl.BlockSpec(memory_space=pltpu.VMEM)] * (len(args) - fetched)
    moved = sum(a.size * a.dtype.itemsize for a in args) if flops else 0
    moved += sum(math.prod(o.shape) * o.dtype.itemsize for o in outs) if flops else 0
    return pl.pallas_call(
        kernel,
        out_shape=outs,
        in_specs=in_specs,
        out_specs=[pl.BlockSpec(memory_space=pltpu.VMEM)] * len(outs),
        scratch_shapes=scratch,
        compiler_params=pltpu.CompilerParams(vmem_limit_bytes=vmem * MIB),
        cost_estimate=pl.CostEstimate(flops=flops, bytes_accessed=moved, transcendentals=0),
    )(pos, *args)


def block_at(pos, s, d, rows):
    block = jnp.bitwise_xor(pos[1], s) * PLANE + jnp.bitwise_xor(pos[2], d)
    return pl.multiple_of(block * rows, rows)


def fetch(pairs, sems):
    copies = [pltpu.make_async_copy(src, dst, sems.at[i]) for i, (src, dst) in enumerate(pairs)]
    for copy in copies:
        copy.start()
    return copies


def start_kernel(share, pos, weight, taps, out_weight, *refs):
    outs, (own, whole, near, out_half) = refs[:PLANE], refs[PLANE : PLANE + 4]
    weight_here, taps_here, sems = refs[PLANE + 4 :]
    rows, wide = own.shape
    deep, width = out_half.shape
    quarter = rows // 4
    side = pl.ds(pl.multiple_of(pos[0] * width, width), width)
    pairs = []
    for source, here in ((weight, weight_here), (taps, taps_here)):
        for q in range(4):
            cut = pl.ds(q * quarter, quarter)
            pairs.append((source.at[cut], here.at[cut]))
    pairs.append((out_weight.at[:, side], out_half))
    copies = fetch(pairs, sems)
    for copy in copies[:4]:
        copy.wait()
    for d, out in enumerate(outs):
        place = jnp.bitwise_xor(pos[2], d)
        for p in range(wide // share):
            at = pl.multiple_of((p * PLANE + place) * share, share)
            out[:, p * share : (p + 1) * share] = weight_here[:, pl.ds(at, share)]
    for copy in copies[4:]:
        copy.wait()

    def columns(s):
        return pl.ds(pl.multiple_of(jnp.bitwise_xor(pos[1], s) * wide, wide), wide)

    own[...] = taps_here[:, columns(0)]
    whole[...] = taps_here[:, columns(2 + pos[0])]
    near[:deep, :] = out_half[...]
    for q in range(2):
        first = pl.multiple_of(pos[0] * (rows // 2) + q * quarter, quarter)
        near[deep:, q * wide : (q + 1) * wide] = taps_here[pl.ds(first, quarter), columns(1)]


def across_kernel(share, pos, x, gate, own, core, across, sems):
    rows = x.shape[0]
    part, wide = rows // 4, own.shape[1]
    pairs = [(x, core.at[pl.ds(0, rows)]), (x, across.at[pl.ds(0, rows)])]
    for d in range(PLANE):
        place = jnp.bitwise_xor(pos[2], d)
        for p in range(wide // share):
            at = pl.multiple_of((p * PLANE + place) * share, share)
            if d == 0:
                here = pl.ds(p * share, share)
                pairs.append((gate.at[:, pl.ds(at, share)], own.at[:, here]))
                continue
            out, first = (core, rows) if d == 1 else (across, rows + (d - 2) * part)
            for q in range(4):
                columns = pl.ds(q * wide + p * share, share)
                source = gate.at[pl.ds(q * part, part), pl.ds(at, share)]
                pairs.append((source, out.at[pl.ds(first, part), columns]))
    for copy in fetch(pairs, sems):
        copy.wait()


def unfold_kernel(pos, core, from_x, both, *outs):
    rows, wide = outs[0].shape
    part = rows // 4
    for source, first, out in zip((core, from_x, both), (0, 0, part), outs):
        for q in range(4):
            out[q * part : (q + 1) * part, :] = source[
                rows + first : rows + first + part, q * wide : (q + 1) * wide
            ]


def join(out, parts):
    at = 0
    for part in parts:
        out[at : at + part.shape[0], :] = part[...]
        at += part.shape[0]


def half_kernel(pos, *refs):
    parts, (whole, near), (out, joined, beside) = refs[:PLANE], refs[PLANE:-3], refs[-3:]
    for y in range(2):

        @pl.when(pos[0] == y)
        def _():
            join(out, parts[2 * y : 2 * y + 2])

    rows, wide = whole.shape
    quarter = rows // 4
    joined[:rows, :] = whole[...]
    for q in range(2):
        here = slice(rows + q * quarter, rows + (q + 1) * quarter)
        joined[here, :] = near[near.shape[0] - quarter :, q * wide : (q + 1) * wide]
    beside[...] = near[: beside.shape[0], :]


def join_kernel(pos, *refs):
    join(refs[-1], refs[:-1])


def places_kernel(pos, own, mine, other, *outs):
    planes, rows, share = outs[0].shape
    part = rows // 2
    for d, out in enumerate(outs):
        columns = pl.ds(pl.multiple_of(jnp.bitwise_xor(pos[2], d) * share, share), share)
        out[0] = own[:, columns]
        for side, block in ((pos[0], mine), (1 - pos[0], other)):
            out[2 + side] = block[:rows, columns]
            out[1, pl.ds(pl.multiple_of(side * part, part), part), :] = block[rows:, columns]


def project_kernel(planes, pos, x, core, from_x, both, own, *refs):
    halves, outs = refs[: 2 * planes - 2], refs[2 * planes - 2 : -3]
    xs, ws, ps = refs[-3:]
    rows = x.shape[0]
    deep = own.shape[0] // PLANE
    share = outs[0].shape[1]
    join(xs, [block.at[:rows] for block in (x, core, from_x, both)])
    for d in range(PLANE):
        ws[pl.ds(block_at(pos, 0, d, deep), deep), :] = own[d * deep : (d + 1) * deep, :]
    for i, half in enumerate(halves):
        side = pos[0] if i < planes - 1 else 1 - pos[0]
        for j in range(2):
            at = block_at(pos, 1 + i % (planes - 1), 2 * side + j, deep)
            ws[pl.ds(at, deep), :] = half[j * deep : (j + 1) * deep, :]
    ps[...] = dot(xs[...], ws[...]).astype(ps.dtype)
    for s in range(planes):
        at = pl.multiple_of(jnp.bitwise_xor(pos[1], s) * share, share)
        outs[s][...] = ps[:, pl.ds(at, share)]


def forward_stage(signal, first, work, blocks, rows):
    share = signal.shape[1]
    for pair in range(rows // (2 * ROWS)):
        halves = []
        for h in range(2):
            at = (2 * pair + h) * ROWS
            halves.append(
                jnp.concatenate(
                    [signal[b * rows + at : b * rows + at + ROWS, :] for b in range(blocks)], 0
                )
            )
        got = dot(first[...], jnp.concatenate(halves, 1)).astype(jnp.bfloat16)
        for h in range(2):
            at = (2 * pair + h) * ROWS
            for f in range(2 * blocks):
                work[f, at : at + ROWS, :] = got[
                    f * ROWS : (f + 1) * ROWS, h * share : (h + 1) * share
                ]


def spectrum_at(f, work, turned, blocks, rows):
    if f == 0 or f == blocks:
        return dot(turned[f, :, :rows], work[0 if f == 0 else 1])
    both = jnp.concatenate([work[2 * f], work[2 * f + 1]], 0)
    return dot(turned[f], both)


def taps_kernel(blocks, planes, pos, *refs):
    parts = refs[:PLANE]
    first, turned, out, signal, work = refs[PLANE:]
    rows = signal.shape[0] // blocks
    for d in range(PLANE):
        for s in range(planes):
            signal[pl.ds(block_at(pos, s, d, rows), rows), :] = parts[d][s]
    forward_stage(signal, first, work, blocks, rows)
    for f in range(blocks + 1):
        out[f] = spectrum_at(f, work, turned, blocks, rows).astype(out.dtype)


def conv_kernel(blocks, planes, pos, *refs):
    parts = refs[:planes]
    taps, skip, response, first, last, turned, back = refs[planes : planes + 7]
    outs = refs[planes + 7 : 3 * planes + 7]
    wide, value, work, result = refs[3 * planes + 7 :]
    rows = value.shape[0] // blocks
    share = value.shape[1]
    lead = wide.shape[0] - value.shape[0]
    own = pos[1] * PLANE + pos[2]
    columns = pl.ds(pl.multiple_of(own * share, share), share)
    taps, skip = taps[:, columns], skip[:, columns]
    wide[:lead, :] = jnp.zeros((lead, share), jnp.float32)
    for s in range(planes):
        for d in range(PLANE):
            at = block_at(pos, s, d, rows)
            wide[pl.ds(pl.multiple_of(lead + at, 8), rows), :] = parts[s][
                d * rows : (d + 1) * rows, :
            ].astype(jnp.float32)
    for b in range(blocks):
        at = lead + b * rows
        value[b * rows : (b + 1) * rows, :] = (
            taps[0:1, :] * wide[at : at + rows, :]
            + taps[1:2, :] * wide[at - 1 : at - 1 + rows, :]
            + taps[2:3, :] * wide[at - 2 : at - 2 + rows, :]
        ).astype(value.dtype)
    forward_stage(value, first, work, blocks, rows)
    for f in range(blocks + 1):
        got = spectrum_at(f, work, turned, blocks, rows)
        re, im = got[:rows], got[rows:]
        response_re = response[f, :rows, :].astype(jnp.float32)
        response_im = response[f, rows:, :].astype(jnp.float32)
        product = jnp.concatenate(
            [re * response_re - im * response_im, re * response_im + im * response_re], 0
        ).astype(jnp.bfloat16)
        if f == 0 or f == blocks:
            work[0 if f == 0 else 1] = dot(back[f, :rows, :], product).astype(work.dtype)
        else:
            inverse = dot(back[f], product).astype(work.dtype)
            work[2 * f] = inverse[:rows]
            work[2 * f + 1] = inverse[rows:]
    for pair in range(rows // (2 * ROWS)):
        halves = []
        for h in range(2):
            at = (2 * pair + h) * ROWS
            halves.append(
                jnp.concatenate([work[f, at : at + ROWS, :] for f in range(2 * blocks)], 0)
            )
        got = dot(last[...], jnp.concatenate(halves, 1))
        for h in range(2):
            at = (2 * pair + h) * ROWS
            for b in range(blocks):
                here = slice(b * rows + at, b * rows + at + ROWS)
                conv = got[b * ROWS : (b + 1) * ROWS, h * share : (h + 1) * share]
                result[here, :] = (
                    conv + skip * value[here, :].astype(jnp.float32)
                ).astype(result.dtype)
    for s in range(planes):
        for d in range(PLANE):
            half, at = d // 2, d % 2 * rows
            outs[half * planes + s][at : at + rows, :] = result[
                pl.ds(block_at(pos, s, d, rows), rows), :
            ]


def mixed_dots(planes, pos, u, gate, ws, mixed, outs):
    share = u[0].shape[1]
    rows = gate[0].shape[0]
    for s in range(planes):
        at = pl.multiple_of(jnp.bitwise_xor(pos[1], s) * share, share)
        for d in range(2):
            mixed[d * rows : (d + 1) * rows, s * share : (s + 1) * share] = (
                gate[d][:, pl.ds(at, share)].astype(jnp.float32)
                * u[s][d * rows : (d + 1) * rows, :].astype(jnp.float32)
            ).astype(mixed.dtype)
    got = dot(mixed[...], ws[...])
    outs[0][...] = got[:rows].astype(outs[0].dtype)
    width = outs[1].shape[1]
    for i, out in enumerate(outs[1:]):
        out[...] = got[rows:, i * width : (i + 1) * width].astype(out.dtype)


def upper_kernel(planes, pos, *refs):
    u, gate = refs[:planes], refs[planes : planes + 2]
    own, halves = refs[planes + 2], refs[planes + 3 : 3 * planes + 1]
    outs, ws, mixed = refs[3 * planes + 1 : -2], refs[-2], refs[-1]
    share = u[0].shape[1]
    width = halves[0].shape[1]
    ws[:share, :] = own[...]
    for i, half in enumerate(halves):
        side = pos[0] if i < planes - 1 else 1 - pos[0]
        columns = pl.ds(pl.multiple_of(side * width, width), width)
        s = 1 + i % (planes - 1)
        ws[s * share : (s + 1) * share, columns] = half[:share, :]
    mixed_dots(planes, pos, u, gate, ws, mixed, outs)


def lower_kernel(planes, pos, *refs):
    u, gate, ws = refs[:planes], refs[planes : planes + 2], refs[planes + 2]
    mixed_dots(planes, pos, u, gate, ws, refs[-1], refs[planes + 3 : -1])


def local(inputs, gate_in, value_weight, short_taps, filter_taps, skip_scale, output_weight):
    rows, features = inputs.shape
    deep, channels = value_weight.shape
    devices = lax.axis_size("seq")
    planes = devices // PLANE
    share = channels // devices
    wide = planes * share
    blocks = devices
    index = lax.axis_index("seq")
    y = lax.axis_index("groups")
    z, place = index // PLANE, index % PLANE
    pos = jnp.stack([y, z, place]).astype(jnp.int32)

    def to_place(block, d):
        return lax.ppermute(block, "seq", [(i, i ^ d) for i in range(devices)])

    def to_plane(block, s):
        return lax.ppermute(block, "seq", [(i, i ^ (s * PLANE)) for i in range(devices)])

    def to_group(block):
        return lax.ppermute(block, "groups", [(0, 1), (1, 0)])

    def shaped(*shape, dtype=jnp.bfloat16):
        return jax.ShapeDtypeStruct(shape, dtype)

    def small(kernel, outs, *args, copies=0, fetched=0, vmem=2):
        scratch = [pltpu.SemaphoreType.DMA((copies,))] if copies else []
        return list(call(kernel, outs, scratch, pos, args, 0, vmem=vmem, fetched=fetched))

    stage = lax.optimization_barrier
    first, last, turned, back = (
        jnp.asarray(t) for t in (*stage_tables(blocks), *turned_tables(blocks, rows))
    )
    part, width, positions = rows // 2, features // 2, blocks * rows

    *cut, taps_own, taps_whole, out_near, out_half = call(
        functools.partial(start_kernel, share),
        [shaped(deep, wide)] * PLANE
        + [shaped(rows, wide), shaped(rows, wide)]
        + [shaped(deep + rows // 4, width), shaped(deep, width)],
        [
            pltpu.VMEM((deep, channels), jnp.bfloat16),
            pltpu.VMEM((rows, channels), jnp.bfloat16),
            pltpu.SemaphoreType.DMA((9,)),
        ],
        pos,
        [value_weight, filter_taps, output_weight],
        0,
        vmem=53,
        fetched=3,
    )
    cut = list(cut)
    out_near = to_plane(out_near, 1)
    gate_own, core, message = small(
        functools.partial(across_kernel, share),
        [shaped(rows, wide), shaped(rows * 5 // 4, features), shaped(rows * 3 // 2, features)],
        inputs,
        gate_in,
        copies=13 * planes + 2,
        fetched=2,
    )
    own = small(join_kernel, [shaped(deep, wide)], cut[0])
    cut = own + [to_place(cut[d], d) for d in range(1, PLANE)]
    route = [
        (y0 * devices + i, y0 * devices + (i ^ (2 + y0) * PLANE))
        for y0 in range(2)
        for i in range(devices)
    ]
    taps_whole = lax.ppermute(taps_whole, ("groups", "seq"), route)
    cut, taps_whole, message, core, out_near = stage((cut, taps_whole, message, core, out_near))

    sent, taps_mine, out_near = small(
        half_kernel,
        [shaped(2 * deep, wide), shaped(rows * 3 // 2, wide), shaped(deep, width)],
        *cut,
        taps_whole,
        out_near,
    )
    near, far = to_plane(sent, 1), to_plane(sent, 2)
    from_x = to_place(message, 2)
    core = to_place(core, 1)
    taps_other, out_other = to_group(taps_mine), to_group(out_near)
    near, far, from_x, taps_other, core, out_half, out_other = stage(
        (near, far, from_x, taps_other, core, out_half, out_other)
    )

    passed = to_plane(far, 1)
    near_other, far_other = to_group(near), to_group(far)
    out_far = to_plane(out_half, 2)
    both = to_place(from_x, 1)
    taps_parts = small(
        places_kernel, [shaped(planes, rows, share)] * PLANE, taps_own, taps_mine, taps_other
    )
    taps_parts, passed, both = stage((taps_parts, passed, both))
    passed_other = to_group(passed)
    taps_parts = [taps_parts[0]] + [to_place(taps_parts[d], d) for d in range(1, PLANE)]
    held = small(join_kernel, [shaped(PLANE * deep, wide)], *cut)[0]
    out_passed = to_plane(out_far, 1)
    passed, near_other, far_other, out_passed, both, taps_parts, passed_other, held = stage(
        (passed, near_other, far_other, out_passed, both, taps_parts, passed_other, held)
    )
    projected = call(
        functools.partial(project_kernel, planes),
        [shaped(PLANE * rows, share)] * planes,
        [
            pltpu.VMEM((PLANE * rows, features), jnp.bfloat16),
            pltpu.VMEM((features, wide), jnp.bfloat16),
            pltpu.VMEM((PLANE * rows, wide), jnp.bfloat16),
        ],
        pos,
        [inputs, core, from_x, both, held, near, far, passed]
        + [near_other, far_other, passed_other],
        2 * PLANE * rows * features * wide,
        vmem=8,
    )
    projected, out_far = stage((projected, out_far))

    def spread(parts):
        return [parts[0]] + [to_plane(parts[s], s) for s in range(1, planes)]

    signal = spread(projected)
    out_other = [out_other, to_group(out_far)]
    response = call(
        functools.partial(taps_kernel, blocks, planes),
        [shaped(blocks + 1, 2 * rows, share)],
        [
            pltpu.VMEM((positions, share), jnp.bfloat16),
            pltpu.VMEM((2 * blocks, rows, share), jnp.bfloat16),
        ],
        pos,
        [*taps_parts, first, turned],
        2 * positions * share * (32 * ROWS + 4 * rows),
        vmem=4,
    )[0]
    gate = [gate_own] + small(unfold_kernel, [shaped(rows, wide)] * 3, core, from_x, both)
    signal, response = stage((signal, response))

    mixed = call(
        functools.partial(conv_kernel, blocks, planes),
        [shaped(2 * rows, share)] * (2 * planes),
        [
            pltpu.VMEM((positions + 8, share), jnp.float32),
            pltpu.VMEM((positions, share), jnp.bfloat16),
            pltpu.VMEM((2 * blocks, rows, share), jnp.bfloat16),
            pltpu.VMEM((positions, share), jnp.bfloat16),
        ],
        pos,
        [*signal, short_taps, skip_scale[None], response, first, last, turned, back],
        4 * positions * share * (32 * ROWS + 4 * rows),
        vmem=8,
    )
    mixed, out_passed, out_other = stage((mixed, out_passed, out_other))

    upper = spread(mixed[planes:])
    out_other += [to_group(out_passed)]
    upper, out_other, lower = stage((upper, out_other, mixed[:planes]))
    scratch = [pltpu.VMEM((2 * rows, wide), jnp.bfloat16)]
    flops = 4 * rows * features * wide
    partial_two, partial_three, gathered = call(
        functools.partial(upper_kernel, planes),
        [shaped(rows, features, dtype=jnp.float32), shaped(rows, features)]
        + [shaped(wide, features)],
        scratch,
        pos,
        [*upper, *gate[2:], output_weight]
        + [out_near, out_far, out_passed, *out_other],
        flops,
        vmem=8,
    )
    across = partial_two + to_place(partial_three, 1).astype(jnp.float32)
    across, lower = stage((across.astype(jnp.bfloat16), lower))

    across = to_place(across, 2)
    lower = spread(lower)
    partial_zero, *partial_one = call(
        functools.partial(lower_kernel, planes),
        [shaped(rows, features, dtype=jnp.float32)] + [shaped(rows, features // 4)] * 4,
        scratch,
        pos,
        [*lower, *gate[:2], gathered],
        0,
        vmem=8,
    )
    partial_one = jnp.concatenate([to_place(block, 1) for block in partial_one], 1)
    result = partial_zero + partial_one.astype(jnp.float32) + across.astype(jnp.float32)
    return result.astype(jnp.bfloat16)


def passed_along(block, axis, distance):
    devices = range(lax.axis_size(axis))
    route = [(i - distance, i) for i in devices if i - distance in devices]
    return lax.ppermute(block, axis, route)


def local_narrow(inputs, gate_in, value_weight, short_taps, filter_taps, skip_scale, output_weight):
    rows, features = inputs.shape
    channels = value_weight.shape[1]
    blocks = lax.axis_size("seq")
    share = channels // blocks
    index = lax.axis_index("seq")
    projected = dot(inputs, lax.all_gather(value_weight, "seq", axis=0, tiled=True)).astype(
        jnp.bfloat16
    )
    earlier = passed_along(projected[rows - 2 :], "seq", 1)
    extended = jnp.concatenate([earlier, projected], 0).astype(jnp.float32)
    value = (
        short_taps[0] * extended[2:]
        + short_taps[1] * extended[1:-1]
        + short_taps[2] * extended[:-2]
    ).astype(jnp.bfloat16)

    def by_channel(signal):
        cut = signal.reshape(rows, blocks, share)
        got = lax.all_to_all(cut, "seq", split_axis=1, concat_axis=0, tiled=True)
        return got.reshape(blocks, rows, share)

    grid = np.arange(2 * blocks)
    angle = 2.0 * np.pi * (grid[:, None] * grid[None, :] % (2 * blocks)) / (2 * blocks)
    wide = np.exp(-1j * angle)[: blocks + 1, :blocks]
    turned, back = (jnp.asarray(t) for t in turned_tables(blocks, rows))
    weight = np.full((blocks + 1, 1), 2.0)
    weight[0] = weight[-1] = 1.0
    narrow = weight * np.conj(wide) / (2 * blocks * rows)

    def einsum(form, table, data):
        return jnp.einsum(form, table, data, preferred_element_type=jnp.float32)

    def table(values):
        return jnp.asarray(values.astype(ml_dtypes.bfloat16))

    def forward(signal):
        re = einsum("fb,bmc->fmc", table(np.real(wide)), signal)
        im = einsum("fb,bmc->fmc", table(np.imag(wide)), signal)
        both = jnp.concatenate([re, im], 1).astype(jnp.bfloat16)
        return einsum("fkm,fmc->fkc", turned, both)

    response = forward(by_channel(filter_taps))
    got = forward(by_channel(value))
    re, im = got[:, :rows], got[:, rows:]
    response_re, response_im = response[:, :rows], response[:, rows:]
    product = jnp.concatenate(
        [re * response_re - im * response_im, re * response_im + im * response_re], 1
    ).astype(jnp.bfloat16)
    inverse = einsum("fmk,fkc->fmc", back, product).astype(jnp.bfloat16)
    conv = einsum("fb,fmc->bmc", table(np.real(narrow)), inverse[:, :rows]) - einsum(
        "fb,fmc->bmc", table(np.imag(narrow)), inverse[:, rows:]
    )
    conv = lax.all_to_all(
        conv.astype(jnp.bfloat16), "seq", split_axis=0, concat_axis=2, tiled=True
    ).reshape(rows, channels)
    mixed = (
        gate_in.astype(jnp.float32)
        * (conv.astype(jnp.float32) + skip_scale * value.astype(jnp.float32))
    ).astype(jnp.bfloat16)
    result = dot(mixed, lax.all_gather(output_weight, "seq", axis=0, tiled=True))
    return result.astype(jnp.bfloat16)


def solution(mesh):
    split = P(("groups", "seq"), None)
    placed = (split, split, P("seq", None), P(), P("seq", None), P(), P("seq", None))

    def run(*args):
        devices = mesh.shape["seq"]
        share = args[2].shape[1] // devices
        tiled = share % LANES == 0 and args[0].shape[0] // mesh.size == LANES
        paired = devices == 4 * PLANE and mesh.shape["groups"] == 2
        body = local if tiled and paired else local_narrow
        return jax.shard_map(body, mesh=mesh, in_specs=placed, out_specs=split, check_vma=False)(
            *args
        )

    return run
```

```python
import functools
import math

import jax
import jax.numpy as jnp
import ml_dtypes
import numpy as np
from jax import lax
from jax.experimental import pallas as pl
from jax.experimental.pallas import tpu as pltpu
from jax.sharding import PartitionSpec as P

PLANE = 4
LANES = 128
ROWS = 16
MIB = 1 << 20


def stage_tables(blocks):
    width = 2 * blocks
    b = np.arange(blocks)
    forward = [np.ones(blocks), np.cos(np.pi * b)]
    backward = [np.ones(blocks), np.cos(np.pi * b)]
    for f in range(1, blocks):
        angle = 2.0 * np.pi * (f * b % width) / width
        forward += [np.cos(angle), -np.sin(angle)]
        backward += [2.0 * np.cos(angle), -2.0 * np.sin(angle)]
    eye = np.eye(ROWS)
    first = np.kron(np.stack(forward, 0), eye)
    last = np.kron(np.stack(backward, 1), eye) / (width * LANES)
    return first.astype(ml_dtypes.bfloat16), last.astype(ml_dtypes.bfloat16)


def turned_tables(blocks, rows):
    width = 2 * blocks
    k = np.arange(rows)[:, None]
    m = np.arange(rows)[None, :]
    out = []
    for f in range(blocks + 1):
        angle = 2.0 * np.pi * ((width * k + f) * m % (width * rows)) / (width * rows)
        cos, sin = np.cos(angle), np.sin(angle)
        out.append(np.block([[cos, sin], [-sin, cos]]))
    forward = np.stack(out, 0)
    return (
        forward.astype(ml_dtypes.bfloat16),
        np.swapaxes(forward, 1, 2).astype(ml_dtypes.bfloat16),
    )


def dot(left, right):
    return jnp.dot(left, right, preferred_element_type=jnp.float32)


def call(kernel, outs, scratch, pos, args, flops, vmem=4, fetched=0):
    in_specs = [pl.BlockSpec(memory_space=pltpu.SMEM)]
    in_specs += [pl.BlockSpec(memory_space=pltpu.HBM)] * fetched
    in_specs += [pl.BlockSpec(memory_space=pltpu.VMEM)] * (len(args) - fetched)
    moved = sum(a.size * a.dtype.itemsize for a in args) if flops else 0
    moved += sum(math.prod(o.shape) * o.dtype.itemsize for o in outs) if flops else 0
    return pl.pallas_call(
        kernel,
        out_shape=outs,
        in_specs=in_specs,
        out_specs=[pl.BlockSpec(memory_space=pltpu.VMEM)] * len(outs),
        scratch_shapes=scratch,
        compiler_params=pltpu.CompilerParams(vmem_limit_bytes=vmem * MIB),
        cost_estimate=pl.CostEstimate(flops=flops, bytes_accessed=moved, transcendentals=0),
    )(pos, *args)


def block_at(pos, s, d, rows):
    block = jnp.bitwise_xor(pos[1], s) * PLANE + jnp.bitwise_xor(pos[2], d)
    return pl.multiple_of(block * rows, rows)


def fetch(pairs, sems):
    copies = [pltpu.make_async_copy(src, dst, sems.at[i]) for i, (src, dst) in enumerate(pairs)]
    for copy in copies:
        copy.start()
    return copies


def start_kernel(share, pos, weight, taps, out_weight, *refs):
    outs, (own, whole, near, out_half) = refs[:PLANE], refs[PLANE : PLANE + 4]
    weight_here, taps_here, sems = refs[PLANE + 4 :]
    rows, wide = own.shape
    deep, width = out_half.shape
    quarter = rows // 4
    side = pl.ds(pl.multiple_of(pos[0] * width, width), width)
    pairs = []
    for source, here in ((weight, weight_here), (taps, taps_here)):
        for q in range(4):
            cut = pl.ds(q * quarter, quarter)
            pairs.append((source.at[cut], here.at[cut]))
    pairs.append((out_weight.at[:, side], out_half))
    copies = fetch(pairs, sems)
    for copy in copies[:4]:
        copy.wait()
    for d, out in enumerate(outs):
        place = jnp.bitwise_xor(pos[2], d)
        for p in range(wide // share):
            at = pl.multiple_of((p * PLANE + place) * share, share)
            out[:, p * share : (p + 1) * share] = weight_here[:, pl.ds(at, share)]
    for copy in copies[4:]:
        copy.wait()

    def columns(s):
        return pl.ds(pl.multiple_of(jnp.bitwise_xor(pos[1], s) * wide, wide), wide)

    own[...] = taps_here[:, columns(0)]
    whole[...] = taps_here[:, columns(2 + pos[0])]
    near[:deep, :] = out_half[...]
    for q in range(2):
        first = pl.multiple_of(pos[0] * (rows // 2) + q * quarter, quarter)
        near[deep:, q * wide : (q + 1) * wide] = taps_here[pl.ds(first, quarter), columns(1)]


def gate_kernel(share, pos, gate, own, beside, across, sems):
    rows, wide = own.shape
    pairs = []
    for d, (out, first) in enumerate(((own, 0), (beside, 0), (across, 0), (across, rows))):
        place = jnp.bitwise_xor(pos[2], d)
        for p in range(wide // share):
            at = pl.multiple_of((p * PLANE + place) * share, share)
            here = out.at[pl.ds(first, rows), pl.ds(p * share, share)]
            pairs.append((gate.at[:, pl.ds(at, share)], here))
    for copy in fetch(pairs, sems):
        copy.wait()


def join(out, parts):
    at = 0
    for part in parts:
        out[at : at + part.shape[0], :] = part[...]
        at += part.shape[0]


def half_kernel(pos, *refs):
    parts, out = refs[:PLANE], refs[PLANE]
    for y in range(2):

        @pl.when(pos[0] == y)
        def _():
            join(out, parts[2 * y : 2 * y + 2])


def trade_kernel(pos, whole, near, joined, beside):
    rows, wide = whole.shape
    quarter = rows // 4
    joined[:rows, :] = whole[...]
    for q in range(2):
        here = slice(rows + q * quarter, rows + (q + 1) * quarter)
        joined[here, :] = near[near.shape[0] - quarter :, q * wide : (q + 1) * wide]
    beside[...] = near[: beside.shape[0], :]


def join_kernel(pos, *refs):
    join(refs[-1], refs[:-1])


def places_kernel(pos, own, mine, other, gate, *outs):
    planes, rows, share = outs[0].shape
    part = rows // 2
    for d, out in enumerate(outs):
        columns = pl.ds(pl.multiple_of(jnp.bitwise_xor(pos[2], d) * share, share), share)
        out[0] = own[:, columns]
        for side, block in ((pos[0], mine), (1 - pos[0], other)):
            out[2 + side] = block[:rows, columns]
            out[1, pl.ds(pl.multiple_of(side * part, part), part), :] = block[rows:, columns]
    for p in range(planes):
        outs[1][planes + p] = gate[:, p * share : (p + 1) * share]


def project_kernel(planes, pos, x, core, from_x, both, own, *refs):
    halves, outs = refs[:5], refs[5:-3]
    xs, ws, ps = refs[-3:]
    rows = x.shape[0]
    deep = own.shape[0] // PLANE
    share = outs[0].shape[1]
    join(xs, (x, core, from_x, both))
    for d in range(PLANE):
        ws[pl.ds(block_at(pos, 0, d, deep), deep), :] = own[d * deep : (d + 1) * deep, :]
    for half, k, first in zip(halves, (0, 0, 0, 1, 1), (1, 2, 3, 1, 3)):
        side = pos[0] if k == 0 else 1 - pos[0]
        for j in range(half.shape[0] // deep):
            at = block_at(pos, first + j // 2, 2 * side + j % 2, deep)
            ws[pl.ds(at, deep), :] = half[j * deep : (j + 1) * deep, :]
    ps[...] = dot(xs[...], ws[...]).astype(ps.dtype)
    for s in range(planes):
        at = pl.multiple_of(jnp.bitwise_xor(pos[1], s) * share, share)
        outs[s][...] = ps[:, pl.ds(at, share)]


def forward_stage(signal, first, work, blocks, rows):
    share = signal.shape[1]
    for pair in range(rows // (2 * ROWS)):
        halves = []
        for h in range(2):
            at = (2 * pair + h) * ROWS
            halves.append(
                jnp.concatenate(
                    [signal[b * rows + at : b * rows + at + ROWS, :] for b in range(blocks)], 0
                )
            )
        got = dot(first[...], jnp.concatenate(halves, 1)).astype(jnp.bfloat16)
        for h in range(2):
            at = (2 * pair + h) * ROWS
            for f in range(2 * blocks):
                work[f, at : at + ROWS, :] = got[
                    f * ROWS : (f + 1) * ROWS, h * share : (h + 1) * share
                ]


def spectrum_at(f, work, turned, blocks, rows):
    if f == 0 or f == blocks:
        return dot(turned[f, :, :rows], work[0 if f == 0 else 1])
    both = jnp.concatenate([work[2 * f], work[2 * f + 1]], 0)
    return dot(turned[f], both)


def taps_kernel(blocks, planes, pos, *refs):
    parts = refs[:PLANE]
    first, turned, out, signal, work = refs[PLANE:]
    rows = signal.shape[0] // blocks
    for d in range(PLANE):
        for s in range(planes):
            signal[pl.ds(block_at(pos, s, d, rows), rows), :] = parts[d][s]
    forward_stage(signal, first, work, blocks, rows)
    for f in range(blocks + 1):
        out[f] = spectrum_at(f, work, turned, blocks, rows).astype(out.dtype)


def conv_kernel(blocks, planes, pos, *refs):
    parts = refs[:planes]
    taps, skip, response, first, last, turned, back = refs[planes : planes + 7]
    outs = refs[planes + 7 : 3 * planes + 7]
    wide, value, work, result = refs[3 * planes + 7 :]
    rows = value.shape[0] // blocks
    share = value.shape[1]
    lead = wide.shape[0] - value.shape[0]
    own = pos[1] * PLANE + pos[2]
    columns = pl.ds(pl.multiple_of(own * share, share), share)
    taps, skip = taps[:, columns], skip[:, columns]
    wide[:lead, :] = jnp.zeros((lead, share), jnp.float32)
    for s in range(planes):
        for d in range(PLANE):
            at = block_at(pos, s, d, rows)
            wide[pl.ds(pl.multiple_of(lead + at, 8), rows), :] = parts[s][
                d * rows : (d + 1) * rows, :
            ].astype(jnp.float32)
    for b in range(blocks):
        at = lead + b * rows
        value[b * rows : (b + 1) * rows, :] = (
            taps[0:1, :] * wide[at : at + rows, :]
            + taps[1:2, :] * wide[at - 1 : at - 1 + rows, :]
            + taps[2:3, :] * wide[at - 2 : at - 2 + rows, :]
        ).astype(value.dtype)
    forward_stage(value, first, work, blocks, rows)
    for f in range(blocks + 1):
        got = spectrum_at(f, work, turned, blocks, rows)
        re, im = got[:rows], got[rows:]
        response_re = response[f, :rows, :].astype(jnp.float32)
        response_im = response[f, rows:, :].astype(jnp.float32)
        product = jnp.concatenate(
            [re * response_re - im * response_im, re * response_im + im * response_re], 0
        ).astype(jnp.bfloat16)
        if f == 0 or f == blocks:
            work[0 if f == 0 else 1] = dot(back[f, :rows, :], product).astype(work.dtype)
        else:
            inverse = dot(back[f], product).astype(work.dtype)
            work[2 * f] = inverse[:rows]
            work[2 * f + 1] = inverse[rows:]
    for pair in range(rows // (2 * ROWS)):
        halves = []
        for h in range(2):
            at = (2 * pair + h) * ROWS
            halves.append(
                jnp.concatenate([work[f, at : at + ROWS, :] for f in range(2 * blocks)], 0)
            )
        got = dot(last[...], jnp.concatenate(halves, 1))
        for h in range(2):
            at = (2 * pair + h) * ROWS
            for b in range(blocks):
                here = slice(b * rows + at, b * rows + at + ROWS)
                conv = got[b * ROWS : (b + 1) * ROWS, h * share : (h + 1) * share]
                result[here, :] = (
                    conv + skip * value[here, :].astype(jnp.float32)
                ).astype(result.dtype)
    for s in range(planes):
        for d in range(PLANE):
            half, at = d // 2, d % 2 * rows
            outs[half * planes + s][at : at + rows, :] = result[
                pl.ds(block_at(pos, s, d, rows), rows), :
            ]


def mixed_dots(planes, pos, u, gate, ws, mixed, outs):
    share = u[0].shape[1]
    rows = u[0].shape[0] // 2
    for s in range(planes):
        plane = jnp.bitwise_xor(pos[1], s)
        for d in range(2):
            if len(gate[d].shape) == 3:
                columns = gate[d][planes + plane]
            else:
                columns = gate[d][:rows, pl.ds(pl.multiple_of(plane * share, share), share)]
            mixed[d * rows : (d + 1) * rows, s * share : (s + 1) * share] = (
                columns.astype(jnp.float32)
                * u[s][d * rows : (d + 1) * rows, :].astype(jnp.float32)
            ).astype(mixed.dtype)
    got = dot(mixed[...], ws[...])
    outs[0][...] = got[:rows].astype(outs[0].dtype)
    width = outs[1].shape[1]
    for i, out in enumerate(outs[1:]):
        out[...] = got[rows:, i * width : (i + 1) * width].astype(out.dtype)


def upper_kernel(planes, pos, *refs):
    u, gate = refs[:planes], refs[planes : planes + 2]
    own, halves = refs[planes + 2], refs[planes + 3 : planes + 7]
    outs, ws, mixed = refs[planes + 7 : -2], refs[-2], refs[-1]
    share = u[0].shape[1]
    width = halves[0].shape[1]
    ws[:share, :] = own[...]
    for k in range(2):
        side = pos[0] if k == 0 else 1 - pos[0]
        columns = pl.ds(pl.multiple_of(side * width, width), width)
        ws[share : 2 * share, columns] = halves[2 * k][...]
        ws[2 * share :, columns] = halves[2 * k + 1][...]
    mixed_dots(planes, pos, u, gate, ws, mixed, outs)


def lower_kernel(planes, pos, *refs):
    u, gate, ws = refs[:planes], refs[planes : planes + 2], refs[planes + 2]
    mixed_dots(planes, pos, u, gate, ws, refs[-1], refs[planes + 3 : -1])


def local(inputs, gate_in, value_weight, short_taps, filter_taps, skip_scale, output_weight):
    rows, features = inputs.shape
    deep, channels = value_weight.shape
    devices = lax.axis_size("seq")
    planes = devices // PLANE
    share = channels // devices
    wide = planes * share
    blocks = devices
    index = lax.axis_index("seq")
    y = lax.axis_index("groups")
    z, place = index // PLANE, index % PLANE
    pos = jnp.stack([y, z, place]).astype(jnp.int32)

    def to_place(block, d):
        return lax.ppermute(block, "seq", [(i, i ^ d) for i in range(devices)])

    def to_plane(block, s):
        return lax.ppermute(block, "seq", [(i, i ^ (s * PLANE)) for i in range(devices)])

    def to_group(block):
        return lax.ppermute(block, "groups", [(0, 1), (1, 0)])

    def shaped(*shape, dtype=jnp.bfloat16):
        return jax.ShapeDtypeStruct(shape, dtype)

    def small(kernel, outs, *args, copies=0, fetched=0, vmem=2, flops=0):
        scratch = [pltpu.SemaphoreType.DMA((copies,))] if copies else []
        return list(call(kernel, outs, scratch, pos, args, flops, vmem=vmem, fetched=fetched))

    stage = lax.optimization_barrier
    first, last, turned, back = (
        jnp.asarray(t) for t in (*stage_tables(blocks), *turned_tables(blocks, rows))
    )
    part, width, positions = rows // 2, features // 2, blocks * rows

    *cut, taps_own, taps_whole, out_near, out_half = call(
        functools.partial(start_kernel, share),
        [shaped(deep, wide)] * PLANE
        + [shaped(rows, wide), shaped(rows, wide)]
        + [shaped(deep + rows // 4, width), shaped(deep, width)],
        [
            pltpu.VMEM((deep, channels), jnp.bfloat16),
            pltpu.VMEM((rows, channels), jnp.bfloat16),
            pltpu.SemaphoreType.DMA((9,)),
        ],
        pos,
        [value_weight, filter_taps, output_weight],
        0,
        vmem=53,
        fetched=3,
    )
    cut = list(cut)
    out_near = to_plane(out_near, 1)
    gate_own, gate_beside, gate_x = small(
        functools.partial(gate_kernel, share),
        [shaped(rows, wide), shaped(rows, wide), shaped(2 * rows, wide)],
        gate_in,
        copies=4 * planes,
        fetched=1,
    )
    core = to_place(inputs, 1)
    own = small(join_kernel, [shaped(deep, wide)], cut[0])
    cut = own + [to_place(cut[d], d) for d in range(1, PLANE)]
    route = [
        (y0 * devices + i, y0 * devices + (i ^ (2 + y0) * PLANE))
        for y0 in range(2)
        for i in range(devices)
    ]
    taps_whole = lax.ppermute(taps_whole, ("groups", "seq"), route)
    sent = small(half_kernel, [shaped(2 * deep, wide)], *cut, flops=1)[0]
    cut, taps_whole, late, core, out_near, sent, gate_own, gate_beside, gate_x = stage(
        (cut, taps_whole, inputs, core, out_near, sent, gate_own, gate_beside, gate_x)
    )

    taps_mine, out_near = small(
        trade_kernel,
        [shaped(rows * 3 // 2, wide), shaped(deep, width)],
        taps_whole,
        out_near,
    )
    near, far = to_plane(sent, 1), to_plane(sent, 2)
    from_x = to_place(late, 2)
    taps_other, out_other = to_group(taps_mine), to_group(out_near)
    near, far, from_x, taps_other, out_half, out_other = stage(
        (near, far, from_x, taps_other, out_half, out_other)
    )

    passed = to_plane(far, 1)
    other = small(
        join_kernel, [shaped(4 * deep, wide)], to_group(near), to_group(far), flops=1073741824
    )[0]
    out_far = to_plane(out_half, 2)
    both = to_place(from_x, 1)
    taps_parts = small(
        places_kernel,
        [shaped(planes * (2 if d == 1 else 1), rows, share) for d in range(PLANE)],
        taps_own,
        taps_mine,
        taps_other,
        gate_beside,
    )
    other, passed, both = stage((other, passed, both))
    passed_other = to_group(passed)
    taps_parts = [taps_parts[0]] + [to_place(taps_parts[d], d) for d in range(1, PLANE)]
    held = small(join_kernel, [shaped(PLANE * deep, wide)], *cut)[0]
    weights = small(join_kernel, [shaped(2 * deep, width)], out_far, to_plane(out_far, 1))[0]
    passed, other, both, taps_parts, passed_other, held = stage(
        (passed, other, both, taps_parts, passed_other, held)
    )
    projected = call(
        functools.partial(project_kernel, planes),
        [shaped(PLANE * rows, share)] * planes,
        [
            pltpu.VMEM((PLANE * rows, features), jnp.bfloat16),
            pltpu.VMEM((features, wide), jnp.bfloat16),
            pltpu.VMEM((PLANE * rows, wide), jnp.bfloat16),
        ],
        pos,
        [inputs, core, from_x, both, held, near, far, passed, other, passed_other],
        2 * PLANE * rows * features * wide,
        vmem=8,
    )
    projected, weights, gate_x = stage((projected, weights, gate_x))

    def spread(parts):
        sent = [to_plane(parts[s], s) for s in reversed(range(1, planes))]
        return [parts[0]] + sent[::-1]

    signal = spread(projected)
    weights_other = to_group(weights)
    gate_x = to_place(gate_x, 2)
    response = call(
        functools.partial(taps_kernel, blocks, planes),
        [shaped(blocks + 1, 2 * rows, share)],
        [
            pltpu.VMEM((positions, share), jnp.bfloat16),
            pltpu.VMEM((2 * blocks, rows, share), jnp.bfloat16),
        ],
        pos,
        [*taps_parts, first, turned],
        2 * positions * share * (32 * ROWS + 4 * rows),
        vmem=4,
    )[0]
    signal, response = stage((signal[::-1], response))
    signal = signal[::-1]

    mixed = call(
        functools.partial(conv_kernel, blocks, planes),
        [shaped(2 * rows, share)] * (2 * planes),
        [
            pltpu.VMEM((positions + 8, share), jnp.float32),
            pltpu.VMEM((positions, share), jnp.bfloat16),
            pltpu.VMEM((2 * blocks, rows, share), jnp.bfloat16),
            pltpu.VMEM((positions, share), jnp.bfloat16),
        ],
        pos,
        [*signal, short_taps, skip_scale[None], response, first, last, turned, back],
        16 * positions * share * (32 * ROWS + 4 * rows),
        vmem=8,
    )
    mixed, weights_other, gate_x = stage((mixed, weights_other, gate_x))

    upper = spread(mixed[planes:])
    gate_three = to_place(gate_x[rows:], 1)
    upper, lower, gate_three = stage((upper[::-1], mixed[:planes], gate_three))
    upper = upper[::-1]
    scratch = [pltpu.VMEM((2 * rows, wide), jnp.bfloat16)]
    flops = 4 * rows * features * wide
    partial_two, partial_three, gathered = call(
        functools.partial(upper_kernel, planes),
        [shaped(rows, features, dtype=jnp.float32), shaped(rows, features)]
        + [shaped(wide, features)],
        scratch,
        pos,
        [*upper, gate_x, gate_three, output_weight]
        + [out_near, weights, out_other, weights_other],
        flops,
        vmem=8,
    )
    across = partial_two + to_place(partial_three, 1).astype(jnp.float32)
    across, lower = stage((across.astype(jnp.bfloat16), lower))

    across = to_place(across, 2)
    lower = spread(lower)
    partial_zero, *partial_one = call(
        functools.partial(lower_kernel, planes),
        [shaped(rows, features, dtype=jnp.float32)] + [shaped(rows, features // 4)] * 4,
        scratch,
        pos,
        [*lower, gate_own, taps_parts[1], gathered],
        0,
        vmem=8,
    )
    partial_one = jnp.concatenate([to_place(block, 1) for block in partial_one], 1)
    result = partial_zero + partial_one.astype(jnp.float32) + across.astype(jnp.float32)
    return result.astype(jnp.bfloat16)


def passed_along(block, axis, distance):
    devices = range(lax.axis_size(axis))
    route = [(i - distance, i) for i in devices if i - distance in devices]
    return lax.ppermute(block, axis, route)


def local_narrow(inputs, gate_in, value_weight, short_taps, filter_taps, skip_scale, output_weight):
    rows, features = inputs.shape
    channels = value_weight.shape[1]
    blocks = lax.axis_size("seq")
    share = channels // blocks
    index = lax.axis_index("seq")
    projected = dot(inputs, lax.all_gather(value_weight, "seq", axis=0, tiled=True)).astype(
        jnp.bfloat16
    )
    earlier = passed_along(projected[rows - 2 :], "seq", 1)
    extended = jnp.concatenate([earlier, projected], 0).astype(jnp.float32)
    value = (
        short_taps[0] * extended[2:]
        + short_taps[1] * extended[1:-1]
        + short_taps[2] * extended[:-2]
    ).astype(jnp.bfloat16)

    def by_channel(signal):
        cut = signal.reshape(rows, blocks, share)
        got = lax.all_to_all(cut, "seq", split_axis=1, concat_axis=0, tiled=True)
        return got.reshape(blocks, rows, share)

    grid = np.arange(2 * blocks)
    angle = 2.0 * np.pi * (grid[:, None] * grid[None, :] % (2 * blocks)) / (2 * blocks)
    wide = np.exp(-1j * angle)[: blocks + 1, :blocks]
    turned, back = (jnp.asarray(t) for t in turned_tables(blocks, rows))
    weight = np.full((blocks + 1, 1), 2.0)
    weight[0] = weight[-1] = 1.0
    narrow = weight * np.conj(wide) / (2 * blocks * rows)

    def einsum(form, table, data):
        return jnp.einsum(form, table, data, preferred_element_type=jnp.float32)

    def table(values):
        return jnp.asarray(values.astype(ml_dtypes.bfloat16))

    def forward(signal):
        re = einsum("fb,bmc->fmc", table(np.real(wide)), signal)
        im = einsum("fb,bmc->fmc", table(np.imag(wide)), signal)
        both = jnp.concatenate([re, im], 1).astype(jnp.bfloat16)
        return einsum("fkm,fmc->fkc", turned, both)

    response = forward(by_channel(filter_taps))
    got = forward(by_channel(value))
    re, im = got[:, :rows], got[:, rows:]
    response_re, response_im = response[:, :rows], response[:, rows:]
    product = jnp.concatenate(
        [re * response_re - im * response_im, re * response_im + im * response_re], 1
    ).astype(jnp.bfloat16)
    inverse = einsum("fmk,fkc->fmc", back, product).astype(jnp.bfloat16)
    conv = einsum("fb,fmc->bmc", table(np.real(narrow)), inverse[:, :rows]) - einsum(
        "fb,fmc->bmc", table(np.imag(narrow)), inverse[:, rows:]
    )
    conv = lax.all_to_all(
        conv.astype(jnp.bfloat16), "seq", split_axis=0, concat_axis=2, tiled=True
    ).reshape(rows, channels)
    mixed = (
        gate_in.astype(jnp.float32)
        * (conv.astype(jnp.float32) + skip_scale * value.astype(jnp.float32))
    ).astype(jnp.bfloat16)
    result = dot(mixed, lax.all_gather(output_weight, "seq", axis=0, tiled=True))
    return result.astype(jnp.bfloat16)


def solution(mesh):
    split = P(("groups", "seq"), None)
    placed = (split, split, P("seq", None), P(), P("seq", None), P(), P("seq", None))

    def run(*args):
        devices = mesh.shape["seq"]
        share = args[2].shape[1] // devices
        tiled = share % LANES == 0 and args[0].shape[0] // mesh.size == LANES
        paired = devices == 4 * PLANE and mesh.shape["groups"] == 2
        body = local if tiled and paired else local_narrow
        return jax.shard_map(body, mesh=mesh, in_specs=placed, out_specs=split, check_vma=False)(
            *args
        )

    return run
```

```python
import functools
import math

import jax
import jax.numpy as jnp
import ml_dtypes
import numpy as np
from jax import lax
from jax.experimental import pallas as pl
from jax.experimental.pallas import tpu as pltpu
from jax.sharding import PartitionSpec as P

PLANE = 4
LANES = 128
ROWS = 16
MIB = 1 << 20


def stage_tables(blocks):
    width = 2 * blocks
    b = np.arange(blocks)
    forward = [np.ones(blocks), np.cos(np.pi * b)]
    backward = [np.ones(blocks), np.cos(np.pi * b)]
    for f in range(1, blocks):
        angle = 2.0 * np.pi * (f * b % width) / width
        forward += [np.cos(angle), -np.sin(angle)]
        backward += [2.0 * np.cos(angle), -2.0 * np.sin(angle)]
    eye = np.eye(ROWS)
    first = np.kron(np.stack(forward, 0), eye)
    last = np.kron(np.stack(backward, 1), eye) / (width * LANES)
    return first.astype(ml_dtypes.bfloat16), last.astype(ml_dtypes.bfloat16)


def turned_tables(blocks, rows):
    width = 2 * blocks
    k = np.arange(rows)[:, None]
    m = np.arange(rows)[None, :]
    out = []
    for f in range(blocks + 1):
        angle = 2.0 * np.pi * ((width * k + f) * m % (width * rows)) / (width * rows)
        cos, sin = np.cos(angle), np.sin(angle)
        out.append(np.block([[cos, sin], [-sin, cos]]))
    forward = np.stack(out, 0)
    return (
        forward.astype(ml_dtypes.bfloat16),
        np.swapaxes(forward, 1, 2).astype(ml_dtypes.bfloat16),
    )


def dot(left, right):
    return jnp.dot(left, right, preferred_element_type=jnp.float32)


def call(kernel, outs, scratch, pos, args, flops, vmem=4, fetched=0):
    in_specs = [pl.BlockSpec(memory_space=pltpu.SMEM)]
    in_specs += [pl.BlockSpec(memory_space=pltpu.HBM)] * fetched
    in_specs += [pl.BlockSpec(memory_space=pltpu.VMEM)] * (len(args) - fetched)
    moved = sum(a.size * a.dtype.itemsize for a in args) if flops else 0
    moved += sum(math.prod(o.shape) * o.dtype.itemsize for o in outs) if flops else 0
    return pl.pallas_call(
        kernel,
        out_shape=outs,
        in_specs=in_specs,
        out_specs=[pl.BlockSpec(memory_space=pltpu.VMEM)] * len(outs),
        scratch_shapes=scratch,
        compiler_params=pltpu.CompilerParams(vmem_limit_bytes=vmem * MIB),
        cost_estimate=pl.CostEstimate(flops=flops, bytes_accessed=moved, transcendentals=0),
    )(pos, *args)


def block_at(pos, s, d, rows):
    block = jnp.bitwise_xor(pos[1], s) * PLANE + jnp.bitwise_xor(pos[2], d)
    return pl.multiple_of(block * rows, rows)


def fetch(pairs, sems):
    copies = [pltpu.make_async_copy(src, dst, sems.at[i]) for i, (src, dst) in enumerate(pairs)]
    for copy in copies:
        copy.start()
    return copies


def start_kernel(share, pos, weight, taps, out_weight, *refs):
    outs, (own, whole, near, out_half) = refs[:PLANE], refs[PLANE : PLANE + 4]
    weight_here, taps_here, sems = refs[PLANE + 4 :]
    rows, wide = own.shape
    deep, width = out_half.shape
    quarter = rows // 4
    side = pl.ds(pl.multiple_of(pos[0] * width, width), width)
    pairs = []
    for source, here in ((weight, weight_here), (taps, taps_here)):
        for q in range(4):
            cut = pl.ds(q * quarter, quarter)
            pairs.append((source.at[cut], here.at[cut]))
    pairs.append((out_weight.at[:, side], out_half))
    copies = fetch(pairs, sems)
    for copy in copies[:4]:
        copy.wait()
    for d, out in enumerate(outs):
        place = jnp.bitwise_xor(pos[2], d)
        for p in range(wide // share):
            at = pl.multiple_of((p * PLANE + place) * share, share)
            out[:, p * share : (p + 1) * share] = weight_here[:, pl.ds(at, share)]
    for copy in copies[4:]:
        copy.wait()

    def columns(s):
        return pl.ds(pl.multiple_of(jnp.bitwise_xor(pos[1], s) * wide, wide), wide)

    own[...] = taps_here[:, columns(0)]
    whole[...] = taps_here[:, columns(2 + pos[0])]
    near[:deep, :] = out_half[...]
    for q in range(2):
        first = pl.multiple_of(pos[0] * (rows // 2) + q * quarter, quarter)
        near[deep:, q * wide : (q + 1) * wide] = taps_here[pl.ds(first, quarter), columns(1)]


def gate_kernel(share, pos, gate, own, beside, across, sems):
    rows, wide = own.shape
    pairs = []
    for d, (out, first) in enumerate(((own, 0), (beside, 0), (across, 0), (across, rows))):
        place = jnp.bitwise_xor(pos[2], d)
        for p in range(wide // share):
            at = pl.multiple_of((p * PLANE + place) * share, share)
            here = out.at[pl.ds(first, rows), pl.ds(p * share, share)]
            pairs.append((gate.at[:, pl.ds(at, share)], here))
    for copy in fetch(pairs, sems):
        copy.wait()


def join(out, parts):
    at = 0
    for part in parts:
        out[at : at + part.shape[0], :] = part[...]
        at += part.shape[0]


def half_kernel(pos, *refs):
    parts, out = refs[:PLANE], refs[PLANE]
    for y in range(2):

        @pl.when(pos[0] == y)
        def _():
            join(out, parts[2 * y : 2 * y + 2])


def trade_kernel(pos, whole, near, joined, beside):
    rows, wide = whole.shape
    quarter = rows // 4
    joined[:rows, :] = whole[...]
    for q in range(2):
        here = slice(rows + q * quarter, rows + (q + 1) * quarter)
        joined[here, :] = near[near.shape[0] - quarter :, q * wide : (q + 1) * wide]
    beside[...] = near[: beside.shape[0], :]


def join_kernel(pos, *refs):
    join(refs[-1], refs[:-1])


def places_kernel(pos, own, mine, other, gate, *outs):
    planes, rows, share = outs[0].shape
    part = rows // 2
    for d, out in enumerate(outs):
        columns = pl.ds(pl.multiple_of(jnp.bitwise_xor(pos[2], d) * share, share), share)
        out[0] = own[:, columns]
        for side, block in ((pos[0], mine), (1 - pos[0], other)):
            out[2 + side] = block[:rows, columns]
            out[1, pl.ds(pl.multiple_of(side * part, part), part), :] = block[rows:, columns]
    for p in range(planes):
        outs[1][planes + p] = gate[:, p * share : (p + 1) * share]


def project_kernel(planes, pos, x, core, from_x, both, own, *refs):
    halves, outs = refs[:5], refs[5:-3]
    xs, ws, ps = refs[-3:]
    rows = x.shape[0]
    deep = own.shape[0] // PLANE
    share = outs[0].shape[1]
    join(xs, (x, core, from_x, both))
    for d in range(PLANE):
        ws[pl.ds(block_at(pos, 0, d, deep), deep), :] = own[d * deep : (d + 1) * deep, :]
    for half, k, first in zip(halves, (0, 0, 0, 1, 1), (1, 2, 3, 1, 3)):
        side = pos[0] if k == 0 else 1 - pos[0]
        for j in range(half.shape[0] // deep):
            at = block_at(pos, first + j // 2, 2 * side + j % 2, deep)
            ws[pl.ds(at, deep), :] = half[j * deep : (j + 1) * deep, :]
    ps[...] = dot(xs[...], ws[...]).astype(ps.dtype)
    for s in range(planes):
        at = pl.multiple_of(jnp.bitwise_xor(pos[1], s) * share, share)
        outs[s][...] = ps[:, pl.ds(at, share)]


def forward_stage(signal, first, work, blocks, rows):
    share = signal.shape[1]
    for pair in range(rows // (2 * ROWS)):
        halves = []
        for h in range(2):
            at = (2 * pair + h) * ROWS
            halves.append(
                jnp.concatenate(
                    [signal[b * rows + at : b * rows + at + ROWS, :] for b in range(blocks)], 0
                )
            )
        got = dot(first[...], jnp.concatenate(halves, 1)).astype(jnp.bfloat16)
        for h in range(2):
            at = (2 * pair + h) * ROWS
            for f in range(2 * blocks):
                work[f, at : at + ROWS, :] = got[
                    f * ROWS : (f + 1) * ROWS, h * share : (h + 1) * share
                ]


def spectrum_at(f, work, turned, blocks, rows):
    if f == 0 or f == blocks:
        return dot(turned[f, :, :rows], work[0 if f == 0 else 1])
    both = jnp.concatenate([work[2 * f], work[2 * f + 1]], 0)
    return dot(turned[f], both)


def taps_kernel(blocks, planes, pos, *refs):
    parts = refs[:PLANE]
    first, turned, out, signal, work = refs[PLANE:]
    rows = signal.shape[0] // blocks
    for d in range(PLANE):
        for s in range(planes):
            signal[pl.ds(block_at(pos, s, d, rows), rows), :] = parts[d][s]
    forward_stage(signal, first, work, blocks, rows)
    for f in range(blocks + 1):
        out[f] = spectrum_at(f, work, turned, blocks, rows).astype(out.dtype)


def conv_kernel(blocks, planes, pos, *refs):
    parts = refs[:planes]
    taps, skip, response, first, last, turned, back = refs[planes : planes + 7]
    outs = refs[planes + 7 : 3 * planes + 7]
    wide, value, work, result = refs[3 * planes + 7 :]
    rows = value.shape[0] // blocks
    share = value.shape[1]
    lead = wide.shape[0] - value.shape[0]
    own = pos[1] * PLANE + pos[2]
    columns = pl.ds(pl.multiple_of(own * share, share), share)
    taps, skip = taps[:, columns], skip[:, columns]
    wide[:lead, :] = jnp.zeros((lead, share), jnp.float32)
    for s in range(planes):
        for d in range(PLANE):
            at = block_at(pos, s, d, rows)
            wide[pl.ds(pl.multiple_of(lead + at, 8), rows), :] = parts[s][
                d * rows : (d + 1) * rows, :
            ].astype(jnp.float32)
    for b in range(blocks):
        at = lead + b * rows
        value[b * rows : (b + 1) * rows, :] = (
            taps[0:1, :] * wide[at : at + rows, :]
            + taps[1:2, :] * wide[at - 1 : at - 1 + rows, :]
            + taps[2:3, :] * wide[at - 2 : at - 2 + rows, :]
        ).astype(value.dtype)
    forward_stage(value, first, work, blocks, rows)
    for f in range(blocks + 1):
        got = spectrum_at(f, work, turned, blocks, rows)
        re, im = got[:rows], got[rows:]
        response_re = response[f, :rows, :].astype(jnp.float32)
        response_im = response[f, rows:, :].astype(jnp.float32)
        product = jnp.concatenate(
            [re * response_re - im * response_im, re * response_im + im * response_re], 0
        ).astype(jnp.bfloat16)
        if f == 0 or f == blocks:
            work[0 if f == 0 else 1] = dot(back[f, :rows, :], product).astype(work.dtype)
        else:
            inverse = dot(back[f], product).astype(work.dtype)
            work[2 * f] = inverse[:rows]
            work[2 * f + 1] = inverse[rows:]
    for pair in range(rows // (2 * ROWS)):
        halves = []
        for h in range(2):
            at = (2 * pair + h) * ROWS
            halves.append(
                jnp.concatenate([work[f, at : at + ROWS, :] for f in range(2 * blocks)], 0)
            )
        got = dot(last[...], jnp.concatenate(halves, 1))
        for h in range(2):
            at = (2 * pair + h) * ROWS
            for b in range(blocks):
                here = slice(b * rows + at, b * rows + at + ROWS)
                conv = got[b * ROWS : (b + 1) * ROWS, h * share : (h + 1) * share]
                result[here, :] = (
                    conv + skip * value[here, :].astype(jnp.float32)
                ).astype(result.dtype)
    for s in range(planes):
        for d in range(PLANE):
            half, at = d // 2, d % 2 * rows
            outs[half * planes + s][at : at + rows, :] = result[
                pl.ds(block_at(pos, s, d, rows), rows), :
            ]


def mixed_dots(planes, pos, u, gate, ws, mixed, outs):
    share = u[0].shape[1]
    rows = u[0].shape[0] // 2
    for s in range(planes):
        plane = jnp.bitwise_xor(pos[1], s)
        for d in range(2):
            if len(gate[d].shape) == 3:
                columns = gate[d][planes + plane]
            else:
                columns = gate[d][:rows, pl.ds(pl.multiple_of(plane * share, share), share)]
            mixed[d * rows : (d + 1) * rows, s * share : (s + 1) * share] = (
                columns.astype(jnp.float32)
                * u[s][d * rows : (d + 1) * rows, :].astype(jnp.float32)
            ).astype(mixed.dtype)
    got = dot(mixed[...], ws[...])
    outs[0][...] = got[:rows].astype(outs[0].dtype)
    width = outs[1].shape[1]
    for i, out in enumerate(outs[1:]):
        out[...] = got[rows:, i * width : (i + 1) * width].astype(out.dtype)


def upper_kernel(planes, pos, *refs):
    u, gate = refs[:planes], refs[planes : planes + 2]
    own, halves = refs[planes + 2], refs[planes + 3 : planes + 7]
    outs, ws, mixed = refs[planes + 7 : -2], refs[-2], refs[-1]
    share = u[0].shape[1]
    width = halves[0].shape[1]
    ws[:share, :] = own[...]
    for k in range(2):
        side = pos[0] if k == 0 else 1 - pos[0]
        columns = pl.ds(pl.multiple_of(side * width, width), width)
        ws[share : 2 * share, columns] = halves[2 * k][...]
        ws[2 * share :, columns] = halves[2 * k + 1][...]
    mixed_dots(planes, pos, u, gate, ws, mixed, outs)


def lower_kernel(planes, pos, *refs):
    u, gate, ws = refs[:planes], refs[planes : planes + 2], refs[planes + 2]
    mixed_dots(planes, pos, u, gate, ws, refs[-1], refs[planes + 3 : -1])


def local(inputs, gate_in, value_weight, short_taps, filter_taps, skip_scale, output_weight):
    rows, features = inputs.shape
    deep, channels = value_weight.shape
    devices = lax.axis_size("seq")
    planes = devices // PLANE
    share = channels // devices
    wide = planes * share
    blocks = devices
    index = lax.axis_index("seq")
    y = lax.axis_index("groups")
    z, place = index // PLANE, index % PLANE
    pos = jnp.stack([y, z, place]).astype(jnp.int32)

    def to_place(block, d):
        return lax.ppermute(block, "seq", [(i, i ^ d) for i in range(devices)])

    def to_plane(block, s):
        return lax.ppermute(block, "seq", [(i, i ^ (s * PLANE)) for i in range(devices)])

    def to_group(block):
        return lax.ppermute(block, "groups", [(0, 1), (1, 0)])

    def shaped(*shape, dtype=jnp.bfloat16):
        return jax.ShapeDtypeStruct(shape, dtype)

    def small(kernel, outs, *args, copies=0, fetched=0, vmem=2, flops=0):
        scratch = [pltpu.SemaphoreType.DMA((copies,))] if copies else []
        return list(call(kernel, outs, scratch, pos, args, flops, vmem=vmem, fetched=fetched))

    stage = lax.optimization_barrier
    first, last, turned, back = (
        jnp.asarray(t) for t in (*stage_tables(blocks), *turned_tables(blocks, rows))
    )
    part, width, positions = rows // 2, features // 2, blocks * rows

    *cut, taps_own, taps_whole, out_near, out_half = call(
        functools.partial(start_kernel, share),
        [shaped(deep, wide)] * PLANE
        + [shaped(rows, wide), shaped(rows, wide)]
        + [shaped(deep + rows // 4, width), shaped(deep, width)],
        [
            pltpu.VMEM((deep, channels), jnp.bfloat16),
            pltpu.VMEM((rows, channels), jnp.bfloat16),
            pltpu.SemaphoreType.DMA((9,)),
        ],
        pos,
        [value_weight, filter_taps, output_weight],
        0,
        vmem=53,
        fetched=3,
    )
    cut = list(cut)
    out_near = to_plane(out_near, 1)
    gate_own, gate_beside, gate_x = small(
        functools.partial(gate_kernel, share),
        [shaped(rows, wide), shaped(rows, wide), shaped(2 * rows, wide)],
        gate_in,
        copies=4 * planes,
        fetched=1,
    )
    core = to_place(inputs, 1)
    own = small(join_kernel, [shaped(deep, wide)], cut[0])
    cut = own + [to_place(cut[d], d) for d in range(1, PLANE)]
    route = [
        (y0 * devices + i, y0 * devices + (i ^ (2 + y0) * PLANE))
        for y0 in range(2)
        for i in range(devices)
    ]
    taps_whole = lax.ppermute(taps_whole, ("groups", "seq"), route)
    sent = small(half_kernel, [shaped(2 * deep, wide)], *cut, flops=1)[0]
    cut, taps_whole, late, core, out_near, sent, gate_own, gate_beside, gate_x = stage(
        (cut, taps_whole, inputs, core, out_near, sent, gate_own, gate_beside, gate_x)
    )

    taps_mine, out_near = small(
        trade_kernel,
        [shaped(rows * 3 // 2, wide), shaped(deep, width)],
        taps_whole,
        out_near,
    )
    near, far = to_plane(sent, 1), to_plane(sent, 2)
    from_x = to_place(late, 2)
    taps_other, out_other = to_group(taps_mine), to_group(out_near)
    near, far, taps_other, out_half, out_other = stage(
        (near, far, taps_other, out_half, out_other)
    )

    passed = to_plane(far, 1)
    other = small(
        join_kernel, [shaped(4 * deep, wide)], to_group(near), to_group(far), flops=1 << 30
    )[0]
    out_far = to_plane(out_half, 2)
    both = to_place(from_x, 1)
    taps_parts = small(
        places_kernel,
        [shaped(planes * (2 if d == 1 else 1), rows, share) for d in range(PLANE)],
        taps_own,
        taps_mine,
        taps_other,
        gate_beside,
    )
    other, passed, both = stage((other, passed, both))
    passed_other = to_group(passed)
    taps_parts = [taps_parts[0]] + [to_place(taps_parts[d], d) for d in range(1, PLANE)]
    held = small(join_kernel, [shaped(PLANE * deep, wide)], *cut)[0]
    weights = small(join_kernel, [shaped(2 * deep, width)], out_far, to_plane(out_far, 1))[0]
    passed, other, both, taps_parts, passed_other, held = stage(
        (passed, other, both, taps_parts, passed_other, held)
    )
    projected = call(
        functools.partial(project_kernel, planes),
        [shaped(PLANE * rows, share)] * planes,
        [
            pltpu.VMEM((PLANE * rows, features), jnp.bfloat16),
            pltpu.VMEM((features, wide), jnp.bfloat16),
            pltpu.VMEM((PLANE * rows, wide), jnp.bfloat16),
        ],
        pos,
        [inputs, core, from_x, both, held, near, far, passed, other, passed_other],
        2 * PLANE * rows * features * wide,
        vmem=8,
    )
    projected, weights, gate_x = stage((projected, weights, gate_x))

    def spread(parts):
        sent = [to_plane(parts[s], s) for s in reversed(range(1, planes))]
        return [parts[0]] + sent[::-1]

    signal = spread(projected)
    weights_other = to_group(weights)
    gate_x = to_place(gate_x, 2)
    response = call(
        functools.partial(taps_kernel, blocks, planes),
        [shaped(blocks + 1, 2 * rows, share)],
        [
            pltpu.VMEM((positions, share), jnp.bfloat16),
            pltpu.VMEM((2 * blocks, rows, share), jnp.bfloat16),
        ],
        pos,
        [*taps_parts, first, turned],
        2 * positions * share * (32 * ROWS + 4 * rows),
        vmem=4,
    )[0]
    signal, response = stage((signal[::-1], response))
    signal = signal[::-1]

    mixed = call(
        functools.partial(conv_kernel, blocks, planes),
        [shaped(2 * rows, share)] * (2 * planes),
        [
            pltpu.VMEM((positions + 8, share), jnp.float32),
            pltpu.VMEM((positions, share), jnp.bfloat16),
            pltpu.VMEM((2 * blocks, rows, share), jnp.bfloat16),
            pltpu.VMEM((positions, share), jnp.bfloat16),
        ],
        pos,
        [*signal, short_taps, skip_scale[None], response, first, last, turned, back],
        16 * positions * share * (32 * ROWS + 4 * rows),
        vmem=8,
    )
    mixed, weights_other, gate_x = stage((mixed, weights_other, gate_x))

    upper = spread(mixed[planes:])
    gate_three = to_place(gate_x[rows:], 1)
    upper, lower, gate_three = stage((upper[::-1], mixed[:planes], gate_three))
    upper = upper[::-1]
    scratch = [pltpu.VMEM((2 * rows, wide), jnp.bfloat16)]
    flops = 4 * rows * features * wide
    partial_two, partial_three, gathered = call(
        functools.partial(upper_kernel, planes),
        [shaped(rows, features, dtype=jnp.float32), shaped(rows, features)]
        + [shaped(wide, features)],
        scratch,
        pos,
        [*upper, gate_x, gate_three, output_weight]
        + [out_near, weights, out_other, weights_other],
        flops,
        vmem=8,
    )
    across = partial_two + to_place(partial_three, 1).astype(jnp.float32)
    across, lower = stage((across.astype(jnp.bfloat16), lower))

    across = to_place(across, 2)
    lower = spread(lower)
    partial_zero, *partial_one = call(
        functools.partial(lower_kernel, planes),
        [shaped(rows, features, dtype=jnp.float32)] + [shaped(rows, features // 4)] * 4,
        scratch,
        pos,
        [*lower, gate_own, taps_parts[1], gathered],
        0,
        vmem=8,
    )
    partial_one = jnp.concatenate([to_place(block, 1) for block in partial_one], 1)
    result = partial_zero + partial_one.astype(jnp.float32) + across.astype(jnp.float32)
    return result.astype(jnp.bfloat16)


def passed_along(block, axis, distance):
    devices = range(lax.axis_size(axis))
    route = [(i - distance, i) for i in devices if i - distance in devices]
    return lax.ppermute(block, axis, route)


def local_narrow(inputs, gate_in, value_weight, short_taps, filter_taps, skip_scale, output_weight):
    rows, features = inputs.shape
    channels = value_weight.shape[1]
    blocks = lax.axis_size("seq")
    share = channels // blocks
    index = lax.axis_index("seq")
    projected = dot(inputs, lax.all_gather(value_weight, "seq", axis=0, tiled=True)).astype(
        jnp.bfloat16
    )
    earlier = passed_along(projected[rows - 2 :], "seq", 1)
    extended = jnp.concatenate([earlier, projected], 0).astype(jnp.float32)
    value = (
        short_taps[0] * extended[2:]
        + short_taps[1] * extended[1:-1]
        + short_taps[2] * extended[:-2]
    ).astype(jnp.bfloat16)

    def by_channel(signal):
        cut = signal.reshape(rows, blocks, share)
        got = lax.all_to_all(cut, "seq", split_axis=1, concat_axis=0, tiled=True)
        return got.reshape(blocks, rows, share)

    grid = np.arange(2 * blocks)
    angle = 2.0 * np.pi * (grid[:, None] * grid[None, :] % (2 * blocks)) / (2 * blocks)
    wide = np.exp(-1j * angle)[: blocks + 1, :blocks]
    turned, back = (jnp.asarray(t) for t in turned_tables(blocks, rows))
    weight = np.full((blocks + 1, 1), 2.0)
    weight[0] = weight[-1] = 1.0
    narrow = weight * np.conj(wide) / (2 * blocks * rows)

    def einsum(form, table, data):
        return jnp.einsum(form, table, data, preferred_element_type=jnp.float32)

    def table(values):
        return jnp.asarray(values.astype(ml_dtypes.bfloat16))

    def forward(signal):
        re = einsum("fb,bmc->fmc", table(np.real(wide)), signal)
        im = einsum("fb,bmc->fmc", table(np.imag(wide)), signal)
        both = jnp.concatenate([re, im], 1).astype(jnp.bfloat16)
        return einsum("fkm,fmc->fkc", turned, both)

    response = forward(by_channel(filter_taps))
    got = forward(by_channel(value))
    re, im = got[:, :rows], got[:, rows:]
    response_re, response_im = response[:, :rows], response[:, rows:]
    product = jnp.concatenate(
        [re * response_re - im * response_im, re * response_im + im * response_re], 1
    ).astype(jnp.bfloat16)
    inverse = einsum("fmk,fkc->fmc", back, product).astype(jnp.bfloat16)
    conv = einsum("fb,fmc->bmc", table(np.real(narrow)), inverse[:, :rows]) - einsum(
        "fb,fmc->bmc", table(np.imag(narrow)), inverse[:, rows:]
    )
    conv = lax.all_to_all(
        conv.astype(jnp.bfloat16), "seq", split_axis=0, concat_axis=2, tiled=True
    ).reshape(rows, channels)
    mixed = (
        gate_in.astype(jnp.float32)
        * (conv.astype(jnp.float32) + skip_scale * value.astype(jnp.float32))
    ).astype(jnp.bfloat16)
    result = dot(mixed, lax.all_gather(output_weight, "seq", axis=0, tiled=True))
    return result.astype(jnp.bfloat16)


def solution(mesh):
    split = P(("groups", "seq"), None)
    placed = (split, split, P("seq", None), P(), P("seq", None), P(), P("seq", None))

    def run(*args):
        devices = mesh.shape["seq"]
        share = args[2].shape[1] // devices
        tiled = share % LANES == 0 and args[0].shape[0] // mesh.size == LANES
        paired = devices == 4 * PLANE and mesh.shape["groups"] == 2
        body = local if tiled and paired else local_narrow
        return jax.shard_map(body, mesh=mesh, in_specs=placed, out_specs=split, check_vma=False)(
            *args
        )

    return run
```

```python
import functools
import math

import jax
import jax.numpy as jnp
import ml_dtypes
import numpy as np
from jax import lax
from jax.experimental import pallas as pl
from jax.experimental.pallas import tpu as pltpu
from jax.sharding import PartitionSpec as P

PLANE = 4
LANES = 128
ROWS = 16
MIB = 1 << 20


def stage_tables(blocks):
    width = 2 * blocks
    b = np.arange(blocks)
    forward = [np.ones(blocks), np.cos(np.pi * b)]
    backward = [np.ones(blocks), np.cos(np.pi * b)]
    for f in range(1, blocks):
        angle = 2.0 * np.pi * (f * b % width) / width
        forward += [np.cos(angle), -np.sin(angle)]
        backward += [2.0 * np.cos(angle), -2.0 * np.sin(angle)]
    eye = np.eye(ROWS)
    first = np.kron(np.stack(forward, 0), eye)
    last = np.kron(np.stack(backward, 1), eye) / (width * LANES)
    return first.astype(ml_dtypes.bfloat16), last.astype(ml_dtypes.bfloat16)


def turned_tables(blocks, rows):
    width = 2 * blocks
    k = np.arange(rows)[:, None]
    m = np.arange(rows)[None, :]
    out = []
    for f in range(blocks + 1):
        angle = 2.0 * np.pi * ((width * k + f) * m % (width * rows)) / (width * rows)
        cos, sin = np.cos(angle), np.sin(angle)
        out.append(np.block([[cos, sin], [-sin, cos]]))
    forward = np.stack(out, 0)
    return (
        forward.astype(ml_dtypes.bfloat16),
        np.swapaxes(forward, 1, 2).astype(ml_dtypes.bfloat16),
    )


def dot(left, right):
    return jnp.dot(left, right, preferred_element_type=jnp.float32)


def call(kernel, outs, scratch, pos, args, flops, vmem=4, fetched=0):
    in_specs = [pl.BlockSpec(memory_space=pltpu.SMEM)]
    in_specs += [pl.BlockSpec(memory_space=pltpu.HBM)] * fetched
    in_specs += [pl.BlockSpec(memory_space=pltpu.VMEM)] * (len(args) - fetched)
    moved = sum(a.size * a.dtype.itemsize for a in args) if flops else 0
    moved += sum(math.prod(o.shape) * o.dtype.itemsize for o in outs) if flops else 0
    return pl.pallas_call(
        kernel,
        out_shape=outs,
        in_specs=in_specs,
        out_specs=[pl.BlockSpec(memory_space=pltpu.VMEM)] * len(outs),
        scratch_shapes=scratch,
        compiler_params=pltpu.CompilerParams(vmem_limit_bytes=vmem * MIB),
        cost_estimate=pl.CostEstimate(flops=flops, bytes_accessed=moved, transcendentals=0),
    )(pos, *args)


def block_at(pos, s, d, rows):
    block = jnp.bitwise_xor(pos[1], s) * PLANE + jnp.bitwise_xor(pos[2], d)
    return pl.multiple_of(block * rows, rows)


def fetch(pairs, sems):
    copies = [pltpu.make_async_copy(src, dst, sems.at[i]) for i, (src, dst) in enumerate(pairs)]
    for copy in copies:
        copy.start()
    return copies


def start_kernel(pos, taps, out_weight, own, whole, near, out_half, taps_here, sems):
    rows, wide = own.shape
    deep, width = out_half.shape
    quarter = rows // 4
    side = pl.ds(pl.multiple_of(pos[0] * width, width), width)
    cuts = [pl.ds(q * quarter, quarter) for q in range(4)]
    pairs = [(taps.at[cut], taps_here.at[cut]) for cut in cuts]
    pairs.append((out_weight.at[:, side], out_half))
    for copy in fetch(pairs, sems):
        copy.wait()

    def columns(s):
        return pl.ds(pl.multiple_of(jnp.bitwise_xor(pos[1], s) * wide, wide), wide)

    own[...] = taps_here[:, columns(0)]
    whole[...] = taps_here[:, columns(2 + pos[0])]
    near[:deep, :] = out_half[...]
    for q in range(2):
        first = pl.multiple_of(pos[0] * (rows // 2) + q * quarter, quarter)
        near[deep:, q * wide : (q + 1) * wide] = taps_here[pl.ds(first, quarter), columns(1)]


def split_kernel(share, pos, weight, *refs):
    outs, (weight_here, sems) = refs[-PLANE - 2 : -2], refs[-2:]
    quarter = weight.shape[0] // 4
    cuts = [pl.ds(q * quarter, quarter) for q in range(4)]
    for copy in fetch([(weight.at[cut], weight_here.at[cut]) for cut in cuts], sems):
        copy.wait()
    for d, out in enumerate(outs):
        place = jnp.bitwise_xor(pos[2], d)
        for p in range(out.shape[1] // share):
            at = pl.multiple_of((p * PLANE + place) * share, share)
            out[:, p * share : (p + 1) * share] = weight_here[:, pl.ds(at, share)]


def gate_kernel(share, pos, gate, own, beside, across, sems):
    rows, wide = own.shape
    pairs = []
    for d, (out, first) in enumerate(((own, 0), (beside, 0), (across, 0), (across, rows))):
        place = jnp.bitwise_xor(pos[2], d)
        for p in range(wide // share):
            at = pl.multiple_of((p * PLANE + place) * share, share)
            here = out.at[pl.ds(first, rows), pl.ds(p * share, share)]
            pairs.append((gate.at[:, pl.ds(at, share)], here))
    for copy in fetch(pairs, sems):
        copy.wait()


def join(out, parts):
    at = 0
    for part in parts:
        out[at : at + part.shape[0], :] = part[...]
        at += part.shape[0]


def half_kernel(pos, *refs):
    parts, out = refs[:PLANE], refs[PLANE]
    for y in range(2):

        @pl.when(pos[0] == y)
        def _():
            join(out, parts[2 * y : 2 * y + 2])


def trade_kernel(pos, whole, near, joined, beside):
    rows, wide = whole.shape
    quarter = rows // 4
    joined[:rows, :] = whole[...]
    for q in range(2):
        here = slice(rows + q * quarter, rows + (q + 1) * quarter)
        joined[here, :] = near[near.shape[0] - quarter :, q * wide : (q + 1) * wide]
    beside[...] = near[: beside.shape[0], :]


def join_kernel(pos, *refs):
    join(refs[-1], refs[:-1])


def places_kernel(pos, own, mine, other, gate, *outs):
    planes, rows, share = outs[0].shape
    part = rows // 2
    for d, out in enumerate(outs):
        columns = pl.ds(pl.multiple_of(jnp.bitwise_xor(pos[2], d) * share, share), share)
        out[0] = own[:, columns]
        for side, block in ((pos[0], mine), (1 - pos[0], other)):
            out[2 + side] = block[:rows, columns]
            out[1, pl.ds(pl.multiple_of(side * part, part), part), :] = block[rows:, columns]
    for p in range(planes):
        outs[1][planes + p] = gate[:, p * share : (p + 1) * share]


def project_kernel(planes, pos, x, core, from_x, both, own, *refs):
    halves, outs = refs[:5], refs[5:-3]
    xs, ws, ps = refs[-3:]
    rows = x.shape[0]
    deep = own.shape[0] // PLANE
    share = outs[0].shape[1]
    join(xs, (x, core, from_x, both))
    for d in range(PLANE):
        ws[pl.ds(block_at(pos, 0, d, deep), deep), :] = own[d * deep : (d + 1) * deep, :]
    for half, k, first in zip(halves, (0, 0, 0, 1, 1), (1, 2, 3, 1, 3)):
        side = pos[0] if k == 0 else 1 - pos[0]
        for j in range(half.shape[0] // deep):
            at = block_at(pos, first + j // 2, 2 * side + j % 2, deep)
            ws[pl.ds(at, deep), :] = half[j * deep : (j + 1) * deep, :]
    ps[...] = dot(xs[...], ws[...]).astype(ps.dtype)
    for s in range(planes):
        at = pl.multiple_of(jnp.bitwise_xor(pos[1], s) * share, share)
        outs[s][...] = ps[:, pl.ds(at, share)]


def forward_stage(signal, first, work, blocks, rows):
    share = signal.shape[1]
    for pair in range(rows // (2 * ROWS)):
        halves = []
        for h in range(2):
            at = (2 * pair + h) * ROWS
            halves.append(
                jnp.concatenate(
                    [signal[b * rows + at : b * rows + at + ROWS, :] for b in range(blocks)], 0
                )
            )
        got = dot(first[...], jnp.concatenate(halves, 1)).astype(jnp.bfloat16)
        for h in range(2):
            at = (2 * pair + h) * ROWS
            for f in range(2 * blocks):
                work[f, at : at + ROWS, :] = got[
                    f * ROWS : (f + 1) * ROWS, h * share : (h + 1) * share
                ]


def spectrum_at(f, work, turned, blocks, rows):
    if f == 0 or f == blocks:
        return dot(turned[f, :, :rows], work[0 if f == 0 else 1])
    both = jnp.concatenate([work[2 * f], work[2 * f + 1]], 0)
    return dot(turned[f], both)


def taps_kernel(blocks, planes, pos, *refs):
    parts = refs[:PLANE]
    first, turned, out, signal, work = refs[PLANE:]
    rows = signal.shape[0] // blocks
    for d in range(PLANE):
        for s in range(planes):
            signal[pl.ds(block_at(pos, s, d, rows), rows), :] = parts[d][s]
    forward_stage(signal, first, work, blocks, rows)
    for f in range(blocks + 1):
        out[f] = spectrum_at(f, work, turned, blocks, rows).astype(out.dtype)


def conv_kernel(blocks, planes, pos, *refs):
    parts = refs[:planes]
    taps, skip, response, first, last, turned, back = refs[planes : planes + 7]
    outs = refs[planes + 7 : 3 * planes + 7]
    wide, value, work, result = refs[3 * planes + 7 :]
    rows = value.shape[0] // blocks
    share = value.shape[1]
    lead = wide.shape[0] - value.shape[0]
    own = pos[1] * PLANE + pos[2]
    columns = pl.ds(pl.multiple_of(own * share, share), share)
    taps, skip = taps[:, columns], skip[:, columns]
    wide[:lead, :] = jnp.zeros((lead, share), jnp.float32)
    for s in range(planes):
        for d in range(PLANE):
            at = block_at(pos, s, d, rows)
            wide[pl.ds(pl.multiple_of(lead + at, 8), rows), :] = parts[s][
                d * rows : (d + 1) * rows, :
            ].astype(jnp.float32)
    for b in range(blocks):
        at = lead + b * rows
        value[b * rows : (b + 1) * rows, :] = (
            taps[0:1, :] * wide[at : at + rows, :]
            + taps[1:2, :] * wide[at - 1 : at - 1 + rows, :]
            + taps[2:3, :] * wide[at - 2 : at - 2 + rows, :]
        ).astype(value.dtype)
    forward_stage(value, first, work, blocks, rows)
    for f in range(blocks + 1):
        got = spectrum_at(f, work, turned, blocks, rows)
        re, im = got[:rows], got[rows:]
        response_re = response[f, :rows, :].astype(jnp.float32)
        response_im = response[f, rows:, :].astype(jnp.float32)
        product = jnp.concatenate(
            [re * response_re - im * response_im, re * response_im + im * response_re], 0
        ).astype(jnp.bfloat16)
        if f == 0 or f == blocks:
            work[0 if f == 0 else 1] = dot(back[f, :rows, :], product).astype(work.dtype)
        else:
            inverse = dot(back[f], product).astype(work.dtype)
            work[2 * f] = inverse[:rows]
            work[2 * f + 1] = inverse[rows:]
    for pair in range(rows // (2 * ROWS)):
        halves = []
        for h in range(2):
            at = (2 * pair + h) * ROWS
            halves.append(
                jnp.concatenate([work[f, at : at + ROWS, :] for f in range(2 * blocks)], 0)
            )
        got = dot(last[...], jnp.concatenate(halves, 1))
        for h in range(2):
            at = (2 * pair + h) * ROWS
            for b in range(blocks):
                here = slice(b * rows + at, b * rows + at + ROWS)
                conv = got[b * ROWS : (b + 1) * ROWS, h * share : (h + 1) * share]
                result[here, :] = (
                    conv + skip * value[here, :].astype(jnp.float32)
                ).astype(result.dtype)
    for s in range(planes):
        for d in range(PLANE):
            half, at = d // 2, d % 2 * rows
            outs[half * planes + s][at : at + rows, :] = result[
                pl.ds(block_at(pos, s, d, rows), rows), :
            ]


def mixed_dots(planes, pos, u, gate, ws, mixed, outs):
    share = u[0].shape[1]
    rows = u[0].shape[0] // 2
    for s in range(planes):
        plane = jnp.bitwise_xor(pos[1], s)
        for d in range(2):
            if len(gate[d].shape) == 3:
                columns = gate[d][planes + plane]
            else:
                columns = gate[d][:rows, pl.ds(pl.multiple_of(plane * share, share), share)]
            mixed[d * rows : (d + 1) * rows, s * share : (s + 1) * share] = (
                columns.astype(jnp.float32)
                * u[s][d * rows : (d + 1) * rows, :].astype(jnp.float32)
            ).astype(mixed.dtype)
    got = dot(mixed[...], ws[...])
    outs[0][...] = got[:rows].astype(outs[0].dtype)
    width = outs[1].shape[1]
    for i, out in enumerate(outs[1:]):
        out[...] = got[rows:, i * width : (i + 1) * width].astype(out.dtype)


def upper_kernel(planes, pos, *refs):
    u, gate = refs[:planes], refs[planes : planes + 2]
    own, halves = refs[planes + 2], refs[planes + 3 : planes + 7]
    outs, ws, mixed = refs[planes + 7 : -2], refs[-2], refs[-1]
    share = u[0].shape[1]
    width = halves[0].shape[1]
    ws[:share, :] = own[...]
    for k in range(2):
        side = pos[0] if k == 0 else 1 - pos[0]
        columns = pl.ds(pl.multiple_of(side * width, width), width)
        ws[share : 2 * share, columns] = halves[2 * k][...]
        ws[2 * share :, columns] = halves[2 * k + 1][...]
    mixed_dots(planes, pos, u, gate, ws, mixed, outs)


def lower_kernel(planes, pos, *refs):
    u, gate, ws = refs[:planes], refs[planes : planes + 2], refs[planes + 2]
    mixed_dots(planes, pos, u, gate, ws, refs[-1], refs[planes + 3 : -1])


def local(inputs, gate_in, value_weight, short_taps, filter_taps, skip_scale, output_weight):
    rows, features = inputs.shape
    deep, channels = value_weight.shape
    devices = lax.axis_size("seq")
    planes = devices // PLANE
    share = channels // devices
    wide = planes * share
    blocks = devices
    index = lax.axis_index("seq")
    y = lax.axis_index("groups")
    z, place = index // PLANE, index % PLANE
    pos = jnp.stack([y, z, place]).astype(jnp.int32)

    def to_place(block, d):
        return lax.ppermute(block, "seq", [(i, i ^ d) for i in range(devices)])

    def to_plane(block, s):
        return lax.ppermute(block, "seq", [(i, i ^ (s * PLANE)) for i in range(devices)])

    def to_group(block):
        return lax.ppermute(block, "groups", [(0, 1), (1, 0)])

    def shaped(*shape, dtype=jnp.bfloat16):
        return jax.ShapeDtypeStruct(shape, dtype)

    def small(kernel, outs, *args, copies=0, fetched=0, vmem=2, flops=0):
        scratch = [pltpu.SemaphoreType.DMA((copies,))] if copies else []
        return list(call(kernel, outs, scratch, pos, args, flops, vmem=vmem, fetched=fetched))

    stage = lax.optimization_barrier
    first, last, turned, back = (
        jnp.asarray(t) for t in (*stage_tables(blocks), *turned_tables(blocks, rows))
    )
    part, width, positions = rows // 2, features // 2, blocks * rows

    taps_own, taps_whole, out_near, out_half = call(
        start_kernel,
        [shaped(rows, wide), shaped(rows, wide)]
        + [shaped(deep + rows // 4, width), shaped(deep, width)],
        [pltpu.VMEM((rows, channels), jnp.bfloat16), pltpu.SemaphoreType.DMA((5,))],
        pos,
        [filter_taps, output_weight],
        0,
        vmem=53,
        fetched=2,
    )
    cut = call(
        functools.partial(split_kernel, share),
        [shaped(deep, wide)] * PLANE,
        [pltpu.VMEM((deep, channels), jnp.bfloat16), pltpu.SemaphoreType.DMA((4,))],
        pos,
        [value_weight],
        0,
        vmem=53,
        fetched=1,
    )
    cut = list(cut)
    out_near = to_plane(out_near, 1)
    gate_own, gate_beside, gate_x = small(
        functools.partial(gate_kernel, share),
        [shaped(rows, wide), shaped(rows, wide), shaped(2 * rows, wide)],
        gate_in,
        copies=4 * planes,
        fetched=1,
    )
    core = to_place(inputs, 1)
    own = small(join_kernel, [shaped(deep, wide)], cut[0])
    cut = own + [to_place(cut[d], d) for d in range(1, PLANE)]
    route = [
        (y0 * devices + i, y0 * devices + (i ^ (2 + y0) * PLANE))
        for y0 in range(2)
        for i in range(devices)
    ]
    taps_whole = lax.ppermute(taps_whole, ("groups", "seq"), route)
    sent = small(half_kernel, [shaped(2 * deep, wide)], *cut, flops=1)[0]
    cut, taps_whole, late, core, out_near, sent, gate_own, gate_beside, gate_x = stage(
        (cut, taps_whole, inputs, core, out_near, sent, gate_own, gate_beside, gate_x)
    )

    taps_mine, out_near = small(
        trade_kernel,
        [shaped(rows * 3 // 2, wide), shaped(deep, width)],
        taps_whole,
        out_near,
    )
    near, far = to_plane(sent, 1), to_plane(sent, 2)
    from_x = to_place(late, 2)
    taps_other, out_other = to_group(taps_mine), to_group(out_near)
    near, far, taps_other, out_half, out_other = stage(
        (near, far, taps_other, out_half, out_other)
    )

    passed = to_plane(far, 1)
    other = small(
        join_kernel, [shaped(4 * deep, wide)], to_group(near), to_group(far), flops=1 << 30
    )[0]
    out_far = to_plane(out_half, 2)
    both = to_place(from_x, 1)
    taps_parts = small(
        places_kernel,
        [shaped(planes * (2 if d == 1 else 1), rows, share) for d in range(PLANE)],
        taps_own,
        taps_mine,
        taps_other,
        gate_beside,
        flops=1 << 30,
    )
    other, passed, both = stage((other, passed, both))
    passed_other = to_group(passed)
    taps_parts = [taps_parts[0]] + [to_place(taps_parts[d], d) for d in range(1, PLANE)]
    held = small(join_kernel, [shaped(PLANE * deep, wide)], *cut)[0]
    weights = small(join_kernel, [shaped(2 * deep, width)], out_far, to_plane(out_far, 1))[0]
    passed, other, both, taps_parts, passed_other, held = stage(
        (passed, other, both, taps_parts, passed_other, held)
    )
    projected = call(
        functools.partial(project_kernel, planes),
        [shaped(PLANE * rows, share)] * planes,
        [
            pltpu.VMEM((PLANE * rows, features), jnp.bfloat16),
            pltpu.VMEM((features, wide), jnp.bfloat16),
            pltpu.VMEM((PLANE * rows, wide), jnp.bfloat16),
        ],
        pos,
        [inputs, core, from_x, both, held, near, far, passed, other, passed_other],
        2 * PLANE * rows * features * wide,
        vmem=8,
    )
    projected, weights, gate_x = stage((projected, weights, gate_x))

    def spread(parts):
        sent = [to_plane(parts[s], s) for s in reversed(range(1, planes))]
        return [parts[0]] + sent[::-1]

    signal = spread(projected)
    weights_other = to_group(weights)
    gate_x = to_place(gate_x, 2)
    response = call(
        functools.partial(taps_kernel, blocks, planes),
        [shaped(blocks + 1, 2 * rows, share)],
        [
            pltpu.VMEM((positions, share), jnp.bfloat16),
            pltpu.VMEM((2 * blocks, rows, share), jnp.bfloat16),
        ],
        pos,
        [*taps_parts, first, turned],
        2 * positions * share * (32 * ROWS + 4 * rows),
        vmem=4,
    )[0]
    signal, response = stage((signal[::-1], response))
    signal = signal[::-1]

    mixed = call(
        functools.partial(conv_kernel, blocks, planes),
        [shaped(2 * rows, share)] * (2 * planes),
        [
            pltpu.VMEM((positions + 8, share), jnp.float32),
            pltpu.VMEM((positions, share), jnp.bfloat16),
            pltpu.VMEM((2 * blocks, rows, share), jnp.bfloat16),
            pltpu.VMEM((positions, share), jnp.bfloat16),
        ],
        pos,
        [*signal, short_taps, skip_scale[None], response, first, last, turned, back],
        16 * positions * share * (32 * ROWS + 4 * rows),
        vmem=8,
    )
    mixed, weights_other, gate_x = stage((mixed, weights_other, gate_x))

    upper = spread(mixed[planes:])
    gate_three = to_place(gate_x[rows:], 1)
    upper, lower, gate_three = stage((upper[::-1], mixed[:planes], gate_three))
    upper = upper[::-1]
    scratch = [pltpu.VMEM((2 * rows, wide), jnp.bfloat16)]
    flops = 4 * rows * features * wide
    partial_two, partial_three, gathered = call(
        functools.partial(upper_kernel, planes),
        [shaped(rows, features, dtype=jnp.float32), shaped(rows, features)]
        + [shaped(wide, features)],
        scratch,
        pos,
        [*upper, gate_x, gate_three, output_weight]
        + [out_near, weights, out_other, weights_other],
        flops,
        vmem=8,
    )
    across = partial_two + to_place(partial_three, 1).astype(jnp.float32)
    across, lower = stage((across.astype(jnp.bfloat16), lower))

    across = to_place(across, 2)
    lower = spread(lower)
    partial_zero, *partial_one = call(
        functools.partial(lower_kernel, planes),
        [shaped(rows, features, dtype=jnp.float32)] + [shaped(rows, features // 4)] * 4,
        scratch,
        pos,
        [*lower, gate_own, taps_parts[1], gathered],
        0,
        vmem=8,
    )
    partial_one = jnp.concatenate([to_place(block, 1) for block in partial_one], 1)
    result = partial_zero + partial_one.astype(jnp.float32) + across.astype(jnp.float32)
    return result.astype(jnp.bfloat16)


def passed_along(block, axis, distance):
    devices = range(lax.axis_size(axis))
    route = [(i - distance, i) for i in devices if i - distance in devices]
    return lax.ppermute(block, axis, route)


def local_narrow(inputs, gate_in, value_weight, short_taps, filter_taps, skip_scale, output_weight):
    rows, features = inputs.shape
    channels = value_weight.shape[1]
    blocks = lax.axis_size("seq")
    share = channels // blocks
    index = lax.axis_index("seq")
    projected = dot(inputs, lax.all_gather(value_weight, "seq", axis=0, tiled=True)).astype(
        jnp.bfloat16
    )
    earlier = passed_along(projected[rows - 2 :], "seq", 1)
    extended = jnp.concatenate([earlier, projected], 0).astype(jnp.float32)
    value = (
        short_taps[0] * extended[2:]
        + short_taps[1] * extended[1:-1]
        + short_taps[2] * extended[:-2]
    ).astype(jnp.bfloat16)

    def by_channel(signal):
        cut = signal.reshape(rows, blocks, share)
        got = lax.all_to_all(cut, "seq", split_axis=1, concat_axis=0, tiled=True)
        return got.reshape(blocks, rows, share)

    grid = np.arange(2 * blocks)
    angle = 2.0 * np.pi * (grid[:, None] * grid[None, :] % (2 * blocks)) / (2 * blocks)
    wide = np.exp(-1j * angle)[: blocks + 1, :blocks]
    turned, back = (jnp.asarray(t) for t in turned_tables(blocks, rows))
    weight = np.full((blocks + 1, 1), 2.0)
    weight[0] = weight[-1] = 1.0
    narrow = weight * np.conj(wide) / (2 * blocks * rows)

    def einsum(form, table, data):
        return jnp.einsum(form, table, data, preferred_element_type=jnp.float32)

    def table(values):
        return jnp.asarray(values.astype(ml_dtypes.bfloat16))

    def forward(signal):
        re = einsum("fb,bmc->fmc", table(np.real(wide)), signal)
        im = einsum("fb,bmc->fmc", table(np.imag(wide)), signal)
        both = jnp.concatenate([re, im], 1).astype(jnp.bfloat16)
        return einsum("fkm,fmc->fkc", turned, both)

    response = forward(by_channel(filter_taps))
    got = forward(by_channel(value))
    re, im = got[:, :rows], got[:, rows:]
    response_re, response_im = response[:, :rows], response[:, rows:]
    product = jnp.concatenate(
        [re * response_re - im * response_im, re * response_im + im * response_re], 1
    ).astype(jnp.bfloat16)
    inverse = einsum("fmk,fkc->fmc", back, product).astype(jnp.bfloat16)
    conv = einsum("fb,fmc->bmc", table(np.real(narrow)), inverse[:, :rows]) - einsum(
        "fb,fmc->bmc", table(np.imag(narrow)), inverse[:, rows:]
    )
    conv = lax.all_to_all(
        conv.astype(jnp.bfloat16), "seq", split_axis=0, concat_axis=2, tiled=True
    ).reshape(rows, channels)
    mixed = (
        gate_in.astype(jnp.float32)
        * (conv.astype(jnp.float32) + skip_scale * value.astype(jnp.float32))
    ).astype(jnp.bfloat16)
    result = dot(mixed, lax.all_gather(output_weight, "seq", axis=0, tiled=True))
    return result.astype(jnp.bfloat16)


def solution(mesh):
    split = P(("groups", "seq"), None)
    placed = (split, split, P("seq", None), P(), P("seq", None), P(), P("seq", None))

    def run(*args):
        devices = mesh.shape["seq"]
        share = args[2].shape[1] // devices
        tiled = share % LANES == 0 and args[0].shape[0] // mesh.size == LANES
        paired = devices == 4 * PLANE and mesh.shape["groups"] == 2
        body = local if tiled and paired else local_narrow
        return jax.shard_map(body, mesh=mesh, in_specs=placed, out_specs=split, check_vma=False)(
            *args
        )

    return run
```

```python
import functools
import math

import jax
import jax.numpy as jnp
import ml_dtypes
import numpy as np
from jax import lax
from jax.experimental import pallas as pl
from jax.experimental.pallas import tpu as pltpu
from jax.sharding import PartitionSpec as P

PLANE = 4
LANES = 128
ROWS = 16
MIB = 1 << 20


def stage_tables(blocks):
    width = 2 * blocks
    b = np.arange(blocks)
    forward = [np.ones(blocks), np.cos(np.pi * b)]
    backward = [np.ones(blocks), np.cos(np.pi * b)]
    for f in range(1, blocks):
        angle = 2.0 * np.pi * (f * b % width) / width
        forward += [np.cos(angle), -np.sin(angle)]
        backward += [2.0 * np.cos(angle), -2.0 * np.sin(angle)]
    eye = np.eye(ROWS)
    first = np.kron(np.stack(forward, 0), eye)
    last = np.kron(np.stack(backward, 1), eye) / (width * LANES)
    return first.astype(ml_dtypes.bfloat16), last.astype(ml_dtypes.bfloat16)


def turned_tables(blocks, rows):
    width = 2 * blocks
    k = np.arange(rows)[:, None]
    m = np.arange(rows)[None, :]
    out = []
    for f in range(blocks + 1):
        angle = 2.0 * np.pi * ((width * k + f) * m % (width * rows)) / (width * rows)
        cos, sin = np.cos(angle), np.sin(angle)
        out.append(np.block([[cos, sin], [-sin, cos]]))
    forward = np.stack(out, 0)
    return (
        forward.astype(ml_dtypes.bfloat16),
        np.swapaxes(forward, 1, 2).astype(ml_dtypes.bfloat16),
    )


def dot(left, right):
    return jnp.dot(left, right, preferred_element_type=jnp.float32)


def call(kernel, outs, scratch, pos, args, flops, vmem=4, fetched=0):
    in_specs = [pl.BlockSpec(memory_space=pltpu.SMEM)]
    in_specs += [pl.BlockSpec(memory_space=pltpu.HBM)] * fetched
    in_specs += [pl.BlockSpec(memory_space=pltpu.VMEM)] * (len(args) - fetched)
    moved = sum(a.size * a.dtype.itemsize for a in args) if flops else 0
    moved += sum(math.prod(o.shape) * o.dtype.itemsize for o in outs) if flops else 0
    return pl.pallas_call(
        kernel,
        out_shape=outs,
        in_specs=in_specs,
        out_specs=[pl.BlockSpec(memory_space=pltpu.VMEM)] * len(outs),
        scratch_shapes=scratch,
        compiler_params=pltpu.CompilerParams(vmem_limit_bytes=vmem * MIB),
        cost_estimate=pl.CostEstimate(flops=flops, bytes_accessed=moved, transcendentals=0),
    )(pos, *args)


def block_at(pos, s, d, rows):
    block = jnp.bitwise_xor(pos[1], s) * PLANE + jnp.bitwise_xor(pos[2], d)
    return pl.multiple_of(block * rows, rows)


def fetch(pairs, sems):
    copies = [pltpu.make_async_copy(src, dst, sems.at[i]) for i, (src, dst) in enumerate(pairs)]
    for copy in copies:
        copy.start()
    return copies


def start_kernel(pos, taps, out_weight, own, whole, near, out_half, taps_here, sems):
    rows, wide = own.shape
    deep, width = out_half.shape
    quarter = rows // 4
    side = pl.ds(pl.multiple_of(pos[0] * width, width), width)
    cuts = [pl.ds(q * quarter, quarter) for q in range(4)]
    pairs = [(taps.at[cut], taps_here.at[cut]) for cut in cuts]
    pairs.append((out_weight.at[:, side], out_half))
    for copy in fetch(pairs, sems):
        copy.wait()

    def columns(s):
        return pl.ds(pl.multiple_of(jnp.bitwise_xor(pos[1], s) * wide, wide), wide)

    own[...] = taps_here[:, columns(0)]
    whole[...] = taps_here[:, columns(2 + pos[0])]
    near[:deep, :] = out_half[...]
    for q in range(2):
        first = pl.multiple_of(pos[0] * (rows // 2) + q * quarter, quarter)
        near[deep:, q * wide : (q + 1) * wide] = taps_here[pl.ds(first, quarter), columns(1)]


def split_kernel(share, pos, weight, *refs):
    outs, (weight_here, sems) = refs[-PLANE - 2 : -2], refs[-2:]
    quarter = weight.shape[0] // 4
    cuts = [pl.ds(q * quarter, quarter) for q in range(4)]
    for copy in fetch([(weight.at[cut], weight_here.at[cut]) for cut in cuts], sems):
        copy.wait()
    for d, out in enumerate(outs):
        place = jnp.bitwise_xor(pos[2], d)
        for p in range(out.shape[1] // share):
            at = pl.multiple_of((p * PLANE + place) * share, share)
            out[:, p * share : (p + 1) * share] = weight_here[:, pl.ds(at, share)]


def gate_kernel(share, pos, gate, own, beside, across, sems):
    rows, wide = own.shape
    pairs = []
    for d, (out, first) in enumerate(((own, 0), (beside, 0), (across, 0), (across, rows))):
        place = jnp.bitwise_xor(pos[2], d)
        for p in range(wide // share):
            at = pl.multiple_of((p * PLANE + place) * share, share)
            here = out.at[pl.ds(first, rows), pl.ds(p * share, share)]
            pairs.append((gate.at[:, pl.ds(at, share)], here))
    for copy in fetch(pairs, sems):
        copy.wait()


def join(out, parts):
    at = 0
    for part in parts:
        out[at : at + part.shape[0], :] = part[...]
        at += part.shape[0]


def half_kernel(pos, *refs):
    parts, out = refs[:PLANE], refs[PLANE]
    for y in range(2):

        @pl.when(pos[0] == y)
        def _():
            join(out, parts[2 * y : 2 * y + 2])


def trade_kernel(pos, whole, near, joined, beside):
    rows, wide = whole.shape
    quarter = rows // 4
    joined[:rows, :] = whole[...]
    for q in range(2):
        here = slice(rows + q * quarter, rows + (q + 1) * quarter)
        joined[here, :] = near[near.shape[0] - quarter :, q * wide : (q + 1) * wide]
    beside[...] = near[: beside.shape[0], :]


def join_kernel(pos, *refs):
    join(refs[-1], refs[:-1])


def places_kernel(pos, own, mine, other, gate, *outs):
    planes, rows, share = outs[0].shape
    part = rows // 2
    for d, out in enumerate(outs):
        columns = pl.ds(pl.multiple_of(jnp.bitwise_xor(pos[2], d) * share, share), share)
        out[0] = own[:, columns]
        for side, block in ((pos[0], mine), (1 - pos[0], other)):
            out[2 + side] = block[:rows, columns]
            out[1, pl.ds(pl.multiple_of(side * part, part), part), :] = block[rows:, columns]
    for p in range(planes):
        outs[1][planes + p] = gate[:, p * share : (p + 1) * share]


def project_kernel(planes, pos, x, core, from_x, both, own, *refs):
    halves, outs = refs[:5], refs[5:-3]
    xs, ws, ps = refs[-3:]
    rows = x.shape[0]
    deep = own.shape[0] // PLANE
    share = outs[0].shape[1]
    join(xs, (x, core, from_x, both))
    for d in range(PLANE):
        ws[pl.ds(block_at(pos, 0, d, deep), deep), :] = own[d * deep : (d + 1) * deep, :]
    for half, k, first in zip(halves, (0, 0, 0, 1, 1), (1, 2, 3, 1, 3)):
        side = pos[0] if k == 0 else 1 - pos[0]
        for j in range(half.shape[0] // deep):
            at = block_at(pos, first + j // 2, 2 * side + j % 2, deep)
            ws[pl.ds(at, deep), :] = half[j * deep : (j + 1) * deep, :]
    ps[...] = dot(xs[...], ws[...]).astype(ps.dtype)
    for s in range(planes):
        at = pl.multiple_of(jnp.bitwise_xor(pos[1], s) * share, share)
        outs[s][...] = ps[:, pl.ds(at, share)]


def forward_stage(signal, first, work, blocks, rows):
    share = signal.shape[1]
    for pair in range(rows // (2 * ROWS)):
        halves = []
        for h in range(2):
            at = (2 * pair + h) * ROWS
            halves.append(
                jnp.concatenate(
                    [signal[b * rows + at : b * rows + at + ROWS, :] for b in range(blocks)], 0
                )
            )
        got = dot(first[...], jnp.concatenate(halves, 1)).astype(jnp.bfloat16)
        for h in range(2):
            at = (2 * pair + h) * ROWS
            for f in range(2 * blocks):
                work[f, at : at + ROWS, :] = got[
                    f * ROWS : (f + 1) * ROWS, h * share : (h + 1) * share
                ]


def spectrum_at(f, work, turned, blocks, rows):
    if f == 0 or f == blocks:
        return dot(turned[f, :, :rows], work[0 if f == 0 else 1])
    both = jnp.concatenate([work[2 * f], work[2 * f + 1]], 0)
    return dot(turned[f], both)


def taps_kernel(blocks, planes, pos, *refs):
    parts = refs[:PLANE]
    first, turned, out, signal, work = refs[PLANE:]
    rows = signal.shape[0] // blocks
    for d in range(PLANE):
        for s in range(planes):
            signal[pl.ds(block_at(pos, s, d, rows), rows), :] = parts[d][s]
    forward_stage(signal, first, work, blocks, rows)
    for f in range(blocks + 1):
        out[f] = spectrum_at(f, work, turned, blocks, rows).astype(out.dtype)


def conv_kernel(blocks, planes, pos, *refs):
    parts = refs[:planes]
    taps, skip, response, first, last, turned, back = refs[planes : planes + 7]
    outs = refs[planes + 7 : 3 * planes + 7]
    wide, value, work, result = refs[3 * planes + 7 :]
    rows = value.shape[0] // blocks
    share = value.shape[1]
    lead = wide.shape[0] - value.shape[0]
    own = pos[1] * PLANE + pos[2]
    columns = pl.ds(pl.multiple_of(own * share, share), share)
    taps, skip = taps[:, columns], skip[:, columns]
    wide[:lead, :] = jnp.zeros((lead, share), jnp.float32)
    for s in range(planes):
        for d in range(PLANE):
            at = block_at(pos, s, d, rows)
            wide[pl.ds(pl.multiple_of(lead + at, 8), rows), :] = parts[s][
                d * rows : (d + 1) * rows, :
            ].astype(jnp.float32)
    for b in range(blocks):
        at = lead + b * rows
        value[b * rows : (b + 1) * rows, :] = (
            taps[0:1, :] * wide[at : at + rows, :]
            + taps[1:2, :] * wide[at - 1 : at - 1 + rows, :]
            + taps[2:3, :] * wide[at - 2 : at - 2 + rows, :]
        ).astype(value.dtype)
    forward_stage(value, first, work, blocks, rows)
    for f in range(blocks + 1):
        got = spectrum_at(f, work, turned, blocks, rows)
        re, im = got[:rows], got[rows:]
        response_re = response[f, :rows, :].astype(jnp.float32)
        response_im = response[f, rows:, :].astype(jnp.float32)
        product = jnp.concatenate(
            [re * response_re - im * response_im, re * response_im + im * response_re], 0
        ).astype(jnp.bfloat16)
        if f == 0 or f == blocks:
            work[0 if f == 0 else 1] = dot(back[f, :rows, :], product).astype(work.dtype)
        else:
            inverse = dot(back[f], product).astype(work.dtype)
            work[2 * f] = inverse[:rows]
            work[2 * f + 1] = inverse[rows:]
    for pair in range(rows // (2 * ROWS)):
        halves = []
        for h in range(2):
            at = (2 * pair + h) * ROWS
            halves.append(
                jnp.concatenate([work[f, at : at + ROWS, :] for f in range(2 * blocks)], 0)
            )
        got = dot(last[...], jnp.concatenate(halves, 1))
        for h in range(2):
            at = (2 * pair + h) * ROWS
            for b in range(blocks):
                here = slice(b * rows + at, b * rows + at + ROWS)
                conv = got[b * ROWS : (b + 1) * ROWS, h * share : (h + 1) * share]
                result[here, :] = (
                    conv + skip * value[here, :].astype(jnp.float32)
                ).astype(result.dtype)
    for s in range(planes):
        for d in range(PLANE):
            half, at = d // 2, d % 2 * rows
            outs[half * planes + s][at : at + rows, :] = result[
                pl.ds(block_at(pos, s, d, rows), rows), :
            ]


def mixed_dot(planes, pos, u, gate, ws, mixed, outs, half):
    rows, share = mixed.shape[0], u[0].shape[1]
    for s in range(planes):
        plane = jnp.bitwise_xor(pos[1], s)
        if len(gate.shape) == 3:
            columns = gate[planes + plane]
        else:
            columns = gate[:rows, pl.ds(pl.multiple_of(plane * share, share), share)]
        mixed[:, s * share : (s + 1) * share] = (
            columns.astype(jnp.float32)
            * u[s][half * rows : (half + 1) * rows, :].astype(jnp.float32)
        ).astype(mixed.dtype)
    got = dot(mixed[...], ws[...])
    width = outs[0].shape[1]
    for i, out in enumerate(outs):
        out[...] = got[:, i * width : (i + 1) * width].astype(out.dtype)


def upper_kernel(planes, pos, *refs):
    u, gate = refs[:planes], refs[planes]
    own, halves = refs[planes + 1], refs[planes + 2 : planes + 6]
    out, ws, mixed = refs[planes + 6 :]
    share = u[0].shape[1]
    width = halves[0].shape[1]
    ws[:share, :] = own[...]
    for k in range(2):
        side = pos[0] if k == 0 else 1 - pos[0]
        columns = pl.ds(pl.multiple_of(side * width, width), width)
        near, far = halves[2 * k : 2 * k + 2]
        ws[share : 2 * share, columns] = near[:share, :]
        ws[2 * share :, columns] = far[...]
    mixed_dot(planes, pos, u, gate, ws, mixed, (out,), 1)


def place_kernel(planes, half, pos, *refs):
    u, gate, ws = refs[:planes], refs[planes], refs[planes + 1]
    mixed_dot(planes, pos, u, gate, ws, refs[-1], refs[planes + 2 : -1], half)


def local(inputs, gate_in, value_weight, short_taps, filter_taps, skip_scale, output_weight):
    rows, features = inputs.shape
    deep, channels = value_weight.shape
    devices = lax.axis_size("seq")
    planes = devices // PLANE
    share = channels // devices
    wide = planes * share
    blocks = devices
    index = lax.axis_index("seq")
    y = lax.axis_index("groups")
    z, place = index // PLANE, index % PLANE
    pos = jnp.stack([y, z, place]).astype(jnp.int32)

    def to_place(block, d):
        return lax.ppermute(block, "seq", [(i, i ^ d) for i in range(devices)])

    def to_plane(block, s):
        return lax.ppermute(block, "seq", [(i, i ^ (s * PLANE)) for i in range(devices)])

    def to_group(block):
        return lax.ppermute(block, "groups", [(0, 1), (1, 0)])

    def shaped(*shape, dtype=jnp.bfloat16):
        return jax.ShapeDtypeStruct(shape, dtype)

    def small(kernel, outs, *args, copies=0, fetched=0, vmem=2, flops=0):
        scratch = [pltpu.SemaphoreType.DMA((copies,))] if copies else []
        return list(call(kernel, outs, scratch, pos, args, flops, vmem=vmem, fetched=fetched))

    stage = lax.optimization_barrier
    first, last, turned, back = (
        jnp.asarray(t) for t in (*stage_tables(blocks), *turned_tables(blocks, rows))
    )
    part, width, positions = rows // 2, features // 2, blocks * rows

    taps_own, taps_whole, out_near, out_half = call(
        start_kernel,
        [shaped(rows, wide), shaped(rows, wide)]
        + [shaped(deep + rows // 4, width), shaped(deep, width)],
        [pltpu.VMEM((rows, channels), jnp.bfloat16), pltpu.SemaphoreType.DMA((5,))],
        pos,
        [filter_taps, output_weight],
        0,
        vmem=53,
        fetched=2,
    )
    cut = call(
        functools.partial(split_kernel, share),
        [shaped(deep, wide)] * PLANE,
        [pltpu.VMEM((deep, channels), jnp.bfloat16), pltpu.SemaphoreType.DMA((4,))],
        pos,
        [value_weight],
        0,
        vmem=53,
        fetched=1,
    )
    cut = list(cut)
    out_near = to_plane(out_near, 1)
    gate_own, gate_beside, gate_x = small(
        functools.partial(gate_kernel, share),
        [shaped(rows, wide), shaped(rows, wide), shaped(2 * rows, wide)],
        gate_in,
        copies=4 * planes,
        fetched=1,
    )
    core = to_place(inputs, 1)
    own = small(join_kernel, [shaped(deep, wide)], cut[0])
    cut = own + [to_place(cut[d], d) for d in range(1, PLANE)]
    route = [
        (y0 * devices + i, y0 * devices + (i ^ (2 + y0) * PLANE))
        for y0 in range(2)
        for i in range(devices)
    ]
    taps_whole = lax.ppermute(taps_whole, ("groups", "seq"), route)
    sent = small(half_kernel, [shaped(2 * deep, wide)], *cut, flops=1)[0]
    cut, taps_whole, late, core, out_near, sent, gate_own, gate_beside, gate_x = stage(
        (cut, taps_whole, inputs, core, out_near, sent, gate_own, gate_beside, gate_x)
    )

    taps_mine, out_near = small(
        trade_kernel,
        [shaped(rows * 3 // 2, wide), shaped(deep, width)],
        taps_whole,
        out_near,
    )
    near, far = to_plane(sent, 1), to_plane(sent, 2)
    from_x = to_place(late, 2)
    taps_other, out_other = to_group(taps_mine), to_group(out_near)
    near, far, taps_other, out_half, out_other = stage(
        (near, far, taps_other, out_half, out_other)
    )

    passed = to_plane(far, 1)
    other = small(
        join_kernel, [shaped(4 * deep, wide)], to_group(near), to_group(far), flops=1 << 30
    )[0]
    out_far = to_plane(out_half, 2)
    both = to_place(from_x, 1)
    taps_parts = small(
        places_kernel,
        [shaped(planes * (2 if d == 1 else 1), rows, share) for d in range(PLANE)],
        taps_own,
        taps_mine,
        taps_other,
        gate_beside,
        flops=1 << 30,
    )
    other, passed, both = stage((other, passed, both))
    passed_other = to_group(passed)
    taps_parts = [taps_parts[0]] + [to_place(taps_parts[d], d) for d in range(1, PLANE)]
    held = small(join_kernel, [shaped(PLANE * deep, wide)], *cut)[0]
    weights = small(join_kernel, [shaped(2 * deep, width)], out_far, to_plane(out_far, 1))[0]
    passed, other, both, taps_parts, passed_other, held = stage(
        (passed, other, both, taps_parts, passed_other, held)
    )
    projected = call(
        functools.partial(project_kernel, planes),
        [shaped(PLANE * rows, share)] * planes,
        [
            pltpu.VMEM((PLANE * rows, features), jnp.bfloat16),
            pltpu.VMEM((features, wide), jnp.bfloat16),
            pltpu.VMEM((PLANE * rows, wide), jnp.bfloat16),
        ],
        pos,
        [inputs, core, from_x, both, held, near, far, passed, other, passed_other],
        2 * PLANE * rows * features * wide,
        vmem=8,
    )
    projected, weights, gate_x = stage((projected, weights, gate_x))

    def spread(parts):
        sent = [to_plane(parts[s], s) for s in reversed(range(1, planes))]
        return [parts[0]] + sent[::-1]

    signal = spread(projected)
    weights_other = to_group(weights)
    gate_x = to_place(gate_x, 2)
    response = call(
        functools.partial(taps_kernel, blocks, planes),
        [shaped(blocks + 1, 2 * rows, share)],
        [
            pltpu.VMEM((positions, share), jnp.bfloat16),
            pltpu.VMEM((2 * blocks, rows, share), jnp.bfloat16),
        ],
        pos,
        [*taps_parts, first, turned],
        2 * positions * share * (32 * ROWS + 4 * rows),
        vmem=4,
    )[0]
    signal, response = stage((signal[::-1], response))
    signal = signal[::-1]

    mixed = call(
        functools.partial(conv_kernel, blocks, planes),
        [shaped(2 * rows, share)] * (2 * planes),
        [
            pltpu.VMEM((positions + 8, share), jnp.float32),
            pltpu.VMEM((positions, share), jnp.bfloat16),
            pltpu.VMEM((2 * blocks, rows, share), jnp.bfloat16),
            pltpu.VMEM((positions, share), jnp.bfloat16),
        ],
        pos,
        [*signal, short_taps, skip_scale[None], response, first, last, turned, back],
        16 * positions * share * (32 * ROWS + 4 * rows),
        vmem=8,
    )
    mixed, weights_other, gate_x = stage((mixed, weights_other, gate_x))

    upper = spread(mixed[planes:])
    gate_three = to_place(gate_x[rows:], 1)
    upper, lower, gate_three = stage((upper[::-1], mixed[:planes], gate_three))
    upper = upper[::-1]
    scratch = [pltpu.VMEM((rows, wide), jnp.bfloat16)]
    flops = 2 * rows * features * wide
    partial_three, gathered = call(
        functools.partial(upper_kernel, planes),
        [shaped(rows, features), shaped(wide, features)],
        scratch,
        pos,
        [*upper, gate_three, output_weight, out_near, weights, out_other, weights_other],
        flops,
        vmem=8,
    )

    def partial_of(parts, half, gate, cost, pieces, dtype):
        return call(
            functools.partial(place_kernel, planes, half),
            [shaped(rows, features // pieces, dtype=dtype)] * pieces,
            scratch,
            pos,
            [*parts, gate, gathered],
            cost,
            vmem=8,
        )

    partial_two = partial_of(upper, 0, gate_x, flops, 1, jnp.float32)[0]
    across = partial_two + to_place(partial_three, 1).astype(jnp.float32)
    across, lower = stage((across.astype(jnp.bfloat16), lower))

    across = to_place(across, 2)
    lower = spread(lower)
    partial_one = partial_of(lower, 1, taps_parts[1], 0, 4, jnp.bfloat16)
    partial_zero = partial_of(lower, 0, gate_own, 0, 1, jnp.float32)[0]
    partial_one = jnp.concatenate([to_place(block, 1) for block in partial_one], 1)
    result = partial_zero + partial_one.astype(jnp.float32) + across.astype(jnp.float32)
    return result.astype(jnp.bfloat16)


def passed_along(block, axis, distance):
    devices = range(lax.axis_size(axis))
    route = [(i - distance, i) for i in devices if i - distance in devices]
    return lax.ppermute(block, axis, route)


def local_narrow(inputs, gate_in, value_weight, short_taps, filter_taps, skip_scale, output_weight):
    rows, features = inputs.shape
    channels = value_weight.shape[1]
    blocks = lax.axis_size("seq")
    share = channels // blocks
    index = lax.axis_index("seq")
    projected = dot(inputs, lax.all_gather(value_weight, "seq", axis=0, tiled=True)).astype(
        jnp.bfloat16
    )
    earlier = passed_along(projected[rows - 2 :], "seq", 1)
    extended = jnp.concatenate([earlier, projected], 0).astype(jnp.float32)
    value = (
        short_taps[0] * extended[2:]
        + short_taps[1] * extended[1:-1]
        + short_taps[2] * extended[:-2]
    ).astype(jnp.bfloat16)

    def by_channel(signal):
        cut = signal.reshape(rows, blocks, share)
        got = lax.all_to_all(cut, "seq", split_axis=1, concat_axis=0, tiled=True)
        return got.reshape(blocks, rows, share)

    grid = np.arange(2 * blocks)
    angle = 2.0 * np.pi * (grid[:, None] * grid[None, :] % (2 * blocks)) / (2 * blocks)
    wide = np.exp(-1j * angle)[: blocks + 1, :blocks]
    turned, back = (jnp.asarray(t) for t in turned_tables(blocks, rows))
    weight = np.full((blocks + 1, 1), 2.0)
    weight[0] = weight[-1] = 1.0
    narrow = weight * np.conj(wide) / (2 * blocks * rows)

    def einsum(form, table, data):
        return jnp.einsum(form, table, data, preferred_element_type=jnp.float32)

    def table(values):
        return jnp.asarray(values.astype(ml_dtypes.bfloat16))

    def forward(signal):
        re = einsum("fb,bmc->fmc", table(np.real(wide)), signal)
        im = einsum("fb,bmc->fmc", table(np.imag(wide)), signal)
        both = jnp.concatenate([re, im], 1).astype(jnp.bfloat16)
        return einsum("fkm,fmc->fkc", turned, both)

    response = forward(by_channel(filter_taps))
    got = forward(by_channel(value))
    re, im = got[:, :rows], got[:, rows:]
    response_re, response_im = response[:, :rows], response[:, rows:]
    product = jnp.concatenate(
        [re * response_re - im * response_im, re * response_im + im * response_re], 1
    ).astype(jnp.bfloat16)
    inverse = einsum("fmk,fkc->fmc", back, product).astype(jnp.bfloat16)
    conv = einsum("fb,fmc->bmc", table(np.real(narrow)), inverse[:, :rows]) - einsum(
        "fb,fmc->bmc", table(np.imag(narrow)), inverse[:, rows:]
    )
    conv = lax.all_to_all(
        conv.astype(jnp.bfloat16), "seq", split_axis=0, concat_axis=2, tiled=True
    ).reshape(rows, channels)
    mixed = (
        gate_in.astype(jnp.float32)
        * (conv.astype(jnp.float32) + skip_scale * value.astype(jnp.float32))
    ).astype(jnp.bfloat16)
    result = dot(mixed, lax.all_gather(output_weight, "seq", axis=0, tiled=True))
    return result.astype(jnp.bfloat16)


def solution(mesh):
    split = P(("groups", "seq"), None)
    placed = (split, split, P("seq", None), P(), P("seq", None), P(), P("seq", None))

    def run(*args):
        devices = mesh.shape["seq"]
        share = args[2].shape[1] // devices
        tiled = share % LANES == 0 and args[0].shape[0] // mesh.size == LANES
        paired = devices == 4 * PLANE and mesh.shape["groups"] == 2
        body = local if tiled and paired else local_narrow
        return jax.shard_map(body, mesh=mesh, in_specs=placed, out_specs=split, check_vma=False)(
            *args
        )

    return run
```

```python
import functools
import math

import jax
import jax.numpy as jnp
import ml_dtypes
import numpy as np
from jax import lax
from jax.experimental import pallas as pl
from jax.experimental.pallas import tpu as pltpu
from jax.sharding import PartitionSpec as P

PLANE = 4
LANES = 128
ROWS = 16
MIB = 1 << 20


def stage_tables(blocks):
    width = 2 * blocks
    b = np.arange(blocks)
    forward = [np.ones(blocks), np.cos(np.pi * b)]
    backward = [np.ones(blocks), np.cos(np.pi * b)]
    for f in range(1, blocks):
        angle = 2.0 * np.pi * (f * b % width) / width
        forward += [np.cos(angle), -np.sin(angle)]
        backward += [2.0 * np.cos(angle), -2.0 * np.sin(angle)]
    eye = np.eye(ROWS)
    first = np.kron(np.stack(forward, 0), eye)
    last = np.kron(np.stack(backward, 1), eye) / (width * LANES)
    return first.astype(ml_dtypes.bfloat16), last.astype(ml_dtypes.bfloat16)


def turned_tables(blocks, rows):
    width = 2 * blocks
    k = np.arange(rows)[:, None]
    m = np.arange(rows)[None, :]
    out = []
    for f in range(blocks + 1):
        angle = 2.0 * np.pi * ((width * k + f) * m % (width * rows)) / (width * rows)
        cos, sin = np.cos(angle), np.sin(angle)
        out.append(np.block([[cos, sin], [-sin, cos]]))
    forward = np.stack(out, 0)
    return (
        forward.astype(ml_dtypes.bfloat16),
        np.swapaxes(forward, 1, 2).astype(ml_dtypes.bfloat16),
    )


def dot(left, right):
    return jnp.dot(left, right, preferred_element_type=jnp.float32)


def call(kernel, outs, scratch, pos, args, flops, vmem=4, fetched=0):
    in_specs = [pl.BlockSpec(memory_space=pltpu.SMEM)]
    in_specs += [pl.BlockSpec(memory_space=pltpu.HBM)] * fetched
    in_specs += [pl.BlockSpec(memory_space=pltpu.VMEM)] * (len(args) - fetched)
    moved = sum(a.size * a.dtype.itemsize for a in args) if flops else 0
    moved += sum(math.prod(o.shape) * o.dtype.itemsize for o in outs) if flops else 0
    return pl.pallas_call(
        kernel,
        out_shape=outs,
        in_specs=in_specs,
        out_specs=[pl.BlockSpec(memory_space=pltpu.VMEM)] * len(outs),
        scratch_shapes=scratch,
        compiler_params=pltpu.CompilerParams(vmem_limit_bytes=vmem * MIB),
        cost_estimate=pl.CostEstimate(flops=flops, bytes_accessed=moved, transcendentals=0),
    )(pos, *args)


def block_at(pos, s, d, rows):
    block = jnp.bitwise_xor(pos[1], s) * PLANE + jnp.bitwise_xor(pos[2], d)
    return pl.multiple_of(block * rows, rows)


def fetch(pairs, sems):
    copies = [pltpu.make_async_copy(src, dst, sems.at[i]) for i, (src, dst) in enumerate(pairs)]
    for copy in copies:
        copy.start()
    return copies


def start_kernel(pos, taps, out_weight, own, whole, near, out_half, taps_here, sems):
    rows, wide = own.shape
    deep, width = out_half.shape
    quarter = rows // 4
    side = pl.ds(pl.multiple_of(pos[0] * width, width), width)
    cuts = [pl.ds(q * quarter, quarter) for q in range(4)]
    pairs = [(taps.at[cut], taps_here.at[cut]) for cut in cuts]
    pairs.append((out_weight.at[:, side], out_half))
    for copy in fetch(pairs, sems):
        copy.wait()

    def columns(s):
        return pl.ds(pl.multiple_of(jnp.bitwise_xor(pos[1], s) * wide, wide), wide)

    own[...] = taps_here[:, columns(0)]
    whole[...] = taps_here[:, columns(2 + pos[0])]
    near[:deep, :] = out_half[...]
    for q in range(2):
        first = pl.multiple_of(pos[0] * (rows // 2) + q * quarter, quarter)
        near[deep:, q * wide : (q + 1) * wide] = taps_here[pl.ds(first, quarter), columns(1)]


def split_kernel(share, pos, weight, *refs):
    outs, (weight_here, sems) = refs[-PLANE - 2 : -2], refs[-2:]
    quarter = weight.shape[0] // 4
    cuts = [pl.ds(q * quarter, quarter) for q in range(4)]
    for copy in fetch([(weight.at[cut], weight_here.at[cut]) for cut in cuts], sems):
        copy.wait()
    for d, out in enumerate(outs):
        place = jnp.bitwise_xor(pos[2], d)
        for p in range(out.shape[1] // share):
            at = pl.multiple_of((p * PLANE + place) * share, share)
            out[:, p * share : (p + 1) * share] = weight_here[:, pl.ds(at, share)]


def gate_kernel(share, pos, gate, own, beside, across, sems):
    rows, wide = own.shape
    pairs = []
    for d, (out, first) in enumerate(((own, 0), (beside, 0), (across, 0), (across, rows))):
        place = jnp.bitwise_xor(pos[2], d)
        for p in range(wide // share):
            at = pl.multiple_of((p * PLANE + place) * share, share)
            here = out.at[pl.ds(first, rows), pl.ds(p * share, share)]
            pairs.append((gate.at[:, pl.ds(at, share)], here))
    for copy in fetch(pairs, sems):
        copy.wait()


def join(out, parts):
    at = 0
    for part in parts:
        out[at : at + part.shape[0], :] = part[...]
        at += part.shape[0]


def half_kernel(pos, *refs):
    parts, out = refs[:PLANE], refs[PLANE]
    for y in range(2):

        @pl.when(pos[0] == y)
        def _():
            join(out, parts[2 * y : 2 * y + 2])


def trade_kernel(pos, whole, near, joined, beside):
    rows, wide = whole.shape
    quarter = rows // 4
    joined[:rows, :] = whole[...]
    for q in range(2):
        here = slice(rows + q * quarter, rows + (q + 1) * quarter)
        joined[here, :] = near[near.shape[0] - quarter :, q * wide : (q + 1) * wide]
    beside[...] = near[: beside.shape[0], :]


def join_kernel(pos, *refs):
    join(refs[-1], refs[:-1])


def places_kernel(pos, own, mine, other, gate, *outs):
    planes, rows, share = outs[0].shape
    part = rows // 2
    for d, out in enumerate(outs):
        columns = pl.ds(pl.multiple_of(jnp.bitwise_xor(pos[2], d) * share, share), share)
        out[0] = own[:, columns]
        for side, block in ((pos[0], mine), (1 - pos[0], other)):
            out[2 + side] = block[:rows, columns]
            out[1, pl.ds(pl.multiple_of(side * part, part), part), :] = block[rows:, columns]
    for p in range(planes):
        outs[1][planes + p] = gate[:, p * share : (p + 1) * share]


def project_kernel(planes, pos, x, core, from_x, both, own, *refs):
    halves, outs = refs[:5], refs[5:-3]
    xs, ws, ps = refs[-3:]
    rows = x.shape[0]
    deep = own.shape[0] // PLANE
    share = outs[0].shape[1]
    join(xs, (x, core, from_x, both))
    for d in range(PLANE):
        ws[pl.ds(block_at(pos, 0, d, deep), deep), :] = own[d * deep : (d + 1) * deep, :]
    for half, k, first in zip(halves, (0, 0, 0, 1, 1), (1, 2, 3, 1, 3)):
        side = pos[0] if k == 0 else 1 - pos[0]
        for j in range(half.shape[0] // deep):
            at = block_at(pos, first + j // 2, 2 * side + j % 2, deep)
            ws[pl.ds(at, deep), :] = half[j * deep : (j + 1) * deep, :]
    ps[...] = dot(xs[...], ws[...]).astype(ps.dtype)
    for s in range(planes):
        at = pl.multiple_of(jnp.bitwise_xor(pos[1], s) * share, share)
        outs[s][...] = ps[:, pl.ds(at, share)]


def forward_stage(signal, first, work, blocks, rows):
    share = signal.shape[1]
    for pair in range(rows // (2 * ROWS)):
        halves = []
        for h in range(2):
            at = (2 * pair + h) * ROWS
            halves.append(
                jnp.concatenate(
                    [signal[b * rows + at : b * rows + at + ROWS, :] for b in range(blocks)], 0
                )
            )
        got = dot(first[...], jnp.concatenate(halves, 1)).astype(jnp.bfloat16)
        for h in range(2):
            at = (2 * pair + h) * ROWS
            for f in range(2 * blocks):
                work[f, at : at + ROWS, :] = got[
                    f * ROWS : (f + 1) * ROWS, h * share : (h + 1) * share
                ]


def spectrum_at(f, work, turned, blocks, rows):
    if f == 0 or f == blocks:
        return dot(turned[f, :, :rows], work[0 if f == 0 else 1])
    both = jnp.concatenate([work[2 * f], work[2 * f + 1]], 0)
    return dot(turned[f], both)


def taps_kernel(blocks, planes, pos, *refs):
    parts = refs[:PLANE]
    first, turned, out, signal, work = refs[PLANE:]
    rows = signal.shape[0] // blocks
    for d in range(PLANE):
        for s in range(planes):
            signal[pl.ds(block_at(pos, s, d, rows), rows), :] = parts[d][s]
    forward_stage(signal, first, work, blocks, rows)
    for f in range(blocks + 1):
        out[f] = spectrum_at(f, work, turned, blocks, rows).astype(out.dtype)


def conv_kernel(blocks, planes, pos, *refs):
    parts = refs[:planes]
    taps, skip, response, first, last, turned, back = refs[planes : planes + 7]
    outs = refs[planes + 7 : 3 * planes + 7]
    wide, value, work, result = refs[3 * planes + 7 :]
    rows = value.shape[0] // blocks
    share = value.shape[1]
    lead = wide.shape[0] - value.shape[0]
    own = pos[1] * PLANE + pos[2]
    columns = pl.ds(pl.multiple_of(own * share, share), share)
    taps, skip = taps[:, columns], skip[:, columns]
    wide[:lead, :] = jnp.zeros((lead, share), jnp.float32)
    for s in range(planes):
        for d in range(PLANE):
            at = block_at(pos, s, d, rows)
            wide[pl.ds(pl.multiple_of(lead + at, 8), rows), :] = parts[s][
                d * rows : (d + 1) * rows, :
            ].astype(jnp.float32)
    for b in range(blocks):
        at = lead + b * rows
        value[b * rows : (b + 1) * rows, :] = (
            taps[0:1, :] * wide[at : at + rows, :]
            + taps[1:2, :] * wide[at - 1 : at - 1 + rows, :]
            + taps[2:3, :] * wide[at - 2 : at - 2 + rows, :]
        ).astype(value.dtype)
    forward_stage(value, first, work, blocks, rows)
    for f in range(blocks + 1):
        got = spectrum_at(f, work, turned, blocks, rows)
        re, im = got[:rows], got[rows:]
        response_re = response[f, :rows, :].astype(jnp.float32)
        response_im = response[f, rows:, :].astype(jnp.float32)
        product = jnp.concatenate(
            [re * response_re - im * response_im, re * response_im + im * response_re], 0
        ).astype(jnp.bfloat16)
        if f == 0 or f == blocks:
            work[0 if f == 0 else 1] = dot(back[f, :rows, :], product).astype(work.dtype)
        else:
            inverse = dot(back[f], product).astype(work.dtype)
            work[2 * f] = inverse[:rows]
            work[2 * f + 1] = inverse[rows:]
    for pair in range(rows // (2 * ROWS)):
        halves = []
        for h in range(2):
            at = (2 * pair + h) * ROWS
            halves.append(
                jnp.concatenate([work[f, at : at + ROWS, :] for f in range(2 * blocks)], 0)
            )
        got = dot(last[...], jnp.concatenate(halves, 1))
        for h in range(2):
            at = (2 * pair + h) * ROWS
            for b in range(blocks):
                here = slice(b * rows + at, b * rows + at + ROWS)
                conv = got[b * ROWS : (b + 1) * ROWS, h * share : (h + 1) * share]
                result[here, :] = (
                    conv + skip * value[here, :].astype(jnp.float32)
                ).astype(result.dtype)
    for s in range(planes):
        for d in range(PLANE):
            half, at = d // 2, d % 2 * rows
            outs[half * planes + s][at : at + rows, :] = result[
                pl.ds(block_at(pos, s, d, rows), rows), :
            ]


def mixed_dot(planes, pos, u, gate, ws, mixed, outs, half):
    rows, share = mixed.shape[0], u[0].shape[1]
    for s in range(planes):
        plane = jnp.bitwise_xor(pos[1], s)
        if len(gate.shape) == 3:
            columns = gate[planes + plane]
        else:
            columns = gate[:rows, pl.ds(pl.multiple_of(plane * share, share), share)]
        mixed[:, s * share : (s + 1) * share] = (
            columns.astype(jnp.float32)
            * u[s][half * rows : (half + 1) * rows, :].astype(jnp.float32)
        ).astype(mixed.dtype)
    got = dot(mixed[...], ws[...])
    width = outs[0].shape[1]
    for i, out in enumerate(outs):
        out[...] = got[:, i * width : (i + 1) * width].astype(out.dtype)


def gather_kernel(pos, own, *refs):
    halves, ws = refs[:4], refs[4]
    share = own.shape[0]
    width = halves[0].shape[1]
    ws[:share, :] = own[...]
    for k in range(2):
        side = pos[0] if k == 0 else 1 - pos[0]
        columns = pl.ds(pl.multiple_of(side * width, width), width)
        ws[share : 2 * share, columns] = halves[2 * k][:share, :]
        ws[2 * share :, columns] = halves[2 * k + 1][...]


def place_kernel(planes, half, pos, *refs):
    u, gate, ws = refs[:planes], refs[planes], refs[planes + 1]
    mixed_dot(planes, pos, u, gate, ws, refs[-1], refs[planes + 2 : -1], half)


def local(inputs, gate_in, value_weight, short_taps, filter_taps, skip_scale, output_weight):
    rows, features = inputs.shape
    deep, channels = value_weight.shape
    devices = lax.axis_size("seq")
    planes = devices // PLANE
    share = channels // devices
    wide = planes * share
    blocks = devices
    index = lax.axis_index("seq")
    y = lax.axis_index("groups")
    z, place = index // PLANE, index % PLANE
    pos = jnp.stack([y, z, place]).astype(jnp.int32)

    def to_place(block, d):
        return lax.ppermute(block, "seq", [(i, i ^ d) for i in range(devices)])

    def to_plane(block, s):
        return lax.ppermute(block, "seq", [(i, i ^ (s * PLANE)) for i in range(devices)])

    def to_group(block):
        return lax.ppermute(block, "groups", [(0, 1), (1, 0)])

    def shaped(*shape, dtype=jnp.bfloat16):
        return jax.ShapeDtypeStruct(shape, dtype)

    def small(kernel, outs, *args, copies=0, fetched=0, vmem=2, flops=0):
        scratch = [pltpu.SemaphoreType.DMA((copies,))] if copies else []
        return list(call(kernel, outs, scratch, pos, args, flops, vmem=vmem, fetched=fetched))

    stage = lax.optimization_barrier
    first, last, turned, back = (
        jnp.asarray(t) for t in (*stage_tables(blocks), *turned_tables(blocks, rows))
    )
    part, width, positions = rows // 2, features // 2, blocks * rows

    taps_own, taps_whole, out_near, out_half = call(
        start_kernel,
        [shaped(rows, wide), shaped(rows, wide)]
        + [shaped(deep + rows // 4, width), shaped(deep, width)],
        [pltpu.VMEM((rows, channels), jnp.bfloat16), pltpu.SemaphoreType.DMA((5,))],
        pos,
        [filter_taps, output_weight],
        0,
        vmem=53,
        fetched=2,
    )
    cut = call(
        functools.partial(split_kernel, share),
        [shaped(deep, wide)] * PLANE,
        [pltpu.VMEM((deep, channels), jnp.bfloat16), pltpu.SemaphoreType.DMA((4,))],
        pos,
        [value_weight],
        0,
        vmem=53,
        fetched=1,
    )
    cut = list(cut)
    out_near = to_plane(out_near, 1)
    gate_own, gate_beside, gate_x = small(
        functools.partial(gate_kernel, share),
        [shaped(rows, wide), shaped(rows, wide), shaped(2 * rows, wide)],
        gate_in,
        copies=4 * planes,
        fetched=1,
    )
    core = to_place(inputs, 1)
    own = small(join_kernel, [shaped(deep, wide)], cut[0])
    cut = own + [to_place(cut[d], d) for d in range(1, PLANE)]
    route = [
        (y0 * devices + i, y0 * devices + (i ^ (2 + y0) * PLANE))
        for y0 in range(2)
        for i in range(devices)
    ]
    taps_whole = lax.ppermute(taps_whole, ("groups", "seq"), route)
    sent = small(half_kernel, [shaped(2 * deep, wide)], *cut, flops=1)[0]
    cut, taps_whole, late, core, out_near, sent, gate_own, gate_beside, gate_x = stage(
        (cut, taps_whole, inputs, core, out_near, sent, gate_own, gate_beside, gate_x)
    )

    taps_mine, out_near = small(
        trade_kernel,
        [shaped(rows * 3 // 2, wide), shaped(deep, width)],
        taps_whole,
        out_near,
    )
    near, far = to_plane(sent, 1), to_plane(sent, 2)
    from_x = to_place(late, 2)
    taps_other, out_other = to_group(taps_mine), to_group(out_near)
    near, far, taps_other, out_half, out_other = stage(
        (near, far, taps_other, out_half, out_other)
    )

    passed = to_plane(far, 1)
    other = small(
        join_kernel, [shaped(4 * deep, wide)], to_group(near), to_group(far), flops=1 << 30
    )[0]
    out_far = to_plane(out_half, 2)
    both = to_place(from_x, 1)
    taps_parts = small(
        places_kernel,
        [shaped(planes * (2 if d == 1 else 1), rows, share) for d in range(PLANE)],
        taps_own,
        taps_mine,
        taps_other,
        gate_beside,
        flops=1 << 30,
    )
    other, passed, both = stage((other, passed, both))
    passed_other = to_group(passed)
    taps_parts = [taps_parts[0]] + [to_place(taps_parts[d], d) for d in range(1, PLANE)]
    held = small(join_kernel, [shaped(PLANE * deep, wide)], *cut)[0]
    weights = small(join_kernel, [shaped(2 * deep, width)], out_far, to_plane(out_far, 1))[0]
    passed, other, both, taps_parts, passed_other, held = stage(
        (passed, other, both, taps_parts, passed_other, held)
    )
    projected = call(
        functools.partial(project_kernel, planes),
        [shaped(PLANE * rows, share)] * planes,
        [
            pltpu.VMEM((PLANE * rows, features), jnp.bfloat16),
            pltpu.VMEM((features, wide), jnp.bfloat16),
            pltpu.VMEM((PLANE * rows, wide), jnp.bfloat16),
        ],
        pos,
        [inputs, core, from_x, both, held, near, far, passed, other, passed_other],
        2 * PLANE * rows * features * wide,
        vmem=8,
    )
    projected, weights, gate_x = stage((projected, weights, gate_x))

    def spread(parts):
        sent = [to_plane(parts[s], s) for s in reversed(range(1, planes))]
        return [parts[0]] + sent[::-1]

    signal = spread(projected)
    weights_other = to_group(weights)
    gate_x = to_place(gate_x, 2)
    response = call(
        functools.partial(taps_kernel, blocks, planes),
        [shaped(blocks + 1, 2 * rows, share)],
        [
            pltpu.VMEM((positions, share), jnp.bfloat16),
            pltpu.VMEM((2 * blocks, rows, share), jnp.bfloat16),
        ],
        pos,
        [*taps_parts, first, turned],
        2 * positions * share * (32 * ROWS + 4 * rows),
        vmem=4,
    )[0]
    signal, response = stage((signal[::-1], response))
    signal = signal[::-1]

    mixed = call(
        functools.partial(conv_kernel, blocks, planes),
        [shaped(2 * rows, share)] * (2 * planes),
        [
            pltpu.VMEM((positions + 8, share), jnp.float32),
            pltpu.VMEM((positions, share), jnp.bfloat16),
            pltpu.VMEM((2 * blocks, rows, share), jnp.bfloat16),
            pltpu.VMEM((positions, share), jnp.bfloat16),
        ],
        pos,
        [*signal, short_taps, skip_scale[None], response, first, last, turned, back],
        16 * positions * share * (32 * ROWS + 4 * rows),
        vmem=8,
    )
    mixed, weights_other, gate_x = stage((mixed, weights_other, gate_x))

    upper = spread(mixed[planes:])
    gate_three = to_place(gate_x[rows:], 1)
    gathered = small(
        gather_kernel,
        [shaped(wide, features)],
        output_weight,
        out_near,
        weights,
        out_other,
        weights_other,
        flops=1,
    )[0]
    upper, lower, gate_three, gathered = stage((upper[::-1], mixed[:planes], gate_three, gathered))
    upper = upper[::-1]
    scratch = [pltpu.VMEM((rows, wide), jnp.bfloat16)]
    flops = 2 * rows * features * wide
    def partial_of(parts, half, gate, cost, pieces, dtype):
        return call(
            functools.partial(place_kernel, planes, half),
            [shaped(rows, features // pieces, dtype=dtype)] * pieces,
            scratch,
            pos,
            [*parts, gate, gathered],
            cost,
            vmem=8,
        )

    partial_three = partial_of(upper, 1, gate_three, flops, 1, jnp.bfloat16)[0]
    partial_two = partial_of(upper, 0, gate_x, flops, 1, jnp.float32)[0]
    across = partial_two + to_place(partial_three, 1).astype(jnp.float32)
    across, lower = stage((across.astype(jnp.bfloat16), lower))

    across = to_place(across, 2)
    lower = spread(lower)
    partial_one = partial_of(lower, 1, taps_parts[1], 0, 4, jnp.bfloat16)
    partial_zero = partial_of(lower, 0, gate_own, 0, 1, jnp.float32)[0]
    partial_one = jnp.concatenate([to_place(block, 1) for block in partial_one], 1)
    result = partial_zero + partial_one.astype(jnp.float32) + across.astype(jnp.float32)
    return result.astype(jnp.bfloat16)


def passed_along(block, axis, distance):
    devices = range(lax.axis_size(axis))
    route = [(i - distance, i) for i in devices if i - distance in devices]
    return lax.ppermute(block, axis, route)


def local_narrow(inputs, gate_in, value_weight, short_taps, filter_taps, skip_scale, output_weight):
    rows, features = inputs.shape
    channels = value_weight.shape[1]
    blocks = lax.axis_size("seq")
    share = channels // blocks
    index = lax.axis_index("seq")
    projected = dot(inputs, lax.all_gather(value_weight, "seq", axis=0, tiled=True)).astype(
        jnp.bfloat16
    )
    earlier = passed_along(projected[rows - 2 :], "seq", 1)
    extended = jnp.concatenate([earlier, projected], 0).astype(jnp.float32)
    value = (
        short_taps[0] * extended[2:]
        + short_taps[1] * extended[1:-1]
        + short_taps[2] * extended[:-2]
    ).astype(jnp.bfloat16)

    def by_channel(signal):
        cut = signal.reshape(rows, blocks, share)
        got = lax.all_to_all(cut, "seq", split_axis=1, concat_axis=0, tiled=True)
        return got.reshape(blocks, rows, share)

    grid = np.arange(2 * blocks)
    angle = 2.0 * np.pi * (grid[:, None] * grid[None, :] % (2 * blocks)) / (2 * blocks)
    wide = np.exp(-1j * angle)[: blocks + 1, :blocks]
    turned, back = (jnp.asarray(t) for t in turned_tables(blocks, rows))
    weight = np.full((blocks + 1, 1), 2.0)
    weight[0] = weight[-1] = 1.0
    narrow = weight * np.conj(wide) / (2 * blocks * rows)

    def einsum(form, table, data):
        return jnp.einsum(form, table, data, preferred_element_type=jnp.float32)

    def table(values):
        return jnp.asarray(values.astype(ml_dtypes.bfloat16))

    def forward(signal):
        re = einsum("fb,bmc->fmc", table(np.real(wide)), signal)
        im = einsum("fb,bmc->fmc", table(np.imag(wide)), signal)
        both = jnp.concatenate([re, im], 1).astype(jnp.bfloat16)
        return einsum("fkm,fmc->fkc", turned, both)

    response = forward(by_channel(filter_taps))
    got = forward(by_channel(value))
    re, im = got[:, :rows], got[:, rows:]
    response_re, response_im = response[:, :rows], response[:, rows:]
    product = jnp.concatenate(
        [re * response_re - im * response_im, re * response_im + im * response_re], 1
    ).astype(jnp.bfloat16)
    inverse = einsum("fmk,fkc->fmc", back, product).astype(jnp.bfloat16)
    conv = einsum("fb,fmc->bmc", table(np.real(narrow)), inverse[:, :rows]) - einsum(
        "fb,fmc->bmc", table(np.imag(narrow)), inverse[:, rows:]
    )
    conv = lax.all_to_all(
        conv.astype(jnp.bfloat16), "seq", split_axis=0, concat_axis=2, tiled=True
    ).reshape(rows, channels)
    mixed = (
        gate_in.astype(jnp.float32)
        * (conv.astype(jnp.float32) + skip_scale * value.astype(jnp.float32))
    ).astype(jnp.bfloat16)
    result = dot(mixed, lax.all_gather(output_weight, "seq", axis=0, tiled=True))
    return result.astype(jnp.bfloat16)


def solution(mesh):
    split = P(("groups", "seq"), None)
    placed = (split, split, P("seq", None), P(), P("seq", None), P(), P("seq", None))

    def run(*args):
        devices = mesh.shape["seq"]
        share = args[2].shape[1] // devices
        tiled = share % LANES == 0 and args[0].shape[0] // mesh.size == LANES
        paired = devices == 4 * PLANE and mesh.shape["groups"] == 2
        body = local if tiled and paired else local_narrow
        return jax.shard_map(body, mesh=mesh, in_specs=placed, out_specs=split, check_vma=False)(
            *args
        )

    return run
```
